32 devices in a mesh: groups: 2 (over y), dp: 8 (over z, core), tensor: 2 (over x).
Axes of the slice: x: 2, y: 2, z: 4, core: 2. Of those that a mesh axis runs over, the one named last changes fastest.
Arguments:
- patches: bfloat16 [16, 128, 16, 1792], P(('groups', 'dp'), 'tensor'), parts along dimension 0, may hold values from -24 to 24
- kept_count: int32 [16], P('groups'), parts along dimension 0, may hold values from 1 to 16, as said below
- keep_list: int32 [16, 16], P(('groups', 'dp')), parts along dimension 0, may hold values from 0 to 15, as said below
- pre_gain: float32 [1792], replicated, may hold values from 0.1 to 1.9
- pre_shift: float32 [1792], replicated, may hold values from -2.5 to 2.5
- w_qkv: bfloat16 [3, 1792, 1792], P(None, None, 'tensor'), may hold values from -9 to 9
- b_qkv: float32 [3, 1792], P(None, 'tensor'), may hold values from -2.5 to 2.5
- w_out: bfloat16 [1792, 1792], P('tensor'), may hold values from -0.125 to 0.125
- b_out: float32 [1792], replicated, may hold values from -2.5 to 2.5
- mlp_gain: float32 [1792], replicated, may hold values from 0.1 to 1.9
- mlp_shift: float32 [1792], replicated, may hold values from -2.5 to 2.5
- w_up: bfloat16 [1792, 9216], P(None, 'tensor'), may hold values from -0.125 to 0.125
- b_up: float32 [9216], P('tensor'), may hold values from -2.5 to 2.5
- w_down: bfloat16 [9216, 1792], P('tensor'), may hold values from -0.0625 to 0.0625
- b_down: float32 [1792], replicated, may hold values from -2.5 to 2.5
Outputs:
- encoded: bfloat16 [16, 128, 16, 1792], P(('groups', 'dp'), 'tensor'), parts along dimension 0
The draws below stay inside these ranges and needn't reach their ends.
There are 2 independent parts, one for each index of `groups`. The reference program is written for one: setup_inputs(seed, part) draws one part's arguments, and reference() takes and returns one part's arrays. A program takes and returns all parts, laid end to end along the dimension named above; an argument that names none is the same for every part. Nothing has to cross between parts.
Inputs may be any that keep to these rules, and one draw needn't show every extreme that they name: kept_count sums to 32, and one page keeps all 16 of its blocks. `keep_list`: each row is a permutation of the page's blocks: its first kept_count[p] entries are the kept blocks in ascending order, the rest the dropped blocks in ascending order.
All inputs are finite; a program needn't handle non-finite values.
Results may differ from the reference program's by a relative error of at most 0.007.
Values may be sent and summed in bfloat16 or wider, within the bound.
No kernel may reach another device: no remote copies, remote signals or barrier semaphores. Data moves between devices by JAX's collectives and lax.ppermute only.
A program may use at most 128 MiB of HBM per device.

```python
import math
import jax
import jax.numpy as jnp
from jax import lax

D = 1792
HEADS = 16
HEAD_DIM = 112
FF = 9216
BLOCK = 128
PAGE_BLOCKS = 16
KEEP = 4
PAGES = 8
TOTAL_KEPT = 32
HEAD_GROUPS = 2
N_DP = 8


def kept_totals(key):
    key_perm, key_page = jax.random.split(key)
    slot_total = PAGES * (PAGE_BLOCKS - 1)
    shuffled = jax.random.permutation(key_perm, slot_total).astype(jnp.int32)
    forced = jax.random.randint(key_page, (), 0, PAGES).astype(jnp.int32)
    slot_ids = jnp.arange(slot_total, dtype=jnp.int32)
    slot_page = slot_ids // (PAGE_BLOCKS - 1)
    priority = jnp.where(slot_page == forced, -1 - slot_ids, shuffled)
    order_rank = jnp.argsort(jnp.argsort(priority)).astype(jnp.int32)
    surplus = TOTAL_KEPT - PAGES
    chosen = (order_rank < surplus).astype(jnp.int32)
    return (1 + jnp.sum(chosen.reshape(PAGES, PAGE_BLOCKS - 1), axis=1)).astype(jnp.int32)


def draw_kept_count(key, part):
    return kept_totals(key)


def draw_keep_list(key, part):
    totals = kept_totals(key)
    key = jax.random.fold_in(key, 11)
    page_keys = jax.random.split(key, PAGES)
    shuffled = jax.vmap(lambda page_key: jax.random.permutation(page_key, PAGE_BLOCKS))(page_keys).astype(jnp.int32)
    placed = jnp.argsort(shuffled, axis=1).astype(jnp.int32)
    is_kept = (placed < totals[:, None]).astype(jnp.int32)
    block_ids = jnp.arange(PAGE_BLOCKS, dtype=jnp.int32)
    sort_key = (1 - is_kept) * PAGE_BLOCKS + block_ids[None, :]
    return jnp.argsort(sort_key, axis=1).astype(jnp.int32)


def draw_patches(key, part):
    key = jax.random.fold_in(key, 5)
    key_a = jax.random.fold_in(key, 0)
    key_b = jax.random.fold_in(key, 1)
    key_d = jax.random.fold_in(key, 3)
    key_e = jax.random.fold_in(key, 4)
    half_shape = (PAGES, BLOCK // 2, PAGE_BLOCKS, D)
    paired = jax.random.truncated_normal(key_a, -2.5, 2.5, half_shape, jnp.float32)
    twin = jax.random.truncated_normal(key_b, -2.5, 2.5, half_shape, jnp.float32)
    mixed = jnp.stack([paired, twin], axis=2).reshape(PAGES, BLOCK, PAGE_BLOCKS, D)
    row_scale = jnp.exp(jax.random.uniform(key_d, (PAGES, BLOCK, PAGE_BLOCKS, 1), jnp.float32, math.log(0.3), math.log(3.0)))
    column_scale = jnp.exp(jax.random.uniform(key_e, (D,), jnp.float32, math.log(0.3), math.log(3.0)))
    return jnp.clip(mixed * row_scale * column_scale, -24.0, 24.0).astype(jnp.bfloat16)


def draw_w_qkv(key, part):
    key = jax.random.fold_in(key, 7)
    key_a = jax.random.fold_in(key, 0)
    return (jax.random.truncated_normal(key_a, -3.0, 3.0, (3, D, D), jnp.float32) / math.sqrt(D)).astype(jnp.bfloat16)


def block_scale(own_key, extent, pieces, low, high):
    def one(axis_at, blocks):
        draws = jax.random.uniform(jax.random.fold_in(jax.random.fold_in(own_key, 6), axis_at), (blocks,), jnp.float32, low / len(pieces), high / len(pieces))
        return jnp.repeat(jnp.exp(draws), extent[axis_at] // blocks).reshape((-1,) + (1,) * (len(extent) - axis_at - 1))

    level = one(*pieces[0])
    for cut in pieces[1:]:
        level = level * one(*cut)
    return level


def bell_draw(stream_key, shape, spread, bound, cuts=(), kind=jnp.bfloat16):
    values = jax.random.normal(stream_key, shape, jnp.float32) * spread
    if len(cuts) > 0:
        values = block_scale(stream_key, shape, cuts, -0.22, 0.18) * values
    return jnp.clip(values, min=-bound, max=bound).astype(kind)


def setup_inputs(seed: int = 0, part: int = 0) -> dict:
    arg_keys = jax.random.split(jax.random.key(seed), 16)
    own_keys = jax.random.split(jax.random.fold_in(arg_keys[15], part), 16)
    return {
        "patches": draw_patches(jax.random.fold_in(jax.random.fold_in(arg_keys[15], part), 71), part),
        "kept_count": draw_kept_count(jax.random.fold_in(jax.random.fold_in(arg_keys[15], part), 71), part),
        "keep_list": draw_keep_list(jax.random.fold_in(jax.random.fold_in(arg_keys[15], part), 71), part),
        "pre_gain": jnp.clip(1.0 + 0.18 * jax.random.normal(arg_keys[3], (D,), jnp.float32), 0.1, 1.9),
        "pre_shift": bell_draw(arg_keys[4], (D,), 0.5, 2.5, (), jnp.float32),
        "w_qkv": draw_w_qkv(jax.random.fold_in(arg_keys[15], 71), part),
        "b_qkv": bell_draw(arg_keys[6], (3, D), 0.5, 2.5, ((1, 2),), jnp.float32),
        "w_out": bell_draw(arg_keys[7], (D, D), D ** -0.5, 0.125, ((0, 2),)),
        "b_out": bell_draw(arg_keys[8], (D,), 0.5, 2.5, (), jnp.float32),
        "mlp_gain": jnp.clip(1.0 + 0.18 * jax.random.normal(arg_keys[9], (D,), jnp.float32), 0.1, 1.9),
        "mlp_shift": bell_draw(arg_keys[10], (D,), 0.5, 2.5, (), jnp.float32),
        "w_up": bell_draw(arg_keys[11], (D, FF), D ** -0.5, 0.125, ((1, 2),)),
        "b_up": bell_draw(arg_keys[12], (FF,), 0.5, 2.5, ((0, 2),), jnp.float32),
        "w_down": bell_draw(arg_keys[13], (FF, D), FF ** -0.5, 0.0625, ((0, 2),)),
        "b_down": bell_draw(arg_keys[14], (D,), 0.5, 2.5, (), jnp.float32),
    }


def layer_norm(inputs, gain, shift):
    average = lax.optimization_barrier(jnp.mean(inputs, axis=-1, keepdims=True))
    centred = inputs - average
    variance = lax.optimization_barrier(jnp.mean(centred * centred, axis=-1, keepdims=True))
    return centred * lax.rsqrt(variance + 1e-06) * gain + shift

def encode_blocks(block_rows, pre_gain, pre_shift, w_qkv, b_qkv, w_out, b_out, mlp_gain, mlp_shift, w_up, b_up, w_down, b_down):
    count_blocks = block_rows.shape[0]
    as_float = block_rows.astype(jnp.float32)
    normed = layer_norm(as_float, pre_gain, pre_shift).astype(jnp.bfloat16)
    projected = jnp.einsum('nbd,jde->jnbe', normed.astype(jnp.float32), w_qkv.astype(jnp.float32))
    projected = projected + b_qkv[:, None, None, :]
    queries = projected[0].reshape(count_blocks, BLOCK, HEADS, HEAD_DIM)
    key_rows = projected[1].reshape(count_blocks, BLOCK, HEADS, HEAD_DIM)
    values = projected[2].astype(jnp.bfloat16).reshape(count_blocks, BLOCK, HEADS, HEAD_DIM)
    scores = jnp.einsum('nqhd,nkhd->nhqk', queries, key_rows, precision=lax.Precision.HIGHEST) * HEAD_DIM ** (-0.5)
    weights = jax.nn.softmax(scores, axis=-1).astype(jnp.bfloat16)
    attended = jnp.einsum('nhqk,nkhd->nqhd', weights.astype(jnp.float32), values.astype(jnp.float32))
    attended = attended.astype(jnp.bfloat16).reshape(count_blocks, BLOCK, HEAD_GROUPS, D // HEAD_GROUPS)
    out_groups = w_out.reshape(HEAD_GROUPS, D // HEAD_GROUPS, D).astype(jnp.float32)
    partials = jnp.einsum('nbge,ged->gnbd', attended.astype(jnp.float32), out_groups)
    attn_proj = lax.optimization_barrier(jnp.sum(partials.astype(jnp.bfloat16).astype(jnp.float32), axis=0))
    residual = as_float + attn_proj + b_out
    renormed = layer_norm(residual, mlp_gain, mlp_shift).astype(jnp.bfloat16).reshape(count_blocks * BLOCK, D)
    raised = jnp.dot(renormed, w_up, preferred_element_type=jnp.float32) + b_up
    hidden = jax.nn.gelu(raised, approximate=True).astype(jnp.bfloat16)
    hidden = hidden.reshape(count_blocks * BLOCK, HEAD_GROUPS, FF // HEAD_GROUPS)
    down_groups = w_down.reshape(HEAD_GROUPS, FF // HEAD_GROUPS, D).astype(jnp.float32)
    mlp_parts = jnp.einsum('rge,ged->grd', hidden.astype(jnp.float32), down_groups)
    mlp_out = lax.optimization_barrier(jnp.sum(mlp_parts.astype(jnp.bfloat16).astype(jnp.float32), axis=0))
    summed = residual.reshape(count_blocks * BLOCK, D) + mlp_out + b_down
    return summed.astype(jnp.bfloat16).reshape(count_blocks, BLOCK, D)

def reference(patches, kept_count, keep_list, pre_gain, pre_shift, w_qkv, b_qkv, w_out, b_out, mlp_gain, mlp_shift, w_up, b_up, w_down, b_down):
    page_ends = jnp.cumsum(kept_count).astype(jnp.int32)
    starts = (page_ends - kept_count).astype(jnp.int32)
    position = jnp.arange(TOTAL_KEPT, dtype=jnp.int32)
    page_of = lax.optimization_barrier(jnp.sum((page_ends[None, :] <= position[:, None]).astype(jnp.int32), axis=1)).astype(jnp.int32)
    local_index = (position - starts[page_of]).astype(jnp.int32)
    block_of = keep_list[page_of, local_index].astype(jnp.int32)
    gathered = patches[page_of, :, block_of, :]
    batches = gathered.reshape(N_DP, KEEP, BLOCK, D)

    def encode_batch(batch_rows):
        return encode_blocks(batch_rows, pre_gain, pre_shift, w_qkv, b_qkv, w_out, b_out, mlp_gain, mlp_shift, w_up, b_up, w_down, b_down)
    encoded_rows = lax.map(encode_batch, batches).reshape(TOTAL_KEPT, BLOCK, D)
    return patches.at[page_of, :, block_of, :].set(encoded_rows)
```

```python
import functools

import jax
import jax.numpy as jnp
from jax import lax
from jax.experimental import pallas as pl
from jax.experimental.pallas import tpu as pltpu
from jax.sharding import PartitionSpec as P

HEAD_DIM = 112
KEEP = 4
LOCAL = 1
MOVED = KEEP - LOCAL
STEPS = 2
WIDTH = 3
PAGE_HALF = 8
GROUP_ROWS = 16
F32 = jnp.float32
BF16 = jnp.bfloat16
MIB = 1 << 20


def norm_rows(inputs, gain, shift):
    average = jnp.mean(inputs, axis=-1, keepdims=True)
    centred = inputs - average
    variance = jnp.mean(centred * centred, axis=-1, keepdims=True)
    return centred * lax.rsqrt(variance + 1e-06) * gain + shift


def pick_at(values, index):
    total = jnp.int32(0)
    for place, value in enumerate(values):
        total = total + jnp.where(index == place, value, 0)
    return total


def page_ends_of(count_ref, pages):
    ends = [jnp.int32(0)]
    for page in range(pages):
        ends.append(ends[-1] + count_ref[page])
    return ends


def line_flows(ends, chips, core):
    prefix = []
    for chip in range(chips + 1):
        prefix.append(((ends[2 * chip] + 1 - core) >> 1) - LOCAL * chip)
    counts = [prefix[i + 1] - prefix[i] for i in range(chips)]
    zero = jnp.int32(0)
    need_right, need_left = [zero] * (chips + 1), [zero] * (chips + 1)
    for cut in range(1, chips):
        need_right[cut] = jnp.maximum(prefix[cut] - MOVED * cut, 0)
        need_left[cut] = jnp.maximum(MOVED * cut - prefix[cut], 0)
    right, left = [[zero] * (chips + 1)], [[zero] * (chips + 1)]
    for _ in range(STEPS):
        last_right, last_left = right[-1], left[-1]
        new_right, new_left = [zero] * (chips + 1), [zero] * (chips + 1)
        for cut in range(1, chips):
            new_right[cut] = jnp.minimum(
                need_right[cut],
                jnp.minimum(last_right[cut] + WIDTH, counts[cut - 1] + last_right[cut - 1]),
            )
            new_left[cut] = jnp.minimum(
                need_left[cut],
                jnp.minimum(last_left[cut] + WIDTH, counts[cut] + last_left[cut + 1]),
            )
        right.append(new_right)
        left.append(new_left)
    short = zero
    for cut in range(1, chips):
        short = short + jnp.where(right[-1][cut] < need_right[cut], 1, 0)
        short = short + jnp.where(left[-1][cut] < need_left[cut], 1, 0)
    return prefix, right, left, short


N_SEND = 2 * STEPS * WIDTH
AT_SEND = 0
AT_DEALT = AT_SEND + N_SEND
AT_BACK = AT_DEALT + KEEP
AT_HOME = AT_BACK + N_SEND
AT_SHORT = AT_HOME + 2 * PAGE_HALF
AT_SLOW_SOURCE = AT_SHORT + 1
AT_SLOW_HOME = AT_SLOW_SOURCE + MOVED
AT_SLOW_SEND = AT_SLOW_HOME + 2 * PAGE_HALF


def plan_kernel(pages, device_ref, count_ref, table_ref):
    chips = pages // 2
    device = device_ref[0]
    core, chip = device & 1, device >> 1
    ends = page_ends_of(count_ref, pages)
    prefix, right, left, short = line_flows(ends, chips, core)
    short_other = line_flows(ends, chips, 1 - core)[3]
    table_ref[AT_SHORT] = jnp.where(short + short_other > 0, 1, 0)

    low, high = pick_at(prefix, chip), pick_at(prefix, chip + 1)
    right_in = [pick_at(step, chip) for step in right]
    right_out = [pick_at(step, chip + 1) for step in right]
    left_out = [pick_at(step, chip) for step in left]
    left_in = [pick_at(step, chip + 1) for step in left]
    own_start, own_end = pick_at(ends, device), pick_at(ends, device + 1)
    mate_start = pick_at(ends, device ^ 1)

    def by_step(count, cuts, first):
        code = first * 16 + count
        for step in range(1, STEPS):
            code = jnp.where(
                count >= cuts[step], (first + step) * 16 + count - cuts[step], code
            )
        return code

    def local_code(position):
        own = (position >= own_start) & (position < own_end)
        return jnp.where(own, (position - own_start) >> 1, 16 + ((position - mate_start) >> 1))

    def rank_position(rank):
        return 2 * (rank + LOCAL * (chip + 1)) + core

    def forward_code(rank):
        code = local_code(rank_position(rank))
        code = jnp.where(rank < low, by_step(low - 1 - rank, right_in, 2), code)
        return jnp.where(rank >= high, by_step(rank - high, left_in, 2 + STEPS), code)

    first_mine = MOVED * chip

    def back_code(rank):
        code = LOCAL + rank - first_mine
        code = jnp.where(
            rank >= first_mine + MOVED, by_step(high - 1 - rank, right_out, 1), code
        )
        return jnp.where(rank < first_mine, by_step(rank - low, left_out, 1 + STEPS), code)

    for step in range(STEPS):
        for slot in range(WIDTH):
            at = 2 * step * WIDTH + slot
            table_ref[AT_SEND + at] = forward_code(high - 1 - (right_out[step] + slot))
            table_ref[AT_SEND + at + WIDTH] = forward_code(low + left_out[step] + slot)
            table_ref[AT_BACK + at] = back_code(low - 1 - (right_in[step] + slot))
            table_ref[AT_BACK + at + WIDTH] = back_code(high + left_in[step] + slot)
    kept_rank = low + LOCAL * chip
    table_ref[AT_DEALT] = local_code(2 * kept_rank + core)
    for slot in range(MOVED):
        table_ref[AT_DEALT + LOCAL + slot] = forward_code(first_mine + slot)
    for half, start in enumerate((own_start, mate_start)):
        for slot in range(PAGE_HALF):
            position = start + ((start + core) & 1) + 2 * slot
            lane_rank = (position - core) >> 1
            rank = lane_rank - LOCAL * (chip + 1)
            at = half * PAGE_HALF + slot
            kept = lane_rank == kept_rank
            table_ref[AT_HOME + at] = jnp.where(kept, 0, back_code(rank))
            node = jnp.int32(0)
            for place in range(1, chips):
                node = node + jnp.where(rank >= MOVED * place, 1, 0)
            slow = (2 * node + core) * KEEP + LOCAL + rank - MOVED * node
            slow = jnp.where(kept, device * KEEP, slow)
            table_ref[AT_SLOW_HOME + at] = jnp.clip(slow, 0, pages * KEEP - 1)
    for slot in range(MOVED):
        rank = first_mine + slot
        node = jnp.int32(0)
        for place in range(1, chips):
            node = node + jnp.where(prefix[place] <= rank, 1, 0)
        table_ref[AT_SLOW_SOURCE + slot] = 2 * node + core
    for rank in range(MOVED * chips):
        table_ref[AT_SLOW_SEND + rank] = jnp.clip(local_code(rank_position(rank)), 0, 31)


def make_plan(device, kept_count):
    pages = kept_count.shape[0]
    size = AT_SLOW_SEND + MOVED * (pages // 2)
    return pl.pallas_call(
        functools.partial(plan_kernel, pages),
        out_shape=jax.ShapeDtypeStruct((size,), jnp.int32),
        in_specs=[pl.BlockSpec(memory_space=pltpu.SMEM)] * 2,
        out_specs=pl.BlockSpec(memory_space=pltpu.SMEM),
        cost_estimate=pl.CostEstimate(flops=2000000, bytes_accessed=1000, transcendentals=0),
        name="plan",
    )(device, kept_count)


def kept_blocks(device_ref, count_ref, keep_ref, pages):
    device = device_ref[0]
    start, count = jnp.int32(0), jnp.int32(0)
    for page in range(pages):
        start = start + jnp.where(page < device, count_ref[page], 0)
        count = count + jnp.where(page == device, count_ref[page], 0)
    blocks = []
    for half in range(2):
        offset = (start + device + half) & 1
        for slot in range(PAGE_HALF):
            index = 2 * slot + offset
            block = keep_ref[jnp.minimum(index, 2 * PAGE_HALF - 1)]
            blocks.append(jnp.where(index < count, block, -1))
    return blocks


def pack_kernel(pages, device_ref, count_ref, keep_ref, home_ref, mine_ref, mate_ref):
    page_blocks, width = home_ref.shape[1], home_ref.shape[2]
    blocks = kept_blocks(device_ref, count_ref, keep_ref, pages)
    span = GROUP_ROWS * page_blocks
    row = lax.broadcasted_iota(jnp.int32, (GROUP_ROWS, span), 0)
    column = lax.broadcasted_iota(jnp.int32, (GROUP_ROWS, span), 1)
    chosen = jnp.concatenate(
        [jnp.where(column == row * page_blocks + block, 1.0, 0.0).astype(BF16) for block in blocks],
        axis=0,
    )
    packed = jnp.dot(
        chosen, home_ref[...].reshape(span, width), preferred_element_type=F32
    ).astype(BF16)
    half = PAGE_HALF * GROUP_ROWS
    mine_ref[...] = packed[:half].reshape(PAGE_HALF, GROUP_ROWS, width)
    mate_ref[...] = packed[half:].reshape(PAGE_HALF, GROUP_ROWS, width)


def pack(device, kept_count, keep_row, home):
    rows, page_blocks, width = home.shape
    shape = jax.ShapeDtypeStruct((PAGE_HALF, rows, width), BF16)
    place = pl.BlockSpec((PAGE_HALF, GROUP_ROWS, width), lambda step, *_: (0, step, 0))
    return pl.pallas_call(
        functools.partial(pack_kernel, kept_count.shape[0]),
        out_shape=(shape, shape),
        grid_spec=pltpu.PrefetchScalarGridSpec(
            num_scalar_prefetch=3,
            grid=(rows // GROUP_ROWS,),
            in_specs=[
                pl.BlockSpec((GROUP_ROWS, page_blocks, width), lambda step, *_: (step, 0, 0))
            ],
            out_specs=(place, place),
        ),
        compiler_params=pltpu.CompilerParams(vmem_limit_bytes=32 * MIB),
        name="pack",
    )(device, kept_count, keep_row, home)


def merge_kernel(pages, device_ref, count_ref, keep_ref, home_ref, mine_ref, mate_ref, out_ref):
    page_blocks, width = home_ref.shape[1], home_ref.shape[2]
    blocks = kept_blocks(device_ref, count_ref, keep_ref, pages)
    span = GROUP_ROWS * page_blocks
    depth = 2 * PAGE_HALF * GROUP_ROWS
    row = lax.broadcasted_iota(jnp.int32, (span, depth), 0)
    column = lax.broadcasted_iota(jnp.int32, (span, depth), 1)
    slot = lax.broadcasted_iota(jnp.int32, (1, depth), 1) // GROUP_ROWS
    block_id = lax.broadcasted_iota(jnp.int32, (span, 1), 0) % page_blocks
    wanted = jnp.full((1, depth), -1, jnp.int32)
    kept = jnp.zeros((span, 1), jnp.int32)
    for place, block in enumerate(blocks):
        wanted = jnp.where(slot == place, block, wanted)
        kept = kept + jnp.where(block_id == block, 1, 0)
    chosen = jnp.where(
        (row // page_blocks == column % GROUP_ROWS) & (row % page_blocks == wanted), 1.0, 0.0
    ).astype(BF16)
    half = PAGE_HALF * GROUP_ROWS
    source = jnp.concatenate(
        [mine_ref[...].reshape(half, width), mate_ref[...].reshape(half, width)], axis=0
    )
    landed = jnp.dot(chosen, source, preferred_element_type=F32)
    home = home_ref[...].reshape(span, width).astype(F32)
    merged = jnp.where(kept > 0, landed, home).astype(BF16)
    out_ref[...] = merged.reshape(GROUP_ROWS, page_blocks, width)


def merge(device, kept_count, keep_row, home, mine, mate):
    rows, page_blocks, width = home.shape
    place = pl.BlockSpec((PAGE_HALF, GROUP_ROWS, width), lambda step, *_: (0, step, 0))
    page = pl.BlockSpec((GROUP_ROWS, page_blocks, width), lambda step, *_: (step, 0, 0))
    return pl.pallas_call(
        functools.partial(merge_kernel, kept_count.shape[0]),
        out_shape=jax.ShapeDtypeStruct(home.shape, BF16),
        grid_spec=pltpu.PrefetchScalarGridSpec(
            num_scalar_prefetch=3,
            grid=(rows // GROUP_ROWS,),
            in_specs=[page, place, place],
            out_specs=page,
        ),
        compiler_params=pltpu.CompilerParams(vmem_limit_bytes=32 * MIB),
        name="merge",
    )(device, kept_count, keep_row, home, mine, mate)


def choose_kernel(at, total, table_ref, *refs):
    sources, out_ref, sems = refs[:-2], refs[-2], refs[-1]
    for slot in range(total):
        code = table_ref[at + slot]
        which, place = code >> 4, code & 15
        for number, source in enumerate(sources):
            if number == 0:
                here = which <= 0
            elif number == len(sources) - 1:
                here = which >= number
            else:
                here = which == number
            if len(sources) == 1:
                here = which > -(1 << 20)

            @pl.when(here)
            def _(source=source, slot=slot, place=place):
                inside = jnp.minimum(place, source.shape[0] - 1)
                pltpu.make_async_copy(source.at[inside], out_ref.at[slot], sems.at[slot]).start()

    for slot in range(total):
        pltpu.make_async_copy(sources[0].at[0], out_ref.at[slot], sems.at[slot]).wait()


def choose(table, at, total, sources, name):
    shape = (total,) + sources[0].shape[1:]
    size = 2 * total * sources[0][0].size * 2
    return pl.pallas_call(
        functools.partial(choose_kernel, at, total),
        out_shape=jax.ShapeDtypeStruct(shape, BF16),
        in_specs=[pl.BlockSpec(memory_space=pltpu.SMEM)]
        + [pl.BlockSpec(memory_space=pl.ANY)] * len(sources),
        out_specs=pl.BlockSpec(memory_space=pl.ANY),
        scratch_shapes=[pltpu.SemaphoreType.DMA((total,))],
        cost_estimate=pl.CostEstimate(flops=0, bytes_accessed=size, transcendentals=0),
        name=name,
    )(table, *sources)


def attend_kernel(own_ref, other_ref, gain_ref, shift_ref, w_ref, b_ref, out_ref, w_held, normed,
                  queries, key_rows, values, sems):
    blocks, rows, width = own_ref.shape
    span = w_held.shape[2]
    loads = [pltpu.make_async_copy(w_ref.at[j], w_held.at[j], sems.at[j]) for j in range(3)]
    for load in loads:
        load.start()
    gain, shift = gain_ref[...], shift_ref[...]
    for half, ref in enumerate((own_ref, other_ref)):
        for block in range(blocks):
            at = (half * blocks + block) * rows
            normed[at : at + rows] = norm_rows(ref[block].astype(F32), gain, shift).astype(BF16)
    for j, held in enumerate((queries, key_rows, values)):
        loads[j].wait()
        product = jnp.dot(normed[...], w_held[j], preferred_element_type=F32)
        held[...] = (product + b_ref[j : j + 1, :]).astype(held.dtype)
    tiles = span // 128
    heads = span // HEAD_DIM
    lane = lax.broadcasted_iota(jnp.int32, (1, 256), 1)

    def one_block(block, carry):
        near = pl.ds(pl.multiple_of(block * rows, rows), rows)
        far = pl.ds(pl.multiple_of((blocks + block) * rows, rows), rows)
        sums = [None] * tiles
        for head in range(heads):
            tile = min(head * HEAD_DIM // 128, tiles - 2)
            columns = slice(tile * 128, tile * 128 + 256)
            first = head * HEAD_DIM - tile * 128
            inside = (lane >= first) & (lane < first + HEAD_DIM)
            q = jnp.concatenate([queries[near, columns], queries[far, columns]], axis=0)
            k = jnp.concatenate([key_rows[near, columns], key_rows[far, columns]], axis=0)
            v = jnp.concatenate([values[near, columns], values[far, columns]], axis=0)
            q = jnp.where(inside, q, 0.0)
            scores = lax.dot_general(
                q, k, (((1,), (1,)), ((), ())),
                precision=lax.Precision.HIGHEST, preferred_element_type=F32,
            ) * HEAD_DIM ** (-0.5)
            scores = jnp.exp(scores - jnp.max(scores, axis=-1, keepdims=True))
            weights = (scores / jnp.sum(scores, axis=-1, keepdims=True)).astype(BF16)
            mixed = jnp.where(inside, jnp.dot(weights, v, preferred_element_type=F32), 0.0)
            for part in range(2):
                piece = mixed[:, part * 128 : part * 128 + 128]
                old = sums[tile + part]
                sums[tile + part] = piece if old is None else old + piece
        result = jnp.concatenate(sums, axis=1).astype(BF16)
        out_ref[0, block] = result[:rows]
        out_ref[1, block] = result[rows:]
        return carry

    lax.fori_loop(0, blocks, one_block, 0)


def attend(own, other, gain, shift, w_qkv, b_qkv):
    blocks, rows, width = own.shape
    span = w_qkv.shape[2]
    total = 2 * blocks * rows
    vmem = pl.BlockSpec(memory_space=pltpu.VMEM)
    return pl.pallas_call(
        attend_kernel,
        out_shape=jax.ShapeDtypeStruct((2, blocks, rows, span), BF16),
        in_specs=[vmem, vmem, vmem, vmem, pl.BlockSpec(memory_space=pl.ANY), vmem],
        out_specs=vmem,
        scratch_shapes=[
            pltpu.VMEM((3, width, span), BF16),
            pltpu.VMEM((total, width), BF16),
            pltpu.VMEM((total, span), F32),
            pltpu.VMEM((total, span), F32),
            pltpu.VMEM((total, span), BF16),
            pltpu.SemaphoreType.DMA((3,)),
        ],
        compiler_params=pltpu.CompilerParams(vmem_limit_bytes=48 * MIB),
        cost_estimate=pl.CostEstimate(
            flops=2 * total * width * span * 3 * 2, bytes_accessed=3 * width * span * 2,
            transcendentals=0,
        ),
        name="attend",
    )(own, other, gain[None], shift[None], w_qkv, b_qkv)


UP_TILE = 512
UP_SLOTS = 4


def mlp_kernel(own_ref, other_ref, mine_ref, theirs_ref, w_mine, w_near, w_side, w_mate,
               spots_ref, b_out_ref, gain_ref, shift_ref, b_up_ref, b_down_ref, w_up, w_down,
               keep_ref, send_ref, w_a, w_b, residual, renormed, total, ups, downs, sems, up_sems,
               down_sems):
    blocks, rows, width = own_ref.shape
    half = blocks * rows
    span = w_a.shape[0]
    piece = w_near.shape[0]
    steps = w_up.shape[1] // UP_TILE

    def load_up(step, slot):
        columns = pl.ds(pl.multiple_of(step * UP_TILE, UP_TILE), UP_TILE)
        return (
            pltpu.make_async_copy(w_up.at[:, columns], ups.at[slot], up_sems.at[slot]),
            pltpu.make_async_copy(w_down.at[columns, :], downs.at[slot], down_sems.at[slot]),
        )

    def spot(number):
        return pl.ds(pl.multiple_of(spots_ref[number] * piece, piece), piece)

    loads = [
        pltpu.make_async_copy(w_mine, w_a, sems.at[0]),
        pltpu.make_async_copy(w_near, w_b.at[spot(0), :], sems.at[1]),
        pltpu.make_async_copy(w_side, w_b.at[spot(1), :], sems.at[2]),
        pltpu.make_async_copy(w_mate.at[0], w_b.at[spot(2), :], sems.at[3]),
        pltpu.make_async_copy(w_mate.at[1], w_b.at[spot(3), :], sems.at[4]),
    ]
    for load in loads:
        load.start()
    for slot in range(UP_SLOTS):
        for load in load_up(slot, slot):
            load.start()
    for load in loads:
        load.wait()
    mine = mine_ref[...].reshape(2 * half, span)
    theirs = jnp.concatenate(
        [theirs_ref[1].reshape(half, span), theirs_ref[0].reshape(half, span)], axis=0
    )
    for column in range(0, width, 256):
        columns = slice(column, column + 256)
        part_a = jnp.dot(mine, w_a[:, columns], preferred_element_type=F32)
        part_b = jnp.dot(theirs, w_b[:, columns], preferred_element_type=F32)
        residual[:, columns] = part_a.astype(BF16).astype(F32) + part_b.astype(BF16).astype(F32)
    gain, shift, b_out = gain_ref[...], shift_ref[...], b_out_ref[...]
    for side, ref in enumerate((own_ref, other_ref)):
        for block in range(blocks):
            at = slice((side * blocks + block) * rows, (side * blocks + block + 1) * rows)
            value = ref[block].astype(F32) + residual[at] + b_out
            if side == 0:
                residual[at] = value
            renormed[at] = norm_rows(value, gain, shift).astype(BF16)
    total[...] = jnp.zeros_like(total)

    def one_step(step, carry):
        slot = lax.rem(step, UP_SLOTS)
        up_load, down_load = load_up(step, slot)
        up_load.wait()
        raised = []
        for part in range(0, UP_TILE, 256):
            bias = b_up_ref[step, :, part : part + 256]
            raised.append(
                jnp.dot(renormed[...], ups[slot, :, part : part + 256], preferred_element_type=F32)
                + bias
            )
        hidden = jnp.concatenate(
            [jax.nn.gelu(value, approximate=True).astype(BF16) for value in raised], axis=1
        )
        down_load.wait()
        total[...] += jnp.dot(hidden, downs[slot], preferred_element_type=F32)

        @pl.when(step + UP_SLOTS < steps)
        def _():
            for load in load_up(step + UP_SLOTS, slot):
                load.start()

        return carry

    lax.fori_loop(0, steps, one_step, 0)
    keep_ref[...] = (residual[:half] + total[:half] + b_down_ref[...]).reshape(keep_ref.shape)
    send_ref[...] = total[half:].astype(BF16).reshape(send_ref.shape)


def mlp(own, other, mine, theirs, w_out_parts, spots, b_out, gain, shift, w_up, b_up, w_down, b_down):
    blocks, rows, width = own.shape
    span = mine.shape[3]
    total = 2 * blocks * rows
    vmem = pl.BlockSpec(memory_space=pltpu.VMEM)
    hbm = pl.BlockSpec(memory_space=pl.ANY)
    smem = pl.BlockSpec(memory_space=pltpu.SMEM)
    hidden = w_up.shape[1]
    return pl.pallas_call(
        mlp_kernel,
        out_shape=(
            jax.ShapeDtypeStruct((blocks, rows, width), F32),
            jax.ShapeDtypeStruct((blocks, rows, width), BF16),
        ),
        in_specs=[vmem] * 4 + [hbm] * 4 + [smem] + [vmem] * 5 + [hbm] * 2,
        out_specs=(vmem, vmem),
        scratch_shapes=[
            pltpu.VMEM((span, width), BF16),
            pltpu.VMEM((span, width), BF16),
            pltpu.VMEM((total, width), F32),
            pltpu.VMEM((total, width), BF16),
            pltpu.VMEM((total, width), F32),
            pltpu.VMEM((UP_SLOTS, width, UP_TILE), BF16),
            pltpu.VMEM((UP_SLOTS, UP_TILE, width), BF16),
            pltpu.SemaphoreType.DMA((5,)),
            pltpu.SemaphoreType.DMA((UP_SLOTS,)),
            pltpu.SemaphoreType.DMA((UP_SLOTS,)),
        ],
        compiler_params=pltpu.CompilerParams(vmem_limit_bytes=56 * MIB),
        cost_estimate=pl.CostEstimate(
            flops=2 * total * width * (2 * span + 2 * hidden) * 2,
            bytes_accessed=2 * width * (2 * span + 2 * hidden),
            transcendentals=0,
        ),
        name="mlp",
    )(
        own, other, mine, theirs, *w_out_parts, spots, b_out[None], gain[None], shift[None],
        b_up.reshape(-1, 1, UP_TILE), b_down[None], w_up, w_down,
    )


def encode_pair(own, w_out_parts, spots, params):
    (pre_gain, pre_shift, w_qkv, b_qkv, _, b_out, mlp_gain, mlp_shift, w_up, b_up, w_down,
     b_down) = params
    swap = functools.partial(lax.ppermute, axis_name="tensor", perm=[(0, 1), (1, 0)])
    other = swap(own)
    mine = attend(own, other, pre_gain, pre_shift, w_qkv, b_qkv)
    theirs = swap(mine)
    keep, send = mlp(own, other, mine, theirs, w_out_parts, spots, b_out, mlp_gain, mlp_shift,
                     w_up, b_up, w_down, b_down)
    return (keep + swap(send).astype(F32)).astype(BF16)


def gather_w_out(w_out):
    core = lax.axis_index("dp") & 1
    group = lax.axis_index("groups")
    dp_size = lax.axis_size("dp")
    piece = w_out.shape[0] // 4
    number = 2 * group + core
    mine = lax.dynamic_slice_in_dim(w_out, number * piece, piece, 0)
    near = lax.ppermute(mine, "tensor", [(0, 1), (1, 0)])
    side = lax.ppermute(near, "groups", [(0, 1), (1, 0)])
    mate = lax.ppermute(jnp.stack([near, side]), "dp", [(d, d ^ 1) for d in range(dp_size)])
    other = 2 * (1 - group) + core
    spots = jnp.stack([number, other, number ^ 1, other ^ 1]).astype(jnp.int32)
    return (w_out, near, side, mate), spots


def attend_rows(projected):
    row_total, count_blocks, width = (projected.shape[0], projected.shape[1], projected.shape[3])
    head_count = width // HEAD_DIM
    queries = projected[:, :, 0].reshape(row_total, count_blocks, head_count, HEAD_DIM)
    key_rows = projected[:, :, 1].reshape(row_total, count_blocks, head_count, HEAD_DIM)
    values = projected[:, :, 2].astype(BF16).reshape(row_total, count_blocks, head_count, HEAD_DIM)
    scores = jnp.einsum(
        "qnhd,snhd->nhqs", queries, key_rows, precision=lax.Precision.HIGHEST
    ) * HEAD_DIM ** (-0.5)
    weights = jax.nn.softmax(scores, axis=-1).astype(BF16)
    attended = jnp.einsum("nhqs,snhd->qnhd", weights, values, preferred_element_type=F32)
    return attended.astype(BF16).reshape(row_total, count_blocks, width)


def encode_split(own, params):
    (pre_gain, pre_shift, w_qkv, b_qkv, w_out, b_out, mlp_gain, mlp_shift, w_up, b_up, w_down,
     b_down) = params
    block_rows = jnp.swapaxes(own, 0, 1)
    rows_dev = block_rows.shape[0]
    gathered = lax.all_gather(block_rows, "tensor", axis=0, tiled=True)
    normed = norm_rows(gathered.astype(F32), pre_gain, pre_shift).astype(BF16)
    attended = attend_rows(
        jnp.einsum("qnd,jde->qnje", normed, w_qkv, preferred_element_type=F32) + b_qkv[None, None]
    )
    partial_value = jnp.einsum("qne,ed->qnd", attended, w_out, preferred_element_type=F32)
    summed = lax.psum(partial_value.astype(BF16), "tensor").astype(F32)
    residual_all = gathered.astype(F32) + summed + b_out
    renormed = norm_rows(residual_all, mlp_gain, mlp_shift).astype(BF16)
    raised = jnp.einsum("qnd,df->qnf", renormed, w_up, preferred_element_type=F32) + b_up
    hidden = jax.nn.gelu(raised, approximate=True).astype(BF16)
    residual = lax.dynamic_slice_in_dim(
        residual_all, lax.axis_index("tensor") * rows_dev, rows_dev, 0
    )
    mlp_out = lax.psum_scatter(
        jnp.einsum("qnf,fd->qnd", hidden, w_down, preferred_element_type=F32).astype(BF16),
        "tensor", scatter_dimension=0, tiled=True,
    ).astype(F32)
    return jnp.swapaxes((residual + mlp_out + b_down).astype(BF16), 0, 1)


def per_device(paired, patches, kept_count, keep_list, *params):
    home = patches[0]
    keep_row = keep_list[0]
    dp_size = lax.axis_size("dp")
    device = lax.axis_index("dp").astype(jnp.int32).reshape(1)
    mates = [(d, d ^ 1) for d in range(dp_size)]
    rightwards = [(d, d + 2) for d in range(dp_size - 2)]
    leftwards = [(d + 2, d) for d in range(dp_size - 2)]

    def to_mate(value):
        return lax.ppermute(value, "dp", mates)

    def to_right(value):
        return lax.ppermute(value, "dp", rightwards)

    def to_left(value):
        return lax.ppermute(value, "dp", leftwards)

    if paired:
        w_out_parts, spots = gather_w_out(params[4])

        def encode(own):
            return encode_pair(own, w_out_parts, spots, params)
    else:

        def encode(own):
            return encode_split(own, params)

    table = make_plan(device, kept_count)
    short = lax.pmax(table[AT_SHORT], "groups")
    mine, for_mate = pack(device, kept_count, keep_row, home)
    from_mate = to_mate(for_mate)
    first = choose(table, AT_DEALT, LOCAL, [mine, from_mate], "deal_local")

    came_right, came_left = [], []
    for step in range(STEPS):
        sources = [mine, from_mate]
        if step:
            sources = sources + came_right + [mine] * (STEPS - step) + came_left
        at = AT_SEND + 2 * step * WIDTH
        going = choose(table, at, 2 * WIDTH, sources, "send_%d" % step)
        came_right.append(to_right(going[:WIDTH]))
        came_left.append(to_left(going[WIDTH:]))
    first_result = encode(first)

    def deal_fast():
        sources = [mine, from_mate] + came_right + came_left
        return choose(table, AT_DEALT + LOCAL, MOVED, sources, "deal_moved")

    def deal_slow():
        chips = dp_size // 2
        picked = choose(table, AT_SLOW_SEND, MOVED * chips, [mine, from_mate], "deal_slow")
        picked = picked.reshape((chips, MOVED) + picked.shape[1:])
        spread = jnp.repeat(picked, 2, axis=0)
        arrived = lax.all_to_all(spread, "dp", split_axis=0, concat_axis=0, tiled=True)
        return jnp.stack([arrived[table[AT_SLOW_SOURCE + j], j] for j in range(MOVED)])

    rest = lax.cond(short > 0, deal_slow, deal_fast)
    rest_result = encode(rest)
    results = jnp.concatenate([first_result, rest_result], axis=0)

    back_right, back_left = [None] * STEPS, [None] * STEPS
    for step in reversed(range(STEPS)):
        sources = [results]
        if step < STEPS - 1:
            known_right = [results if value is None else value for value in back_right]
            known_left = [results if value is None else value for value in back_left]
            sources = sources + known_right + known_left
        at = AT_BACK + 2 * step * WIDTH
        going = choose(table, at, 2 * WIDTH, sources, "back_%d" % step)
        back_right[step] = to_left(going[:WIDTH])
        back_left[step] = to_right(going[WIDTH:])

    def home_fast():
        return choose(table, AT_HOME, 2 * PAGE_HALF, [results] + back_right + back_left, "home_fast")

    def home_slow():
        spread = lax.all_gather(results, "dp", axis=0, tiled=True)
        return jnp.take(spread, table[AT_SLOW_HOME : AT_SLOW_HOME + 2 * PAGE_HALF], axis=0)

    returned = lax.cond(short > 0, home_slow, home_fast)
    back_mine, back_mate = returned[:PAGE_HALF], to_mate(returned[PAGE_HALF:])
    return merge(device, kept_count, keep_row, home, back_mine, back_mate)[None]


def solution(mesh):
    in_specs = (
        P(("groups", "dp"), "tensor", None, None),
        P("groups"),
        P(("groups", "dp"), None),
        P(),
        P(),
        P(None, None, "tensor"),
        P(None, "tensor"),
        P("tensor", None),
        P(),
        P(),
        P(),
        P(None, "tensor"),
        P("tensor"),
        P("tensor", None),
        P(),
    )
    out_specs = P(("groups", "dp"), "tensor", None, None)
    paired = mesh.shape["tensor"] == 2 and mesh.shape["groups"] == 2
    return jax.shard_map(
        functools.partial(per_device, paired), mesh=mesh, in_specs=in_specs, out_specs=out_specs,
        check_vma=False,
    )
```

```python
import functools

import jax
import jax.numpy as jnp
from jax import lax
from jax.experimental import pallas as pl
from jax.experimental.pallas import tpu as pltpu
from jax.sharding import PartitionSpec as P

HEAD_DIM = 112
KEEP = 4
LOCAL = 1
MOVED = KEEP - LOCAL
STEPS = 2
WIDTH = 3
PAGE_HALF = 8
GROUP_ROWS = 16
F32 = jnp.float32
BF16 = jnp.bfloat16
MIB = 1 << 20
SMALL_COST = pl.CostEstimate(flops=1000, bytes_accessed=1000, transcendentals=0)


def norm_rows(inputs, gain, shift):
    average = jnp.mean(inputs, axis=-1, keepdims=True)
    centred = inputs - average
    variance = jnp.mean(centred * centred, axis=-1, keepdims=True)
    return centred * lax.rsqrt(variance + 1e-06) * gain + shift


def pick_at(values, index):
    total = jnp.int32(0)
    for place, value in enumerate(values):
        total = total + jnp.where(index == place, value, 0)
    return total


def page_ends_of(count_ref, pages):
    ends = [jnp.int32(0)]
    for page in range(pages):
        ends.append(ends[-1] + count_ref[page])
    return ends


def here_early(rank, low, high, from_left, from_right):
    return jnp.where((rank >= low - from_left) & (rank < high + from_right), 1, 0)


def line_flows(ends, chips, core):
    prefix = []
    for chip in range(chips + 1):
        prefix.append(((ends[2 * chip] + 1 - core) >> 1) - LOCAL * chip)
    counts = [prefix[i + 1] - prefix[i] for i in range(chips)]
    zero = jnp.int32(0)
    need_right, need_left = [zero] * (chips + 1), [zero] * (chips + 1)
    for cut in range(1, chips):
        need_right[cut] = jnp.maximum(prefix[cut] - MOVED * cut, 0)
        need_left[cut] = jnp.maximum(MOVED * cut - prefix[cut], 0)
    right, left = [[zero] * (chips + 1)], [[zero] * (chips + 1)]
    for _ in range(STEPS):
        last_right, last_left = right[-1], left[-1]
        new_right, new_left = [zero] * (chips + 1), [zero] * (chips + 1)
        for cut in range(1, chips):
            new_right[cut] = jnp.minimum(
                need_right[cut],
                jnp.minimum(last_right[cut] + WIDTH, counts[cut - 1] + last_right[cut - 1]),
            )
            new_left[cut] = jnp.minimum(
                need_left[cut],
                jnp.minimum(last_left[cut] + WIDTH, counts[cut] + last_left[cut + 1]),
            )
        right.append(new_right)
        left.append(new_left)
    short = zero
    for cut in range(1, chips):
        short = short + jnp.where(right[-1][cut] < need_right[cut], 1, 0)
        short = short + jnp.where(left[-1][cut] < need_left[cut], 1, 0)
    for chip in range(chips):
        early = zero
        for slot in range(MOVED):
            early = early + here_early(
                MOVED * chip + slot, prefix[chip], prefix[chip + 1], right[1][chip], left[1][chip + 1]
            )
        short = short + jnp.where(early == 0, 1, 0)
    return prefix, right, left, short


N_SEND = 2 * STEPS * WIDTH
AT_SEND = 0
AT_DEALT = AT_SEND + N_SEND
AT_BACK = AT_DEALT + KEEP
AT_HOME = AT_BACK + N_SEND
AT_SHORT = AT_HOME + 2 * PAGE_HALF
AT_SLOW_SOURCE = AT_SHORT + 1
AT_SLOW_HOME = AT_SLOW_SOURCE + MOVED
AT_SLOW_SEND = AT_SLOW_HOME + 2 * PAGE_HALF


def plan_kernel(pages, device_ref, count_ref, table_ref):
    chips = pages // 2
    device = device_ref[0]
    core, chip = device & 1, device >> 1
    ends = page_ends_of(count_ref, pages)
    prefix, right, left, short = line_flows(ends, chips, core)
    short_other = line_flows(ends, chips, 1 - core)[3]
    table_ref[AT_SHORT] = jnp.where(short + short_other > 0, 1, 0)

    low, high = pick_at(prefix, chip), pick_at(prefix, chip + 1)
    right_in = [pick_at(step, chip) for step in right]
    right_out = [pick_at(step, chip + 1) for step in right]
    left_out = [pick_at(step, chip) for step in left]
    left_in = [pick_at(step, chip + 1) for step in left]
    own_start, own_end = pick_at(ends, device), pick_at(ends, device + 1)
    mate_start = pick_at(ends, device ^ 1)

    def by_step(count, cuts, first):
        code = first * 16 + count
        for step in range(1, STEPS):
            code = jnp.where(
                count >= cuts[step], (first + step) * 16 + count - cuts[step], code
            )
        return code

    def local_code(position):
        own = (position >= own_start) & (position < own_end)
        return jnp.where(own, (position - own_start) >> 1, 16 + ((position - mate_start) >> 1))

    def rank_position(rank):
        return 2 * (rank + LOCAL * (chip + 1)) + core

    def forward_code(rank):
        code = local_code(rank_position(rank))
        code = jnp.where(rank < low, by_step(low - 1 - rank, right_in, 2), code)
        return jnp.where(rank >= high, by_step(rank - high, left_in, 2 + STEPS), code)

    first_mine = MOVED * chip
    second = jnp.int32(0)
    for slot in range(1, MOVED):
        early = here_early(first_mine + slot, low, high, right_in[1], left_in[1])
        second = jnp.where(early > 0, slot, second)

    def result_slot(offset):
        slot = LOCAL + 1 + offset - jnp.where(offset > second, 1, 0)
        return jnp.where(offset == second, LOCAL, slot)

    order = [second] + [
        slot + jnp.where(second <= slot, 1, 0) for slot in range(MOVED - 1)
    ]

    def back_code(rank):
        code = result_slot(rank - first_mine)
        code = jnp.where(
            rank >= first_mine + MOVED, by_step(high - 1 - rank, right_out, 1), code
        )
        return jnp.where(rank < first_mine, by_step(rank - low, left_out, 1 + STEPS), code)

    for step in range(STEPS):
        for slot in range(WIDTH):
            at = 2 * step * WIDTH + slot
            table_ref[AT_SEND + at] = forward_code(high - 1 - (right_out[step] + slot))
            table_ref[AT_SEND + at + WIDTH] = forward_code(low + left_out[step] + slot)
            table_ref[AT_BACK + at] = back_code(low - 1 - (right_in[step] + slot))
            table_ref[AT_BACK + at + WIDTH] = back_code(high + left_in[step] + slot)
    kept_rank = low + LOCAL * chip
    table_ref[AT_DEALT] = local_code(2 * kept_rank + core)
    for slot in range(MOVED):
        table_ref[AT_DEALT + LOCAL + slot] = forward_code(first_mine + order[slot])
    for half, start in enumerate((own_start, mate_start)):
        for slot in range(PAGE_HALF):
            position = start + ((start + core) & 1) + 2 * slot
            lane_rank = (position - core) >> 1
            rank = lane_rank - LOCAL * (chip + 1)
            at = half * PAGE_HALF + slot
            kept = lane_rank == kept_rank
            table_ref[AT_HOME + at] = jnp.where(kept, 0, back_code(rank))
            node = jnp.int32(0)
            for place in range(1, chips):
                node = node + jnp.where(rank >= MOVED * place, 1, 0)
            slow = (2 * node + core) * KEEP + LOCAL + rank - MOVED * node
            slow = jnp.where(kept, device * KEEP, slow)
            table_ref[AT_SLOW_HOME + at] = jnp.clip(slow, 0, pages * KEEP - 1)
    for slot in range(MOVED):
        rank = first_mine + slot
        node = jnp.int32(0)
        for place in range(1, chips):
            node = node + jnp.where(prefix[place] <= rank, 1, 0)
        table_ref[AT_SLOW_SOURCE + slot] = 2 * node + core
    for rank in range(MOVED * chips):
        table_ref[AT_SLOW_SEND + rank] = jnp.clip(local_code(rank_position(rank)), 0, 31)


def make_plan(device, kept_count):
    pages = kept_count.shape[0]
    size = AT_SLOW_SEND + MOVED * (pages // 2)
    return pl.pallas_call(
        functools.partial(plan_kernel, pages),
        out_shape=jax.ShapeDtypeStruct((size,), jnp.int32),
        in_specs=[pl.BlockSpec(memory_space=pltpu.SMEM)] * 2,
        out_specs=pl.BlockSpec(memory_space=pltpu.SMEM),
        compiler_params=pltpu.CompilerParams(vmem_limit_bytes=MIB),
        cost_estimate=SMALL_COST,
        name="plan",
    )(device, kept_count)


def kept_blocks(device_ref, count_ref, keep_ref, pages):
    device = device_ref[0]
    start, count = jnp.int32(0), jnp.int32(0)
    for page in range(pages):
        start = start + jnp.where(page < device, count_ref[page], 0)
        count = count + jnp.where(page == device, count_ref[page], 0)
    blocks = []
    for half in range(2):
        offset = (start + device + half) & 1
        for slot in range(PAGE_HALF):
            index = 2 * slot + offset
            block = keep_ref[jnp.minimum(index, 2 * PAGE_HALF - 1)]
            blocks.append(jnp.where(index < count, block, -1))
    return blocks


def pack_kernel(pages, device_ref, count_ref, keep_ref, home_ref, mine_ref, mate_ref):
    page_blocks, width = home_ref.shape[1], home_ref.shape[2]
    blocks = kept_blocks(device_ref, count_ref, keep_ref, pages)
    span = GROUP_ROWS * page_blocks
    row = lax.broadcasted_iota(jnp.int32, (GROUP_ROWS, span), 0)
    column = lax.broadcasted_iota(jnp.int32, (GROUP_ROWS, span), 1)
    chosen = jnp.concatenate(
        [jnp.where(column == row * page_blocks + block, 1.0, 0.0).astype(BF16) for block in blocks],
        axis=0,
    )
    packed = jnp.dot(
        chosen, home_ref[...].reshape(span, width), preferred_element_type=F32
    ).astype(BF16)
    half = PAGE_HALF * GROUP_ROWS
    mine_ref[...] = packed[:half].reshape(PAGE_HALF, GROUP_ROWS, width)
    mate_ref[...] = packed[half:].reshape(PAGE_HALF, GROUP_ROWS, width)


def pack(device, kept_count, keep_row, home):
    rows, page_blocks, width = home.shape
    shape = jax.ShapeDtypeStruct((PAGE_HALF, rows, width), BF16)
    place = pl.BlockSpec((PAGE_HALF, GROUP_ROWS, width), lambda step, *_: (0, step, 0))
    return pl.pallas_call(
        functools.partial(pack_kernel, kept_count.shape[0]),
        out_shape=(shape, shape),
        grid_spec=pltpu.PrefetchScalarGridSpec(
            num_scalar_prefetch=3,
            grid=(rows // GROUP_ROWS,),
            in_specs=[
                pl.BlockSpec((GROUP_ROWS, page_blocks, width), lambda step, *_: (step, 0, 0))
            ],
            out_specs=(place, place),
        ),
        compiler_params=pltpu.CompilerParams(vmem_limit_bytes=16 * MIB),
        name="pack",
    )(device, kept_count, keep_row, home)


def merge_kernel(pages, device_ref, count_ref, keep_ref, home_ref, mine_ref, mate_ref, out_ref):
    page_blocks, width = home_ref.shape[1], home_ref.shape[2]
    blocks = kept_blocks(device_ref, count_ref, keep_ref, pages)
    span = GROUP_ROWS * page_blocks
    depth = 2 * PAGE_HALF * GROUP_ROWS
    row = lax.broadcasted_iota(jnp.int32, (span, depth), 0)
    column = lax.broadcasted_iota(jnp.int32, (span, depth), 1)
    slot = lax.broadcasted_iota(jnp.int32, (1, depth), 1) // GROUP_ROWS
    block_id = lax.broadcasted_iota(jnp.int32, (span, 1), 0) % page_blocks
    wanted = jnp.full((1, depth), -1, jnp.int32)
    kept = jnp.zeros((span, 1), jnp.int32)
    for place, block in enumerate(blocks):
        wanted = jnp.where(slot == place, block, wanted)
        kept = kept + jnp.where(block_id == block, 1, 0)
    chosen = jnp.where(
        (row // page_blocks == column % GROUP_ROWS) & (row % page_blocks == wanted), 1.0, 0.0
    ).astype(BF16)
    half = PAGE_HALF * GROUP_ROWS
    source = jnp.concatenate(
        [mine_ref[...].reshape(half, width), mate_ref[...].reshape(half, width)], axis=0
    )
    landed = jnp.dot(chosen, source, preferred_element_type=F32)
    home = home_ref[...].reshape(span, width).astype(F32)
    merged = jnp.where(kept > 0, landed, home).astype(BF16)
    out_ref[...] = merged.reshape(GROUP_ROWS, page_blocks, width)


def merge(device, kept_count, keep_row, home, mine, mate):
    rows, page_blocks, width = home.shape
    place = pl.BlockSpec((PAGE_HALF, GROUP_ROWS, width), lambda step, *_: (0, step, 0))
    page = pl.BlockSpec((GROUP_ROWS, page_blocks, width), lambda step, *_: (step, 0, 0))
    return pl.pallas_call(
        functools.partial(merge_kernel, kept_count.shape[0]),
        out_shape=jax.ShapeDtypeStruct(home.shape, BF16),
        grid_spec=pltpu.PrefetchScalarGridSpec(
            num_scalar_prefetch=3,
            grid=(rows // GROUP_ROWS,),
            in_specs=[page, place, place],
            out_specs=page,
        ),
        compiler_params=pltpu.CompilerParams(vmem_limit_bytes=16 * MIB),
        name="merge",
    )(device, kept_count, keep_row, home, mine, mate)


def choose_kernel(parts, n_sources, table_ref, *refs):
    sources, outs, sems = refs[:n_sources], refs[-1 - len(parts) : -1], refs[-1]
    number = 0
    for (at, total), out_ref in zip(parts, outs):
        for slot in range(total):
            code = table_ref[at + slot]
            which, place = code >> 4, code & 15
            for index, source in enumerate(sources):
                if len(sources) == 1:
                    here = which > -(1 << 20)
                elif index == 0:
                    here = which <= 0
                elif index == len(sources) - 1:
                    here = which >= index
                else:
                    here = which == index

                @pl.when(here)
                def _(source=source, out_ref=out_ref, slot=slot, place=place, number=number):
                    inside = jnp.minimum(place, source.shape[0] - 1)
                    pltpu.make_async_copy(
                        source.at[inside], out_ref.at[slot], sems.at[number]
                    ).start()

            number += 1
    number = 0
    for (_, total), out_ref in zip(parts, outs):
        for slot in range(total):
            pltpu.make_async_copy(sources[0].at[0], out_ref.at[slot], sems.at[number]).wait()
            number += 1


def choose(table, parts, sources, name, after=()):
    block = sources[0].shape[1:]
    total = sum(count for _, count in parts)
    return pl.pallas_call(
        functools.partial(choose_kernel, parts, len(sources)),
        out_shape=tuple(pltpu.VMEM((count,) + block, BF16) for _, count in parts),
        in_specs=[pl.BlockSpec(memory_space=pltpu.SMEM)]
        + [pl.BlockSpec(memory_space=pl.ANY)] * (len(sources) + len(after)),
        out_specs=tuple(pl.BlockSpec(memory_space=pl.ANY) for _ in parts),
        scratch_shapes=[pltpu.SemaphoreType.DMA((total,))],
        compiler_params=pltpu.CompilerParams(vmem_limit_bytes=MIB),
        cost_estimate=SMALL_COST,
        name=name,
    )(table, *sources, *after)


def join_kernel(spots_ref, near, side, mate, out_ref, sems):
    piece = near.shape[0]
    sources = (near, side, mate.at[0], mate.at[1])
    copies = []
    for number, source in enumerate(sources):
        place = pl.ds(pl.multiple_of(spots_ref[number] * piece, piece), piece)
        copies.append(pltpu.make_async_copy(source, out_ref.at[place, :], sems.at[number]))
    for copy in copies:
        copy.start()
    for copy in copies:
        copy.wait()


def join(spots, near, side, mate):
    shape = (4 * near.shape[0], near.shape[1])
    any_space = pl.BlockSpec(memory_space=pl.ANY)
    return pl.pallas_call(
        join_kernel,
        out_shape=pltpu.VMEM(shape, BF16),
        in_specs=[pl.BlockSpec(memory_space=pltpu.SMEM)] + [any_space] * 3,
        out_specs=any_space,
        scratch_shapes=[pltpu.SemaphoreType.DMA((4,))],
        compiler_params=pltpu.CompilerParams(vmem_limit_bytes=MIB),
        name="join",
    )(spots, near, side, mate)


def in_vmem(array):
    return pltpu.with_memory_space_constraint(array, pltpu.VMEM)


def in_hbm(array):
    return pltpu.with_memory_space_constraint(array, pltpu.HBM)


def attend_kernel(n_after, own_ref, other_ref, rows_ref, w_ref, b_ref, *refs):
    out_ref, normed, queries, key_rows, values = refs[n_after:]
    blocks, rows, width = own_ref.shape
    span = w_ref.shape[2]
    gain, shift = rows_ref[0:1, :], rows_ref[1:2, :]
    for half, ref in enumerate((own_ref, other_ref)):
        for block in range(blocks):
            at = (half * blocks + block) * rows
            normed[at : at + rows] = norm_rows(ref[block].astype(F32), gain, shift).astype(BF16)
    for j, held in enumerate((queries, key_rows, values)):
        product = jnp.dot(normed[...], w_ref[j], preferred_element_type=F32)
        held[...] = (product + b_ref[j : j + 1, :]).astype(held.dtype)
    tiles = span // 128
    heads = span // HEAD_DIM
    lane = lax.broadcasted_iota(jnp.int32, (1, 256), 1)

    def one_block(block, carry):
        near = pl.ds(pl.multiple_of(block * rows, rows), rows)
        far = pl.ds(pl.multiple_of((blocks + block) * rows, rows), rows)
        sums = [None] * tiles
        for head in range(heads):
            tile = min(head * HEAD_DIM // 128, tiles - 2)
            columns = slice(tile * 128, tile * 128 + 256)
            first = head * HEAD_DIM - tile * 128
            inside = (lane >= first) & (lane < first + HEAD_DIM)
            q = jnp.concatenate([queries[near, columns], queries[far, columns]], axis=0)
            k = jnp.concatenate([key_rows[near, columns], key_rows[far, columns]], axis=0)
            v = jnp.concatenate([values[near, columns], values[far, columns]], axis=0)
            q = jnp.where(inside, q * HEAD_DIM ** (-0.5), 0.0)
            scores = lax.dot_general(
                q, k, (((1,), (1,)), ((), ())),
                precision=lax.Precision.HIGHEST, preferred_element_type=F32,
            )
            scores = jnp.exp(scores - jnp.max(scores, axis=-1, keepdims=True))
            weights = (scores * (1.0 / jnp.sum(scores, axis=-1, keepdims=True))).astype(BF16)
            mixed = jnp.where(inside, jnp.dot(weights, v, preferred_element_type=F32), 0.0)
            for part in range(2):
                piece = mixed[:, part * 128 : part * 128 + 128]
                old = sums[tile + part]
                sums[tile + part] = piece if old is None else old + piece
        result = jnp.concatenate(sums, axis=1).astype(BF16)
        out_ref[0, block] = result[:rows]
        out_ref[1, block] = result[rows:]
        return carry

    lax.fori_loop(0, blocks, one_block, 0)


def attend(own, other, rows_params, w_qkv, b_qkv, after=()):
    blocks, rows, width = own.shape
    span = w_qkv.shape[2]
    total = 2 * blocks * rows
    vmem = pl.BlockSpec(memory_space=pltpu.VMEM)
    return pl.pallas_call(
        functools.partial(attend_kernel, len(after)),
        out_shape=jax.ShapeDtypeStruct((2, blocks, rows, span), BF16),
        in_specs=[vmem] * 5 + [pl.BlockSpec(memory_space=pl.ANY)] * len(after),
        out_specs=vmem,
        scratch_shapes=[
            pltpu.VMEM((total, width), BF16),
            pltpu.VMEM((total, span), F32),
            pltpu.VMEM((total, span), F32),
            pltpu.VMEM((total, span), BF16),
        ],
        compiler_params=pltpu.CompilerParams(vmem_limit_bytes=12 * MIB),
        cost_estimate=SMALL_COST,
        name="attend",
    )(own, other, rows_params, in_vmem(w_qkv), b_qkv, *after)


UP_TILE = 512
DOWN_TILE = 256
SLOTS = 5


def mlp_kernel(n_after, own_ref, other_ref, mine_ref, theirs_ref, rows_ref, b_up_ref, w_a, w_b, w_up,
               w_down, *refs):
    (keep_ref, send_ref, residual, renormed, hidden, ups, downs, up_sems,
     down_sems) = refs[n_after:]
    blocks, rows, width = own_ref.shape
    half = blocks * rows
    span = w_a.shape[0]
    up_steps, down_steps = w_up.shape[1] // UP_TILE, width // DOWN_TILE

    def load_up(step):
        columns = pl.ds(pl.multiple_of(step * UP_TILE, UP_TILE), UP_TILE)
        slot = lax.rem(step, SLOTS)
        return pltpu.make_async_copy(w_up.at[:, columns], ups.at[slot], up_sems.at[slot])

    def load_down(step):
        columns = pl.ds(pl.multiple_of(step * DOWN_TILE, DOWN_TILE), DOWN_TILE)
        slot = lax.rem(step, SLOTS)
        return pltpu.make_async_copy(w_down.at[:, columns], downs.at[slot], down_sems.at[slot])

    for slot in range(SLOTS):
        load_up(jnp.int32(slot)).start()
    gain, shift = rows_ref[2:3, :], rows_ref[3:4, :]
    mine = mine_ref[...].reshape(2 * half, span)
    theirs = jnp.concatenate(
        [theirs_ref[1].reshape(half, span), theirs_ref[0].reshape(half, span)], axis=0
    )
    for column in range(0, width, DOWN_TILE):
        columns = slice(column, column + DOWN_TILE)
        part_a = jnp.dot(mine, w_a[:, columns], preferred_element_type=F32)
        part_b = jnp.dot(theirs, w_b[:, columns], preferred_element_type=F32)
        residual[:, columns] = (
            part_a.astype(BF16).astype(F32) + part_b.astype(BF16).astype(F32) + rows_ref[4:5, columns]
        )
    for side, ref in enumerate((own_ref, other_ref)):
        for block in range(blocks):
            at = slice((side * blocks + block) * rows, (side * blocks + block + 1) * rows)
            value = ref[block].astype(F32) + residual[at]
            if side == 0:
                residual[at] = value
            renormed[at] = norm_rows(value, gain, shift).astype(BF16)

    def one_up(step, carry):
        load_up(step).wait()
        slot = lax.rem(step, SLOTS)
        for part in range(0, UP_TILE, 256):
            columns = pl.ds(pl.multiple_of(step * UP_TILE + part, 256), 256)
            raised = jnp.dot(
                renormed[...], ups[slot, :, part : part + 256], preferred_element_type=F32
            )
            raised = raised + b_up_ref[0:1, columns]
            hidden[:, columns] = jax.nn.gelu(raised, approximate=True).astype(BF16)
        ahead = step + SLOTS

        @pl.when(ahead < up_steps)
        def _():
            load_up(ahead).start()

        @pl.when((ahead >= up_steps) & (ahead < up_steps + down_steps))
        def _():
            load_down(ahead - up_steps).start()

        return carry

    lax.fori_loop(0, up_steps, one_up, 0)

    def one_down(step, carry):
        load_down(step).wait()
        columns = pl.ds(pl.multiple_of(step * DOWN_TILE, DOWN_TILE), DOWN_TILE)
        lowered = jnp.dot(
            hidden[...], downs[lax.rem(step, SLOTS)], preferred_element_type=F32
        )
        kept = residual[:half, columns] + lowered[:half] + rows_ref[5:6, columns]
        keep_ref[:, :, columns] = kept.reshape(blocks, rows, DOWN_TILE)
        send_ref[:, :, columns] = lowered[half:].astype(BF16).reshape(blocks, rows, DOWN_TILE)

        @pl.when(step + SLOTS < down_steps)
        def _():
            load_down(step + SLOTS).start()

        return carry

    lax.fori_loop(0, down_steps, one_down, 0)


def mlp(own, other, mine, theirs, rows_params, b_up, weights, after):
    blocks, rows, width = own.shape
    span = mine.shape[3]
    total = 2 * blocks * rows
    vmem = pl.BlockSpec(memory_space=pltpu.VMEM)
    hbm = pl.BlockSpec(memory_space=pl.ANY)
    w_mine, w_theirs, w_up, w_down = weights
    hidden = w_up.shape[1]
    return pl.pallas_call(
        functools.partial(mlp_kernel, len(after)),
        out_shape=(
            jax.ShapeDtypeStruct((blocks, rows, width), F32),
            jax.ShapeDtypeStruct((blocks, rows, width), BF16),
        ),
        in_specs=[vmem] * 8 + [hbm] * (2 + len(after)),
        out_specs=(vmem, vmem),
        scratch_shapes=[
            pltpu.VMEM((total, width), F32),
            pltpu.VMEM((total, width), BF16),
            pltpu.VMEM((total, hidden), BF16),
            pltpu.VMEM((SLOTS, width, UP_TILE), BF16),
            pltpu.VMEM((SLOTS, hidden, DOWN_TILE), BF16),
            pltpu.SemaphoreType.DMA((SLOTS,)),
            pltpu.SemaphoreType.DMA((SLOTS,)),
        ],
        compiler_params=pltpu.CompilerParams(vmem_limit_bytes=36 * MIB),
        cost_estimate=SMALL_COST,
        name="mlp",
    )(
        own, other, mine, theirs, rows_params, b_up, in_vmem(w_mine), in_vmem(w_theirs),
        in_hbm(w_up), in_hbm(w_down), *after,
    )


def swap(value):
    return lax.ppermute(value, "tensor", [(0, 1), (1, 0)])


def line_up_kernel(total, n_after, *refs):
    sources, out_ref, sems = refs[:total], refs[total + n_after], refs[-1]
    copies = [
        pltpu.make_async_copy(source, out_ref.at[number], sems.at[number])
        for number, source in enumerate(sources)
    ]
    for copy in copies:
        copy.start()
    for copy in copies:
        copy.wait()


def line_up(arrays, after, name):
    any_space = pl.BlockSpec(memory_space=pl.ANY)
    total = len(arrays)
    return pl.pallas_call(
        functools.partial(line_up_kernel, total, len(after)),
        out_shape=pltpu.VMEM((total,) + arrays[0].shape, arrays[0].dtype),
        in_specs=[any_space] * (total + len(after)),
        out_specs=any_space,
        scratch_shapes=[pltpu.SemaphoreType.DMA((total,))],
        compiler_params=pltpu.CompilerParams(vmem_limit_bytes=MIB),
        cost_estimate=SMALL_COST,
        name=name,
    )(*arrays, *after)


def w_out_place(w_out):
    core = lax.axis_index("dp") & 1
    group = lax.axis_index("groups")
    return 2 * group + core, 2 * (1 - group) + core, w_out.shape[0] // 4


def other_w_out(w_out, near, early, late):
    number, other, _ = w_out_place(w_out)
    dp_size = lax.axis_size("dp")
    sent = line_up([near], early, "w_near")
    side = lax.ppermute(sent, "groups", [(0, 1), (1, 0)])[0]
    both = line_up([near, side], late, "w_both")
    mate = lax.ppermute(both, "dp", [(d, d ^ 1) for d in range(dp_size)])
    spots = jnp.stack([number, other, number ^ 1, other ^ 1]).astype(jnp.int32)
    return join(spots, near, side, mate)


def attend_rows(projected):
    row_total, count_blocks, width = (projected.shape[0], projected.shape[1], projected.shape[3])
    head_count = width // HEAD_DIM
    queries = projected[:, :, 0].reshape(row_total, count_blocks, head_count, HEAD_DIM)
    key_rows = projected[:, :, 1].reshape(row_total, count_blocks, head_count, HEAD_DIM)
    values = projected[:, :, 2].astype(BF16).reshape(row_total, count_blocks, head_count, HEAD_DIM)
    scores = jnp.einsum(
        "qnhd,snhd->nhqs", queries, key_rows, precision=lax.Precision.HIGHEST
    ) * HEAD_DIM ** (-0.5)
    weights = jax.nn.softmax(scores, axis=-1).astype(BF16)
    attended = jnp.einsum("nhqs,snhd->qnhd", weights, values, preferred_element_type=F32)
    return attended.astype(BF16).reshape(row_total, count_blocks, width)


def encode_split(own, params):
    (pre_gain, pre_shift, w_qkv, b_qkv, w_out, b_out, mlp_gain, mlp_shift, w_up, b_up, w_down,
     b_down) = params
    block_rows = jnp.swapaxes(own, 0, 1)
    rows_dev = block_rows.shape[0]
    gathered = lax.all_gather(block_rows, "tensor", axis=0, tiled=True)
    normed = norm_rows(gathered.astype(F32), pre_gain, pre_shift).astype(BF16)
    attended = attend_rows(
        jnp.einsum("qnd,jde->qnje", normed, w_qkv, preferred_element_type=F32) + b_qkv[None, None]
    )
    partial_value = jnp.einsum("qne,ed->qnd", attended, w_out, preferred_element_type=F32)
    summed = lax.psum(partial_value.astype(BF16), "tensor").astype(F32)
    residual_all = gathered.astype(F32) + summed + b_out
    renormed = norm_rows(residual_all, mlp_gain, mlp_shift).astype(BF16)
    raised = jnp.einsum("qnd,df->qnf", renormed, w_up, preferred_element_type=F32) + b_up
    hidden = jax.nn.gelu(raised, approximate=True).astype(BF16)
    residual = lax.dynamic_slice_in_dim(
        residual_all, lax.axis_index("tensor") * rows_dev, rows_dev, 0
    )
    mlp_out = lax.psum_scatter(
        jnp.einsum("qnf,fd->qnd", hidden, w_down, preferred_element_type=F32).astype(BF16),
        "tensor", scatter_dimension=0, tiled=True,
    ).astype(F32)
    return jnp.swapaxes((residual + mlp_out + b_down).astype(BF16), 0, 1)


def per_device(paired, patches, kept_count, keep_list, *params):
    home = in_hbm(patches[0])
    keep_row = in_hbm(keep_list[0])
    kept_count = in_hbm(kept_count)
    dp_size = lax.axis_size("dp")
    device = lax.axis_index("dp").astype(jnp.int32).reshape(1)
    mates = [(d, d ^ 1) for d in range(dp_size)]
    rightwards = [(d, d + 2) for d in range(dp_size - 2)]
    leftwards = [(d + 2, d) for d in range(dp_size - 2)]

    def to_mate(value):
        return lax.ppermute(value, "dp", mates)

    def to_right(value):
        return lax.ppermute(value, "dp", rightwards)

    def to_left(value):
        return lax.ppermute(value, "dp", leftwards)

    mine, for_mate = pack(device, kept_count, keep_row, home)
    from_mate = to_mate(for_mate)
    table = make_plan(device, kept_count)
    short = table[AT_SHORT : AT_SHORT + 1].astype(F32)
    if paired:
        short = short + lax.ppermute(short, "groups", [(0, 1), (1, 0)])
    else:
        short = lax.pmax(short, "groups")
    short = short[0] > 0

    if paired:
        (pre_gain, pre_shift, w_qkv, b_qkv, w_out, b_out, mlp_gain, mlp_shift, w_up, b_up, w_down,
         b_down) = params
        rows_params = jnp.stack([pre_gain, pre_shift, mlp_gain, mlp_shift, b_out, b_down])
        b_up = b_up.reshape(1, -1)
        number, _, piece = w_out_place(w_out)
        w_near = swap(lax.dynamic_slice_in_dim(w_out, number * piece, piece, 0))

        def start(own, after):
            other = swap(own)
            mine = attend(own, other, rows_params, w_qkv, b_qkv, after)
            return own, other, mine, swap(mine)

        def finish(state, weights, after):
            keep, send = mlp(*state, rows_params, b_up, weights, after)
            return keep, swap(send)

        def result(state):
            keep, came = state
            return (keep + came.astype(F32)).astype(BF16)

    first_at, second_at, third_at = AT_DEALT, AT_DEALT + LOCAL, AT_DEALT + 2 * LOCAL
    right_0, left_0, first = choose(
        table,
        [(AT_SEND, WIDTH), (AT_SEND + WIDTH, WIDTH), (first_at, LOCAL)],
        [mine, from_mate],
        "send_0",
    )
    came_right = [to_right(right_0)]
    came_left = [to_left(left_0)]
    after = []
    if paired:
        first_state = start(first, [])
        after = [first_state[2]]
    sources = [mine, from_mate, came_right[0], mine, came_left[0]]
    at = AT_SEND + 2 * WIDTH
    right_1, left_1 = choose(table, [(at, WIDTH), (at + WIDTH, WIDTH)], sources, "send_1", after)

    def deal_slow():
        chips = dp_size // 2
        (picked,) = choose(
            table, [(AT_SLOW_SEND, MOVED * chips)], [mine, from_mate], "deal_slow"
        )
        picked = picked.reshape((chips, MOVED) + picked.shape[1:])
        spread = jnp.repeat(picked, 2, axis=0)
        arrived = lax.all_to_all(spread, "dp", split_axis=0, concat_axis=0, tiled=True)
        dealt = [arrived[table[AT_SLOW_SOURCE + j], j] for j in range(MOVED)]
        return dealt[0][None], jnp.stack(dealt[1:])

    def deal_second(after):
        return choose(
            table, [(second_at, 1), (third_at, MOVED - 1)], sources, "deal_second", after
        )

    second, spare = lax.cond(short, deal_slow, functools.partial(deal_second, [right_1]))
    came_right.append(to_right(right_1))
    came_left.append(to_left(left_1))
    after = []
    if paired:
        second_state = start(second, [])
        w_theirs = other_w_out(
            w_out, w_near, [second, first_state[3]], [came_right[1], came_left[1], second_state[3]]
        )
        weights = (w_out, w_theirs, w_up, w_down)
        after = [second_state[2]]

    def deal_third():
        sources = [mine, from_mate] + came_right + came_left
        return choose(table, [(third_at, MOVED - 1)], sources, "deal_third", after)[0]

    third = lax.cond(short, lambda: spare, deal_third)
    if paired:
        first_done = finish(first_state, weights, [third])
        third_state = start(third, [first_done[0]])
        second_done = finish(second_state, weights, [third_state[2]])
        third_done = finish(third_state, weights, [second_done[0]])
        results = jnp.concatenate([result(first_done), result(second_done), result(third_done)])
    else:
        results = jnp.concatenate([encode_split(part, params) for part in (first, second, third)])

    at = AT_BACK + 2 * WIDTH
    going_left, going_right = choose(
        table, [(at, WIDTH), (at + WIDTH, WIDTH)], [results], "back_1"
    )
    back_right, back_left = [results, to_left(going_left)], [results, to_right(going_right)]
    at = AT_BACK
    going_left, going_right = choose(
        table, [(at, WIDTH), (at + WIDTH, WIDTH)], [results] + back_right + back_left, "back_0"
    )
    back_right[0], back_left[0] = to_left(going_left), to_right(going_right)

    def home_fast():
        return choose(
            table,
            [(AT_HOME, PAGE_HALF), (AT_HOME + PAGE_HALF, PAGE_HALF)],
            [results] + back_right + back_left,
            "home_fast",
        )

    def home_slow():
        spread = lax.all_gather(results, "dp", axis=0, tiled=True)
        places = table[AT_SLOW_HOME : AT_SLOW_HOME + 2 * PAGE_HALF]
        return (
            jnp.take(spread, places[:PAGE_HALF], axis=0),
            jnp.take(spread, places[PAGE_HALF:], axis=0),
        )

    back_mine, back_mate = lax.cond(short, home_slow, home_fast)
    return merge(device, kept_count, keep_row, home, back_mine, to_mate(back_mate))[None]


def solution(mesh):
    in_specs = (
        P(("groups", "dp"), "tensor", None, None),
        P("groups"),
        P(("groups", "dp"), None),
        P(),
        P(),
        P(None, None, "tensor"),
        P(None, "tensor"),
        P("tensor", None),
        P(),
        P(),
        P(),
        P(None, "tensor"),
        P("tensor"),
        P("tensor", None),
        P(),
    )
    out_specs = P(("groups", "dp"), "tensor", None, None)
    paired = mesh.shape["tensor"] == 2 and mesh.shape["groups"] == 2
    return jax.shard_map(
        functools.partial(per_device, paired), mesh=mesh, in_specs=in_specs, out_specs=out_specs,
        check_vma=False,
    )
```

```python
import functools

import jax
import jax.numpy as jnp
from jax import lax
from jax.experimental import pallas as pl
from jax.experimental.pallas import tpu as pltpu
from jax.sharding import PartitionSpec as P

HEAD_DIM = 112
CHUNKS = (2, 2, 1)
STARTS = (0, 2, 4)
ROOM = 5
PAGE_HALF = 8
GROUP_ROWS = 16
F32 = jnp.float32
BF16 = jnp.bfloat16
MIB = 1 << 20
SMALL_COST = pl.CostEstimate(flops=1000, bytes_accessed=1000, transcendentals=0)


def norm_rows(inputs, gain, shift):
    average = jnp.mean(inputs, axis=-1, keepdims=True)
    centred = inputs - average
    variance = jnp.mean(centred * centred, axis=-1, keepdims=True)
    return centred * lax.rsqrt(variance + 1e-06) * gain + shift


def pick_at(values, index):
    total = jnp.int32(0)
    for place, value in enumerate(values):
        total = total + jnp.where(index == place, value, 0)
    return total


def page_ends_of(count_ref, pages):
    ends = [jnp.int32(0)]
    for page in range(pages):
        ends.append(ends[-1] + count_ref[page])
    return ends


def chunk_of(slot):
    number, start = jnp.int32(0), jnp.int32(0)
    for chunk in range(1, len(CHUNKS)):
        number = jnp.where(slot >= STARTS[chunk], chunk, number)
        start = jnp.where(slot >= STARTS[chunk], STARTS[chunk], start)
    return number, slot - start


def line_plan(ends, chips, core):
    held = [(ends[2 * chip] + 1 - core) >> 1 for chip in range(chips + 1)]
    total = held[chips]
    wanted = [
        jnp.clip(held[i], jnp.maximum(total - ROOM * (chips - i), 0), jnp.minimum(total, ROOM * i))
        for i in range(chips + 1)
    ]
    below, above = list(wanted), list(wanted)
    for i in range(1, chips + 1):
        below[i] = jnp.minimum(below[i], below[i - 1] + ROOM)
    for i in range(chips - 1, -1, -1):
        above[i] = jnp.maximum(above[i], above[i + 1] - ROOM)
    dealt = [(low + high) >> 1 for low, high in zip(below, above)]
    short = jnp.int32(0)
    for cut in range(1, chips):
        right = held[cut] - dealt[cut]
        most_right = jnp.minimum(held[cut] - held[cut - 1], ROOM)
        most_left = jnp.minimum(held[cut + 1] - held[cut], ROOM)
        short = short + jnp.where((right > most_right) | (-right > most_left), 1, 0)
    return held, dealt, short


AT_RIGHT = 0
AT_LEFT = AT_RIGHT + ROOM
AT_DEALT = AT_LEFT + ROOM
AT_HOME = AT_DEALT + ROOM
AT_SHORT = AT_HOME + 2 * PAGE_HALF
AT_SLOW_SOURCE = AT_SHORT + 1
AT_SLOW_PLACE = AT_SLOW_SOURCE + ROOM
AT_SLOW_HOME = AT_SLOW_PLACE + ROOM
AT_SLOW_SEND = AT_SLOW_HOME + 2 * PAGE_HALF


def plan_kernel(pages, device_ref, count_ref, table_ref):
    chips = pages // 2
    device = device_ref[0]
    core, chip = device & 1, device >> 1
    ends = page_ends_of(count_ref, pages)
    held, dealt, short = line_plan(ends, chips, core)
    short_other = line_plan(ends, chips, 1 - core)[2]
    table_ref[AT_SHORT] = jnp.where(short + short_other > 0, 1, 0)
    falls = [jnp.where(held[i] - dealt[i] > 2, 1, 0) for i in range(chips)]

    low, high = pick_at(held, chip), pick_at(held, chip + 1)
    first, end = pick_at(dealt, chip), pick_at(dealt, chip + 1)
    before = pick_at(dealt, chip - 1)
    falls_here, falls_right, falls_left = (pick_at(falls, chip + i) for i in (0, 1, -1))
    own_start, own_end = pick_at(ends, device), pick_at(ends, device + 1)
    mate_start = pick_at(ends, device ^ 1)

    def turned(offset, falling):
        return jnp.where(falling > 0, ROOM - 1 - offset, offset)

    def local_code(rank):
        position = 2 * rank + core
        own = (position >= own_start) & (position < own_end)
        return jnp.where(own, (position - own_start) >> 1, 16 + ((position - mate_start) >> 1))

    def part_code(count, source):
        number, place = chunk_of(count)
        return (source + number) * 16 + place

    for slot in range(ROOM):
        table_ref[AT_RIGHT + slot] = local_code(high - 1 - slot)
        table_ref[AT_LEFT + slot] = local_code(low + slot)
        offset = turned(jnp.int32(slot), falls_here)
        rank = first + offset
        code = jnp.where(rank < low, part_code(low - 1 - rank, 2), local_code(rank))
        code = jnp.where(rank >= high, part_code(rank - high, 2 + len(CHUNKS)), code)
        table_ref[AT_DEALT + slot] = code
        node = jnp.int32(0)
        for place in range(1, chips):
            node = node + jnp.where(held[place] <= rank, 1, 0)
        table_ref[AT_SLOW_SOURCE + slot] = 2 * node + core
        table_ref[AT_SLOW_PLACE + slot] = offset
    for half, start in enumerate((own_start, mate_start)):
        for slot in range(PAGE_HALF):
            rank = (start + ((start + core) & 1) + 2 * slot - core) >> 1
            at = half * PAGE_HALF + slot
            code = part_code(turned(rank - first, falls_here), 0)
            right = part_code(turned(rank - end, falls_right), len(CHUNKS))
            left = part_code(turned(rank - before, falls_left), 2 * len(CHUNKS))
            code = jnp.where(rank >= end, right, code)
            table_ref[AT_HOME + at] = jnp.where(rank < first, left, code)
            node, start_there, falls_there = jnp.int32(0), jnp.int32(0), falls[0]
            for place in range(1, chips):
                there = dealt[place] <= rank
                node = node + jnp.where(there, 1, 0)
                start_there = jnp.where(there, dealt[place], start_there)
                falls_there = jnp.where(there, falls[place], falls_there)
            slow = (2 * node + core) * ROOM + turned(rank - start_there, falls_there)
            table_ref[AT_SLOW_HOME + at] = jnp.clip(slow, 0, pages * ROOM - 1)
    for node in range(chips):
        for slot in range(ROOM):
            code = local_code(dealt[node] + slot)
            table_ref[AT_SLOW_SEND + node * ROOM + slot] = jnp.clip(code, 0, 31)


def make_plan(device, kept_count):
    pages = kept_count.shape[0]
    size = AT_SLOW_SEND + ROOM * (pages // 2)
    return pl.pallas_call(
        functools.partial(plan_kernel, pages),
        out_shape=jax.ShapeDtypeStruct((size,), jnp.int32),
        in_specs=[pl.BlockSpec(memory_space=pltpu.SMEM)] * 2,
        out_specs=pl.BlockSpec(memory_space=pltpu.SMEM),
        compiler_params=pltpu.CompilerParams(vmem_limit_bytes=MIB),
        cost_estimate=SMALL_COST,
        name="plan",
    )(device, kept_count)


def kept_blocks(device_ref, count_ref, keep_ref, pages):
    device = device_ref[0]
    start, count = jnp.int32(0), jnp.int32(0)
    for page in range(pages):
        start = start + jnp.where(page < device, count_ref[page], 0)
        count = count + jnp.where(page == device, count_ref[page], 0)
    blocks = []
    for half in range(2):
        offset = (start + device + half) & 1
        for slot in range(PAGE_HALF):
            index = 2 * slot + offset
            block = keep_ref[jnp.minimum(index, 2 * PAGE_HALF - 1)]
            blocks.append(jnp.where(index < count, block, -1))
    return blocks


def pack_kernel(pages, device_ref, count_ref, keep_ref, home_ref, mine_ref, mate_ref):
    page_blocks, width = home_ref.shape[1], home_ref.shape[2]
    blocks = kept_blocks(device_ref, count_ref, keep_ref, pages)
    span = GROUP_ROWS * page_blocks
    row = lax.broadcasted_iota(jnp.int32, (GROUP_ROWS, span), 0)
    column = lax.broadcasted_iota(jnp.int32, (GROUP_ROWS, span), 1)
    chosen = jnp.concatenate(
        [jnp.where(column == row * page_blocks + block, 1.0, 0.0).astype(BF16) for block in blocks],
        axis=0,
    )
    packed = jnp.dot(
        chosen, home_ref[...].reshape(span, width), preferred_element_type=F32
    ).astype(BF16)
    half = PAGE_HALF * GROUP_ROWS
    mine_ref[...] = packed[:half].reshape(PAGE_HALF, GROUP_ROWS, width)
    mate_ref[...] = packed[half:].reshape(PAGE_HALF, GROUP_ROWS, width)


def pack(device, kept_count, keep_row, home):
    rows, page_blocks, width = home.shape
    shape = jax.ShapeDtypeStruct((PAGE_HALF, rows, width), BF16)
    place = pl.BlockSpec((PAGE_HALF, GROUP_ROWS, width), lambda step, *_: (0, step, 0))
    return pl.pallas_call(
        functools.partial(pack_kernel, kept_count.shape[0]),
        out_shape=(shape, shape),
        grid_spec=pltpu.PrefetchScalarGridSpec(
            num_scalar_prefetch=3,
            grid=(rows // GROUP_ROWS,),
            in_specs=[
                pl.BlockSpec((GROUP_ROWS, page_blocks, width), lambda step, *_: (step, 0, 0))
            ],
            out_specs=(place, place),
        ),
        compiler_params=pltpu.CompilerParams(vmem_limit_bytes=16 * MIB),
        name="pack",
    )(device, kept_count, keep_row, home)


def merge_kernel(pages, device_ref, count_ref, keep_ref, home_ref, mine_ref, mate_ref, out_ref):
    page_blocks, width = home_ref.shape[1], home_ref.shape[2]
    blocks = kept_blocks(device_ref, count_ref, keep_ref, pages)
    span = GROUP_ROWS * page_blocks
    depth = 2 * PAGE_HALF * GROUP_ROWS
    row = lax.broadcasted_iota(jnp.int32, (span, depth), 0)
    column = lax.broadcasted_iota(jnp.int32, (span, depth), 1)
    slot = lax.broadcasted_iota(jnp.int32, (1, depth), 1) // GROUP_ROWS
    block_id = lax.broadcasted_iota(jnp.int32, (span, 1), 0) % page_blocks
    wanted = jnp.full((1, depth), -1, jnp.int32)
    kept = jnp.zeros((span, 1), jnp.int32)
    for place, block in enumerate(blocks):
        wanted = jnp.where(slot == place, block, wanted)
        kept = kept + jnp.where(block_id == block, 1, 0)
    chosen = jnp.where(
        (row // page_blocks == column % GROUP_ROWS) & (row % page_blocks == wanted), 1.0, 0.0
    ).astype(BF16)
    half = PAGE_HALF * GROUP_ROWS
    source = jnp.concatenate(
        [mine_ref[...].reshape(half, width), mate_ref[...].reshape(half, width)], axis=0
    )
    landed = jnp.dot(chosen, source, preferred_element_type=F32)
    home = home_ref[...].reshape(span, width).astype(F32)
    merged = jnp.where(kept > 0, landed, home).astype(BF16)
    out_ref[...] = merged.reshape(GROUP_ROWS, page_blocks, width)


def merge(device, kept_count, keep_row, home, mine, mate):
    rows, page_blocks, width = home.shape
    place = pl.BlockSpec((PAGE_HALF, GROUP_ROWS, width), lambda step, *_: (0, step, 0))
    page = pl.BlockSpec((GROUP_ROWS, page_blocks, width), lambda step, *_: (step, 0, 0))
    return pl.pallas_call(
        functools.partial(merge_kernel, kept_count.shape[0]),
        out_shape=jax.ShapeDtypeStruct(home.shape, BF16),
        grid_spec=pltpu.PrefetchScalarGridSpec(
            num_scalar_prefetch=3,
            grid=(rows // GROUP_ROWS,),
            in_specs=[page, place, place],
            out_specs=page,
        ),
        compiler_params=pltpu.CompilerParams(vmem_limit_bytes=16 * MIB),
        name="merge",
    )(device, kept_count, keep_row, home, mine, mate)


def choose_kernel(parts, n_sources, table_ref, *refs):
    sources, outs, sems = refs[:n_sources], refs[-1 - len(parts) : -1], refs[-1]
    number = 0
    for (at, total), out_ref in zip(parts, outs):
        for slot in range(total):
            code = table_ref[at + slot]
            which, place = code >> 4, code & 15
            for index, source in enumerate(sources):
                if len(sources) == 1:
                    here = which > -(1 << 20)
                elif index == 0:
                    here = which <= 0
                elif index == len(sources) - 1:
                    here = which >= index
                else:
                    here = which == index

                @pl.when(here)
                def _(source=source, out_ref=out_ref, slot=slot, place=place, number=number):
                    inside = jnp.minimum(place, source.shape[0] - 1)
                    pltpu.make_async_copy(
                        source.at[inside], out_ref.at[slot], sems.at[number]
                    ).start()

            number += 1
    number = 0
    for (_, total), out_ref in zip(parts, outs):
        for slot in range(total):
            pltpu.make_async_copy(sources[0].at[0], out_ref.at[slot], sems.at[number]).wait()
            number += 1


def choose(table, parts, sources, name, after=()):
    block = sources[0].shape[1:]
    total = sum(count for _, count in parts)
    return pl.pallas_call(
        functools.partial(choose_kernel, parts, len(sources)),
        out_shape=tuple(jax.ShapeDtypeStruct((count,) + block, BF16) for _, count in parts),
        in_specs=[pl.BlockSpec(memory_space=pltpu.SMEM)]
        + [pl.BlockSpec(memory_space=pl.ANY)] * (len(sources) + len(after)),
        out_specs=tuple(pl.BlockSpec(memory_space=pltpu.VMEM) for _ in parts),
        scratch_shapes=[pltpu.SemaphoreType.DMA((total,))],
        compiler_params=pltpu.CompilerParams(vmem_limit_bytes=8 * MIB),
        cost_estimate=SMALL_COST,
        name=name,
    )(table, *sources, *after)


def join_kernel(spots_ref, near, side, mate, out_ref, sems):
    piece = near.shape[0]
    sources = (near, side, mate.at[0], mate.at[1])
    copies = []
    for number, source in enumerate(sources):
        place = pl.ds(pl.multiple_of(spots_ref[number] * piece, piece), piece)
        copies.append(pltpu.make_async_copy(source, out_ref.at[place, :], sems.at[number]))
    for copy in copies:
        copy.start()
    for copy in copies:
        copy.wait()


def join(spots, near, side, mate):
    shape = (4 * near.shape[0], near.shape[1])
    any_space = pl.BlockSpec(memory_space=pl.ANY)
    return pl.pallas_call(
        join_kernel,
        out_shape=jax.ShapeDtypeStruct(shape, BF16),
        in_specs=[pl.BlockSpec(memory_space=pltpu.SMEM)] + [any_space] * 3,
        out_specs=pl.BlockSpec(memory_space=pltpu.VMEM),
        scratch_shapes=[pltpu.SemaphoreType.DMA((4,))],
        compiler_params=pltpu.CompilerParams(vmem_limit_bytes=8 * MIB),
        name="join",
    )(spots, near, side, mate)


def in_hbm(array):
    return pltpu.with_memory_space_constraint(array, pltpu.HBM)


def split_store(value, high_ref, low_ref):
    high = value.astype(BF16)
    high_ref[...] = high
    low_ref[...] = (value - high.astype(F32)).astype(BF16)


def attend_kernel(n_after, own_ref, other_ref, rows_ref, b_ref, w_ref, *refs):
    (out_ref, held, normed, q_high, q_low, k_high, k_low, values, scores, sems) = refs[n_after:]
    blocks, rows, width = own_ref.shape
    span = held.shape[2]
    loads = [pltpu.make_async_copy(w_ref.at[j], held.at[j], sems.at[j]) for j in range(3)]
    for load in loads:
        load.start()
    gain, shift = rows_ref[0:1, :], rows_ref[1:2, :]
    for half, ref in enumerate((own_ref, other_ref)):
        for block in range(blocks):
            at = (half * blocks + block) * rows
            normed[at : at + rows] = norm_rows(ref[block].astype(F32), gain, shift).astype(BF16)

    def project(j):
        loads[j].wait()
        product = jnp.dot(normed[...], held[j], preferred_element_type=F32)
        return product + b_ref[j : j + 1, :]

    split_store(project(0) * HEAD_DIM ** (-0.5), q_high, q_low)
    split_store(project(1), k_high, k_low)
    values[...] = project(2).astype(BF16)
    tiles = span // 128
    heads = span // HEAD_DIM
    size = 2 * rows
    lane = lax.broadcasted_iota(jnp.int32, (1, 256), 1)

    def window(head):
        tile = min(head * HEAD_DIM // 128, tiles - 2)
        first = head * HEAD_DIM - tile * 128
        inside = (lane >= first) & (lane < first + HEAD_DIM)
        return tile, slice(tile * 128, tile * 128 + 256), inside

    def one_block(block, carry):
        near = pl.ds(pl.multiple_of(block * rows, rows), rows)
        far = pl.ds(pl.multiple_of((blocks + block) * rows, rows), rows)

        def both(ref, columns):
            return jnp.concatenate([ref[near, columns], ref[far, columns]], axis=0)

        def times(left, right):
            return lax.dot_general(
                left, right, (((1,), (1,)), ((), ())), preferred_element_type=F32
            )

        for head in range(heads):
            _, columns, inside = window(head)
            none = jnp.zeros((), BF16)
            qh = jnp.where(inside, both(q_high, columns), none)
            ql = jnp.where(inside, both(q_low, columns), none)
            kh, kl = both(k_high, columns), both(k_low, columns)
            scores[head * size : (head + 1) * size, :] = (
                times(qh, kh) + times(qh, kl) + times(ql, kh)
            )
        value = scores[...]
        value = jnp.exp(value - jnp.max(value, axis=-1, keepdims=True))
        weights = (value * (1.0 / jnp.sum(value, axis=-1, keepdims=True))).astype(BF16)
        sums = [None] * tiles
        for head in range(heads):
            tile, columns, inside = window(head)
            mixed = jnp.dot(
                weights[head * size : (head + 1) * size, :], both(values, columns),
                preferred_element_type=F32,
            )
            mixed = jnp.where(inside, mixed, 0.0)
            for part in range(2):
                piece = mixed[:, part * 128 : part * 128 + 128]
                old = sums[tile + part]
                sums[tile + part] = piece if old is None else old + piece
        result = jnp.concatenate(sums, axis=1).astype(BF16)
        out_ref[0, block] = result[:rows]
        out_ref[1, block] = result[rows:]
        return carry

    lax.fori_loop(0, blocks, one_block, 0)


def attend(own, other, rows_params, w_qkv, b_qkv, after=()):
    blocks, rows, width = own.shape
    span = w_qkv.shape[2]
    total = 2 * blocks * rows
    vmem = pl.BlockSpec(memory_space=pltpu.VMEM)
    return pl.pallas_call(
        functools.partial(attend_kernel, len(after)),
        out_shape=jax.ShapeDtypeStruct((2, blocks, rows, span), BF16),
        in_specs=[vmem] * 4 + [pl.BlockSpec(memory_space=pl.ANY)] * (1 + len(after)),
        out_specs=vmem,
        scratch_shapes=[pltpu.VMEM((3, width, span), BF16), pltpu.VMEM((total, width), BF16)]
        + [pltpu.VMEM((total, span), BF16)] * 5
        + [
            pltpu.VMEM((2 * rows * (span // HEAD_DIM), 2 * rows), F32),
            pltpu.SemaphoreType.DMA((3,)),
        ],
        compiler_params=pltpu.CompilerParams(vmem_limit_bytes=28 * MIB),
        cost_estimate=SMALL_COST,
        name="attend",
    )(own, other, rows_params, b_qkv, in_hbm(w_qkv), *after)


UP_TILE = 512
DOWN_TILE = 256
SLOTS = 5


def mlp_kernel(n_after, own_ref, other_ref, mine_ref, theirs_ref, rows_ref, b_up_ref, w_mine, w_theirs,
               w_up, w_down, *refs):
    (keep_ref, send_ref, residual, renormed, hidden, outs, ups, downs, out_sems, up_sems,
     down_sems) = refs[n_after:]
    blocks, rows, width = own_ref.shape
    half = blocks * rows
    span = outs.shape[1]
    up_steps, down_steps = w_up.shape[1] // UP_TILE, width // DOWN_TILE

    def load_up(step):
        columns = pl.ds(pl.multiple_of(step * UP_TILE, UP_TILE), UP_TILE)
        slot = lax.rem(step, SLOTS)
        return pltpu.make_async_copy(w_up.at[:, columns], ups.at[slot], up_sems.at[slot])

    def load_down(step):
        columns = pl.ds(pl.multiple_of(step * DOWN_TILE, DOWN_TILE), DOWN_TILE)
        slot = lax.rem(step, SLOTS)
        return pltpu.make_async_copy(w_down.at[:, columns], downs.at[slot], down_sems.at[slot])

    out_loads = [
        pltpu.make_async_copy(source, outs.at[number], out_sems.at[number])
        for number, source in enumerate((w_mine, w_theirs))
    ]
    for load in out_loads:
        load.start()
    for slot in range(SLOTS):
        load_up(jnp.int32(slot)).start()
    gain, shift = rows_ref[2:3, :], rows_ref[3:4, :]
    mine = mine_ref[...].reshape(2 * half, span)
    theirs = jnp.concatenate(
        [theirs_ref[1].reshape(half, span), theirs_ref[0].reshape(half, span)], axis=0
    )
    for number, attended in enumerate((mine, theirs)):
        out_loads[number].wait()
        for column in range(0, width, DOWN_TILE):
            columns = slice(column, column + DOWN_TILE)
            part = jnp.dot(attended, outs[number, :, columns], preferred_element_type=F32)
            part = part.astype(BF16).astype(F32)
            if number == 0:
                residual[:, columns] = part + rows_ref[4:5, columns]
            else:
                residual[:, columns] += part
    for side, ref in enumerate((own_ref, other_ref)):
        for block in range(blocks):
            at = slice((side * blocks + block) * rows, (side * blocks + block + 1) * rows)
            value = ref[block].astype(F32) + residual[at]
            if side == 0:
                residual[at] = value
            renormed[at] = norm_rows(value, gain, shift).astype(BF16)

    def one_up(step, carry):
        load_up(step).wait()
        slot = lax.rem(step, SLOTS)
        for part in range(0, UP_TILE, 256):
            columns = pl.ds(pl.multiple_of(step * UP_TILE + part, 256), 256)
            raised = jnp.dot(
                renormed[...], ups[slot, :, part : part + 256], preferred_element_type=F32
            )
            raised = raised + b_up_ref[0:1, columns]
            hidden[:, columns] = jax.nn.gelu(raised, approximate=True).astype(BF16)
        ahead = step + SLOTS

        @pl.when(ahead < up_steps)
        def _():
            load_up(ahead).start()

        @pl.when((ahead >= up_steps) & (ahead < up_steps + down_steps))
        def _():
            load_down(ahead - up_steps).start()

        return carry

    lax.fori_loop(0, up_steps, one_up, 0)

    def one_down(step, carry):
        load_down(step).wait()
        columns = pl.ds(pl.multiple_of(step * DOWN_TILE, DOWN_TILE), DOWN_TILE)
        lowered = jnp.dot(
            hidden[...], downs[lax.rem(step, SLOTS)], preferred_element_type=F32
        )
        kept = residual[:half, columns] + lowered[:half] + rows_ref[5:6, columns]
        keep_ref[:, :, columns] = kept.reshape(blocks, rows, DOWN_TILE)
        send_ref[:, :, columns] = lowered[half:].astype(BF16).reshape(blocks, rows, DOWN_TILE)

        @pl.when(step + SLOTS < down_steps)
        def _():
            load_down(step + SLOTS).start()

        return carry

    lax.fori_loop(0, down_steps, one_down, 0)


def mlp(own, other, mine, theirs, rows_params, b_up, weights, after):
    blocks, rows, width = own.shape
    span = mine.shape[3]
    total = 2 * blocks * rows
    vmem = pl.BlockSpec(memory_space=pltpu.VMEM)
    hbm = pl.BlockSpec(memory_space=pl.ANY)
    w_mine, w_theirs, w_up, w_down = weights
    hidden = w_up.shape[1]
    return pl.pallas_call(
        functools.partial(mlp_kernel, len(after)),
        out_shape=(
            jax.ShapeDtypeStruct((blocks, rows, width), F32),
            jax.ShapeDtypeStruct((blocks, rows, width), BF16),
        ),
        in_specs=[vmem] * 6 + [hbm] * (4 + len(after)),
        out_specs=(vmem, vmem),
        scratch_shapes=[
            pltpu.VMEM((total, width), F32),
            pltpu.VMEM((total, width), BF16),
            pltpu.VMEM((total, hidden), BF16),
            pltpu.VMEM((2, span, width), BF16),
            pltpu.VMEM((SLOTS, width, UP_TILE), BF16),
            pltpu.VMEM((SLOTS, hidden, DOWN_TILE), BF16),
            pltpu.SemaphoreType.DMA((2,)),
            pltpu.SemaphoreType.DMA((SLOTS,)),
            pltpu.SemaphoreType.DMA((SLOTS,)),
        ],
        compiler_params=pltpu.CompilerParams(vmem_limit_bytes=46 * MIB),
        cost_estimate=SMALL_COST,
        name="mlp",
    )(
        own, other, mine, theirs, rows_params, b_up, in_hbm(w_mine), w_theirs, in_hbm(w_up),
        in_hbm(w_down), *after,
    )


def add_kernel(n_after, keep_ref, came_ref, *refs):
    out_ref = refs[n_after]
    out_ref[...] = (keep_ref[...] + came_ref[...].astype(F32)).astype(BF16)


def add(keep, came, after):
    vmem = pl.BlockSpec(memory_space=pltpu.VMEM)
    return pl.pallas_call(
        functools.partial(add_kernel, len(after)),
        out_shape=jax.ShapeDtypeStruct(came.shape, BF16),
        in_specs=[vmem] * 2 + [pl.BlockSpec(memory_space=pl.ANY)] * len(after),
        out_specs=vmem,
        compiler_params=pltpu.CompilerParams(vmem_limit_bytes=8 * MIB),
        cost_estimate=SMALL_COST,
        name="add",
    )(keep, came, *after)


def swap(value):
    return lax.ppermute(value, "tensor", [(0, 1), (1, 0)])


def line_up_kernel(total, n_after, *refs):
    sources, out_ref, sems = refs[:total], refs[total + n_after], refs[-1]
    copies = [
        pltpu.make_async_copy(source, out_ref.at[number], sems.at[number])
        for number, source in enumerate(sources)
    ]
    for copy in copies:
        copy.start()
    for copy in copies:
        copy.wait()


def line_up(arrays, after, name):
    any_space = pl.BlockSpec(memory_space=pl.ANY)
    total = len(arrays)
    return pl.pallas_call(
        functools.partial(line_up_kernel, total, len(after)),
        out_shape=jax.ShapeDtypeStruct((total,) + arrays[0].shape, arrays[0].dtype),
        in_specs=[any_space] * (total + len(after)),
        out_specs=pl.BlockSpec(memory_space=pltpu.VMEM),
        scratch_shapes=[pltpu.SemaphoreType.DMA((total,))],
        compiler_params=pltpu.CompilerParams(vmem_limit_bytes=8 * MIB),
        cost_estimate=SMALL_COST,
        name=name,
    )(*arrays, *after)


def w_out_place(w_out):
    core = lax.axis_index("dp") & 1
    group = lax.axis_index("groups")
    return 2 * group + core, 2 * (1 - group) + core, w_out.shape[0] // 4


def other_w_out(w_out, near, early, late):
    number, other, _ = w_out_place(w_out)
    dp_size = lax.axis_size("dp")
    sent = line_up([near], early, "w_near")
    side = lax.ppermute(sent, "groups", [(0, 1), (1, 0)])[0]
    both = line_up([near, side], late, "w_both")
    mate = lax.ppermute(both, "dp", [(d, d ^ 1) for d in range(dp_size)])
    spots = jnp.stack([number, other, number ^ 1, other ^ 1]).astype(jnp.int32)
    return join(spots, near, side, mate)


def attend_rows(projected):
    row_total, count_blocks, width = (projected.shape[0], projected.shape[1], projected.shape[3])
    head_count = width // HEAD_DIM
    queries = projected[:, :, 0].reshape(row_total, count_blocks, head_count, HEAD_DIM)
    key_rows = projected[:, :, 1].reshape(row_total, count_blocks, head_count, HEAD_DIM)
    values = projected[:, :, 2].astype(BF16).reshape(row_total, count_blocks, head_count, HEAD_DIM)
    scores = jnp.einsum(
        "qnhd,snhd->nhqs", queries, key_rows, precision=lax.Precision.HIGHEST
    ) * HEAD_DIM ** (-0.5)
    weights = jax.nn.softmax(scores, axis=-1).astype(BF16)
    attended = jnp.einsum("nhqs,snhd->qnhd", weights, values, preferred_element_type=F32)
    return attended.astype(BF16).reshape(row_total, count_blocks, width)


def encode_split(own, params):
    (pre_gain, pre_shift, w_qkv, b_qkv, w_out, b_out, mlp_gain, mlp_shift, w_up, b_up, w_down,
     b_down) = params
    block_rows = jnp.swapaxes(own, 0, 1)
    rows_dev = block_rows.shape[0]
    gathered = lax.all_gather(block_rows, "tensor", axis=0, tiled=True)
    normed = norm_rows(gathered.astype(F32), pre_gain, pre_shift).astype(BF16)
    attended = attend_rows(
        jnp.einsum("qnd,jde->qnje", normed, w_qkv, preferred_element_type=F32) + b_qkv[None, None]
    )
    partial_value = jnp.einsum("qne,ed->qnd", attended, w_out, preferred_element_type=F32)
    summed = lax.psum(partial_value.astype(BF16), "tensor").astype(F32)
    residual_all = gathered.astype(F32) + summed + b_out
    renormed = norm_rows(residual_all, mlp_gain, mlp_shift).astype(BF16)
    raised = jnp.einsum("qnd,df->qnf", renormed, w_up, preferred_element_type=F32) + b_up
    hidden = jax.nn.gelu(raised, approximate=True).astype(BF16)
    residual = lax.dynamic_slice_in_dim(
        residual_all, lax.axis_index("tensor") * rows_dev, rows_dev, 0
    )
    mlp_out = lax.psum_scatter(
        jnp.einsum("qnf,fd->qnd", hidden, w_down, preferred_element_type=F32).astype(BF16),
        "tensor", scatter_dimension=0, tiled=True,
    ).astype(F32)
    return jnp.swapaxes((residual + mlp_out + b_down).astype(BF16), 0, 1)


def per_device(paired, patches, kept_count, keep_list, *params):
    home = in_hbm(patches[0])
    keep_row = in_hbm(keep_list[0])
    kept_count = in_hbm(kept_count)
    dp_size = lax.axis_size("dp")
    device = lax.axis_index("dp").astype(jnp.int32).reshape(1)
    mates = [(d, d ^ 1) for d in range(dp_size)]
    rightwards = [(d, d + 2) for d in range(dp_size - 2)]
    leftwards = [(d + 2, d) for d in range(dp_size - 2)]

    def to_mate(value):
        return lax.ppermute(value, "dp", mates)

    def to_right(value):
        return lax.ppermute(value, "dp", rightwards)

    def to_left(value):
        return lax.ppermute(value, "dp", leftwards)

    mine, for_mate = pack(device, kept_count, keep_row, home)
    from_mate = to_mate(for_mate)
    table = make_plan(device, kept_count)
    short = table[AT_SHORT : AT_SHORT + 1].astype(F32)
    if paired:
        short = short + lax.ppermute(short, "groups", [(0, 1), (1, 0)])
    else:
        short = lax.pmax(short, "groups")
    short = short[0] > 0

    parts = tuple(zip(STARTS, CHUNKS))
    sends = [(AT_RIGHT + at, size) for at, size in parts] + [(AT_LEFT + at, size) for at, size in parts]
    going = choose(table, sends, [mine, from_mate], "send")
    came_right = [to_right(value) for value in going[: len(parts)]]
    came_left = [to_left(value) for value in going[len(parts) :]]

    def deal_fast(chunk, spare, after):
        right = [came_right[min(part, chunk)] for part in range(len(parts))]
        left = [came_left[min(part, chunk)] for part in range(len(parts))]
        wanted = [(AT_DEALT + at, size) for at, size in parts[chunk : len(parts) if spare else chunk + 1]]
        return choose(table, wanted, [mine, from_mate] + right + left, "deal_%d" % chunk, after)

    def deal_slow():
        chips = dp_size // 2
        (picked,) = choose(table, [(AT_SLOW_SEND, ROOM * chips)], [mine, from_mate], "deal_slow")
        picked = picked.reshape((chips, ROOM) + picked.shape[1:])
        spread = jnp.repeat(picked, 2, axis=0)
        arrived = lax.all_to_all(spread, "dp", split_axis=0, concat_axis=0, tiled=True)
        dealt = [arrived[table[AT_SLOW_SOURCE + j], table[AT_SLOW_PLACE + j]] for j in range(ROOM)]
        return tuple(jnp.stack(dealt[at : at + size]) for at, size in parts)

    spares = lax.cond(short, deal_slow, functools.partial(deal_fast, 0, True, ()))

    def deal(chunk, after):
        return lax.cond(
            short, lambda: spares[chunk], lambda: deal_fast(chunk, False, after)[0]
        )

    if paired:
        (pre_gain, pre_shift, w_qkv, b_qkv, w_out, b_out, mlp_gain, mlp_shift, w_up, b_up, w_down,
         b_down) = params
        rows_params = jnp.stack([pre_gain, pre_shift, mlp_gain, mlp_shift, b_out, b_down])
        b_up = b_up.reshape(1, -1)
        number, _, piece = w_out_place(w_out)
        w_near = swap(lax.dynamic_slice_in_dim(w_out, number * piece, piece, 0))

        def start(own, after):
            other = swap(own)
            mine = attend(own, other, rows_params, w_qkv, b_qkv, after)
            return own, other, mine, swap(mine)

        def finish(state, after):
            keep, send = mlp(*state, rows_params, b_up, weights, after)
            return keep, swap(send)

        blocks_0 = spares[0]
        state_0 = start(blocks_0, [])
        blocks_1 = deal(1, [])
        state_1 = start(blocks_1, [])
        blocks_2 = deal(2, [])
        state_2 = start(blocks_2, [state_1[2]])
        w_theirs = other_w_out(w_out, w_near, [blocks_0], [blocks_1, state_0[2]])
        weights = (w_out, w_theirs, w_up, w_down)
        done_0 = finish(state_0, [state_2[2]])
        done_1 = finish(state_1, [done_0[0], state_2[3]])
        done_2 = finish(state_2, [done_1[0]])
        results, from_right, from_left = [], [], []
        for done, beside in ((done_0, done_1[:1]), (done_1, done_2[:1]), (done_2, ())):
            results.append(add(*done, list(beside) + from_right[-1:] + from_left[-1:]))
            from_right.append(to_left(results[-1]))
            from_left.append(to_right(results[-1]))
    else:
        results = [
            encode_split(part, params) for part in (spares[0], deal(1, ()), deal(2, ()))
        ]
        from_right = [to_left(value) for value in results]
        from_left = [to_right(value) for value in results]

    def home_fast():
        return choose(
            table,
            [(AT_HOME, PAGE_HALF), (AT_HOME + PAGE_HALF, PAGE_HALF)],
            results + from_right + from_left,
            "home_fast",
        )

    def home_slow():
        spread = lax.all_gather(jnp.concatenate(results), "dp", axis=0, tiled=True)
        places = table[AT_SLOW_HOME : AT_SLOW_HOME + 2 * PAGE_HALF]
        return (
            jnp.take(spread, places[:PAGE_HALF], axis=0),
            jnp.take(spread, places[PAGE_HALF:], axis=0),
        )

    back_mine, back_mate = lax.cond(short, home_slow, home_fast)
    return merge(device, kept_count, keep_row, home, back_mine, to_mate(back_mate))[None]


def solution(mesh):
    in_specs = (
        P(("groups", "dp"), "tensor", None, None),
        P("groups"),
        P(("groups", "dp"), None),
        P(),
        P(),
        P(None, None, "tensor"),
        P(None, "tensor"),
        P("tensor", None),
        P(),
        P(),
        P(),
        P(None, "tensor"),
        P("tensor"),
        P("tensor", None),
        P(),
    )
    out_specs = P(("groups", "dp"), "tensor", None, None)
    paired = mesh.shape["tensor"] == 2 and mesh.shape["groups"] == 2
    return jax.shard_map(
        functools.partial(per_device, paired), mesh=mesh, in_specs=in_specs, out_specs=out_specs,
        check_vma=False,
    )
```

```python
import functools

import jax
import jax.numpy as jnp
from jax import lax
from jax.experimental import pallas as pl
from jax.experimental.pallas import tpu as pltpu
from jax.sharding import PartitionSpec as P

HEAD_DIM = 112
CHUNKS = (3, 2)
STARTS = (0, 3)
ROOM = 5
PAGE_HALF = 8
GROUP_ROWS = 16
F32 = jnp.float32
BF16 = jnp.bfloat16
MIB = 1 << 20
SMALL_COST = pl.CostEstimate(flops=1000, bytes_accessed=1000, transcendentals=0)


def norm_rows(inputs, gain, shift):
    average = jnp.mean(inputs, axis=-1, keepdims=True)
    centred = inputs - average
    variance = jnp.mean(centred * centred, axis=-1, keepdims=True)
    return centred * lax.rsqrt(variance + 1e-06) * gain + shift


def pick_at(values, index):
    total = jnp.int32(0)
    for place, value in enumerate(values):
        total = total + jnp.where(index == place, value, 0)
    return total


def page_ends_of(count_ref, pages):
    ends = [jnp.int32(0)]
    for page in range(pages):
        ends.append(ends[-1] + count_ref[page])
    return ends


def chunk_of(slot):
    number, start = jnp.int32(0), jnp.int32(0)
    for chunk in range(1, len(CHUNKS)):
        number = jnp.where(slot >= STARTS[chunk], chunk, number)
        start = jnp.where(slot >= STARTS[chunk], STARTS[chunk], start)
    return number, slot - start


def line_plan(ends, chips, core):
    held = [(ends[2 * chip] + 1 - core) >> 1 for chip in range(chips + 1)]
    total = held[chips]
    wanted = [
        jnp.clip(held[i], jnp.maximum(total - ROOM * (chips - i), 0), jnp.minimum(total, ROOM * i))
        for i in range(chips + 1)
    ]
    below, above = list(wanted), list(wanted)
    for i in range(1, chips + 1):
        below[i] = jnp.minimum(below[i], below[i - 1] + ROOM)
    for i in range(chips - 1, -1, -1):
        above[i] = jnp.maximum(above[i], above[i + 1] - ROOM)
    dealt = [(low + high) >> 1 for low, high in zip(below, above)]
    short = jnp.int32(0)
    for cut in range(1, chips):
        right = held[cut] - dealt[cut]
        most_right = jnp.minimum(held[cut] - held[cut - 1], ROOM)
        most_left = jnp.minimum(held[cut + 1] - held[cut], ROOM)
        short = short + jnp.where((right > most_right) | (-right > most_left), 1, 0)
    return held, dealt, short


AT_RIGHT = 0
AT_LEFT = AT_RIGHT + ROOM
AT_DEALT = AT_LEFT + ROOM
AT_HOME = AT_DEALT + ROOM
AT_SHORT = AT_HOME + 2 * PAGE_HALF
AT_SLOW_SOURCE = AT_SHORT + 1
AT_SLOW_PLACE = AT_SLOW_SOURCE + ROOM
AT_SLOW_HOME = AT_SLOW_PLACE + ROOM
AT_IN_ORDER = AT_SLOW_HOME + 2 * PAGE_HALF
AT_SLOW_SEND = AT_IN_ORDER + 2 * PAGE_HALF


def plan_kernel(pages, device_ref, count_ref, table_ref):
    chips = pages // 2
    device = device_ref[0]
    core, chip = device & 1, device >> 1
    ends = page_ends_of(count_ref, pages)
    held, dealt, short = line_plan(ends, chips, core)
    held_mate, dealt_mate, short_mate = line_plan(ends, chips, 1 - core)
    table_ref[AT_SHORT] = jnp.where(short + short_mate > 0, 1, 0)
    falls, falls_mate = (
        [jnp.where(ranks[i] - ranks_dealt[i] > 2, 1, 0) for i in range(chips)]
        for ranks, ranks_dealt in ((held, dealt), (held_mate, dealt_mate))
    )

    low, high = pick_at(held, chip), pick_at(held, chip + 1)
    first, end = pick_at(dealt, chip), pick_at(dealt, chip + 1)
    falls_here = pick_at(falls, chip)
    own_start, own_end = pick_at(ends, device), pick_at(ends, device + 1)
    mate_start = pick_at(ends, device ^ 1)

    def turned(offset, falling):
        return jnp.where(falling > 0, ROOM - 1 - offset, offset)

    def local_code(rank):
        position = 2 * rank + core
        own = (position >= own_start) & (position < own_end)
        return jnp.where(own, (position - own_start) >> 1, 16 + ((position - mate_start) >> 1))

    def part_code(count, source):
        number, place = chunk_of(count)
        return (source + number) * 16 + place

    for slot in range(ROOM):
        table_ref[AT_RIGHT + slot] = local_code(high - 1 - slot)
        table_ref[AT_LEFT + slot] = local_code(low + slot)
        offset = turned(jnp.int32(slot), falls_here)
        rank = first + offset
        code = jnp.where(rank < low, part_code(low - 1 - rank, 2), local_code(rank))
        code = jnp.where(rank >= high, part_code(rank - high, 2 + len(CHUNKS)), code)
        table_ref[AT_DEALT + slot] = code
        node = jnp.int32(0)
        for place in range(1, chips):
            node = node + jnp.where(held[place] <= rank, 1, 0)
        table_ref[AT_SLOW_SOURCE + slot] = 2 * node + core
        table_ref[AT_SLOW_PLACE + slot] = offset
    sides = len(CHUNKS)
    for half, (ranks_dealt, turns) in enumerate(((dealt, falls), (dealt_mate, falls_mate))):
        lane = core ^ half
        here, there = pick_at(ranks_dealt, chip), pick_at(ranks_dealt, chip + 1)
        before = pick_at(ranks_dealt, chip - 1)
        turns_here, turns_right, turns_left = (pick_at(turns, chip + i) for i in (0, 1, -1))
        for slot in range(PAGE_HALF):
            rank = (own_start + ((own_start + lane) & 1) + 2 * slot - lane) >> 1
            at = half * PAGE_HALF + slot
            base = 3 * sides * half
            code = part_code(turned(rank - here, turns_here), base)
            right = part_code(turned(rank - there, turns_right), base + sides)
            left = part_code(turned(rank - before, turns_left), base + 2 * sides)
            code = jnp.where(rank >= there, right, code)
            table_ref[AT_HOME + at] = jnp.where(rank < here, left, code)
            node, start_there, turns_there = jnp.int32(0), jnp.int32(0), turns[0]
            for place in range(1, chips):
                beyond = ranks_dealt[place] <= rank
                node = node + jnp.where(beyond, 1, 0)
                start_there = jnp.where(beyond, ranks_dealt[place], start_there)
                turns_there = jnp.where(beyond, turns[place], turns_there)
            slow = (2 * node + lane) * ROOM + turned(rank - start_there, turns_there)
            table_ref[AT_SLOW_HOME + at] = jnp.clip(slow, 0, pages * ROOM - 1)
            table_ref[AT_IN_ORDER + at] = jnp.int32((6 * sides + half) * 16 + slot)
    for node in range(chips):
        for slot in range(ROOM):
            code = local_code(dealt[node] + slot)
            table_ref[AT_SLOW_SEND + node * ROOM + slot] = jnp.clip(code, 0, 31)


def make_plan(device, kept_count):
    pages = kept_count.shape[0]
    size = AT_SLOW_SEND + ROOM * (pages // 2)
    return pl.pallas_call(
        functools.partial(plan_kernel, pages),
        out_shape=jax.ShapeDtypeStruct((size,), jnp.int32),
        in_specs=[pl.BlockSpec(memory_space=pltpu.SMEM)] * 2,
        out_specs=pl.BlockSpec(memory_space=pltpu.SMEM),
        compiler_params=pltpu.CompilerParams(vmem_limit_bytes=MIB),
        cost_estimate=SMALL_COST,
        name="plan",
    )(device, kept_count)


def kept_blocks(device_ref, count_ref, keep_ref, pages):
    device = device_ref[0]
    start, count = jnp.int32(0), jnp.int32(0)
    for page in range(pages):
        start = start + jnp.where(page < device, count_ref[page], 0)
        count = count + jnp.where(page == device, count_ref[page], 0)
    blocks = []
    for half in range(2):
        offset = (start + device + half) & 1
        for slot in range(PAGE_HALF):
            index = 2 * slot + offset
            block = keep_ref[jnp.minimum(index, 2 * PAGE_HALF - 1)]
            blocks.append(jnp.where(index < count, block, -1))
    return blocks


def kept_blocks_once(device_ref, count_ref, keep_ref, pages, held):
    @pl.when(pl.program_id(0) == 0)
    def _():
        for slot, block in enumerate(kept_blocks(device_ref, count_ref, keep_ref, pages)):
            held[slot] = block

    return [held[slot] for slot in range(2 * PAGE_HALF)]


def pack_kernel(pages, device_ref, count_ref, keep_ref, home_ref, mine_ref, mate_ref, held):
    page_blocks, width = home_ref.shape[1], home_ref.shape[2]
    blocks = kept_blocks_once(device_ref, count_ref, keep_ref, pages, held)
    span = GROUP_ROWS * page_blocks
    row = lax.broadcasted_iota(jnp.int32, (GROUP_ROWS, span), 0)
    column = lax.broadcasted_iota(jnp.int32, (GROUP_ROWS, span), 1)
    chosen = jnp.concatenate(
        [jnp.where(column == row * page_blocks + block, 1.0, 0.0).astype(BF16) for block in blocks],
        axis=0,
    )
    packed = jnp.dot(
        chosen, home_ref[...].reshape(span, width), preferred_element_type=F32
    ).astype(BF16)
    half = PAGE_HALF * GROUP_ROWS
    mine_ref[...] = packed[:half].reshape(PAGE_HALF, GROUP_ROWS, width)
    mate_ref[...] = packed[half:].reshape(PAGE_HALF, GROUP_ROWS, width)


def pack(device, kept_count, keep_row, home):
    rows, page_blocks, width = home.shape
    shape = jax.ShapeDtypeStruct((PAGE_HALF, rows, width), BF16)
    place = pl.BlockSpec((PAGE_HALF, GROUP_ROWS, width), lambda step, *_: (0, step, 0))
    return pl.pallas_call(
        functools.partial(pack_kernel, kept_count.shape[0]),
        out_shape=(shape, shape),
        grid_spec=pltpu.PrefetchScalarGridSpec(
            num_scalar_prefetch=3,
            grid=(rows // GROUP_ROWS,),
            in_specs=[
                pl.BlockSpec((GROUP_ROWS, page_blocks, width), lambda step, *_: (step, 0, 0))
            ],
            out_specs=(place, place),
            scratch_shapes=[pltpu.SMEM((2 * PAGE_HALF,), jnp.int32)],
        ),
        compiler_params=pltpu.CompilerParams(vmem_limit_bytes=16 * MIB),
        name="pack",
    )(device, kept_count, keep_row, home)


def merge_kernel(pages, total, device_ref, count_ref, keep_ref, table_ref, slow_ref, home_ref, *refs):
    sources = refs[:total]
    out_ref, held, landed, sems = refs[total:]
    page_blocks, width = home_ref.shape[1], home_ref.shape[2]
    step = pl.program_id(0)
    slots = 2 * PAGE_HALF

    @pl.when(step == 0)
    def _():
        at = jnp.where(slow_ref[0] > 0, AT_IN_ORDER, AT_HOME)
        start_copies(
            sources,
            [(table_ref[at + slot], landed.at[slot], sems.at[slot]) for slot in range(slots)],
        )

    blocks = kept_blocks_once(device_ref, count_ref, keep_ref, pages, held)
    span = GROUP_ROWS * page_blocks
    depth = slots * GROUP_ROWS
    row = lax.broadcasted_iota(jnp.int32, (span, depth), 0)
    column = lax.broadcasted_iota(jnp.int32, (span, depth), 1)
    slot_id = lax.broadcasted_iota(jnp.int32, (1, depth), 1) // GROUP_ROWS
    block_id = lax.broadcasted_iota(jnp.int32, (span, 1), 0) % page_blocks
    wanted = jnp.full((1, depth), -1, jnp.int32)
    kept = jnp.zeros((span, 1), jnp.int32)
    for place, block in enumerate(blocks):
        wanted = jnp.where(slot_id == place, block, wanted)
        kept = kept + jnp.where(block_id == block, 1, 0)
    chosen = jnp.where(
        (row // page_blocks == column % GROUP_ROWS) & (row % page_blocks == wanted), 1.0, 0.0
    ).astype(BF16)

    @pl.when(step == 0)
    def _():
        for slot in range(slots):
            pltpu.make_async_copy(sources[0].at[0], landed.at[slot], sems.at[slot]).wait()

    rows = pl.ds(pl.multiple_of(step * GROUP_ROWS, GROUP_ROWS), GROUP_ROWS)
    source = landed[:, rows, :].reshape(depth, width)
    result = jnp.dot(chosen, source, preferred_element_type=F32)
    home = home_ref[...].reshape(span, width).astype(F32)
    merged = jnp.where(kept > 0, result, home).astype(BF16)
    out_ref[...] = merged.reshape(GROUP_ROWS, page_blocks, width)


def merge(device, kept_count, keep_row, table, slow, home, sources):
    rows, page_blocks, width = home.shape
    page = pl.BlockSpec((GROUP_ROWS, page_blocks, width), lambda step, *_: (step, 0, 0))
    slots = 2 * PAGE_HALF
    return pl.pallas_call(
        functools.partial(merge_kernel, kept_count.shape[0], len(sources)),
        out_shape=jax.ShapeDtypeStruct(home.shape, BF16),
        grid_spec=pltpu.PrefetchScalarGridSpec(
            num_scalar_prefetch=5,
            grid=(rows // GROUP_ROWS,),
            in_specs=[page] + [pl.BlockSpec(memory_space=pl.ANY)] * len(sources),
            out_specs=page,
            scratch_shapes=[
                pltpu.SMEM((slots,), jnp.int32),
                pltpu.VMEM((slots, rows, width), BF16),
                pltpu.SemaphoreType.DMA((slots,)),
            ],
        ),
        compiler_params=pltpu.CompilerParams(vmem_limit_bytes=20 * MIB),
        cost_estimate=SMALL_COST,
        name="merge",
    )(device, kept_count, keep_row, table, slow, home, *sources)


def start_copies(sources, wanted):
    for code, target, sem in wanted:
        which, place = code >> 4, code & 15
        for index, source in enumerate(sources):
            if len(sources) == 1:
                here = which > -(1 << 20)
            elif index == 0:
                here = which <= 0
            elif index == len(sources) - 1:
                here = which >= index
            else:
                here = which == index

            @pl.when(here)
            def _(source=source, place=place, target=target, sem=sem):
                inside = jnp.minimum(place, source.shape[0] - 1)
                pltpu.make_async_copy(source.at[inside], target, sem).start()


def choose_kernel(parts, n_sources, table_ref, *refs):
    sources, outs, sems = refs[:n_sources], refs[-1 - len(parts) : -1], refs[-1]
    targets = [
        (at + slot, out_ref.at[slot])
        for (at, total), out_ref in zip(parts, outs)
        for slot in range(total)
    ]
    start_copies(
        sources,
        [(table_ref[at], target, sems.at[number]) for number, (at, target) in enumerate(targets)],
    )
    for number, (_, target) in enumerate(targets):
        pltpu.make_async_copy(sources[0].at[0], target, sems.at[number]).wait()


def choose(table, parts, sources, name, after=()):
    block = sources[0].shape[1:]
    total = sum(count for _, count in parts)
    return pl.pallas_call(
        functools.partial(choose_kernel, parts, len(sources)),
        out_shape=tuple(jax.ShapeDtypeStruct((count,) + block, BF16) for _, count in parts),
        in_specs=[pl.BlockSpec(memory_space=pltpu.SMEM)]
        + [pl.BlockSpec(memory_space=pl.ANY)] * (len(sources) + len(after)),
        out_specs=tuple(pl.BlockSpec(memory_space=pltpu.VMEM) for _ in parts),
        scratch_shapes=[pltpu.SemaphoreType.DMA((total,))],
        compiler_params=pltpu.CompilerParams(vmem_limit_bytes=8 * MIB),
        cost_estimate=SMALL_COST,
        name=name,
    )(table, *sources, *after)


def join_kernel(spots_ref, near, side, mate, out_ref, sems):
    piece = near.shape[0]
    sources = (near, side, mate.at[0], mate.at[1])
    copies = []
    for number, source in enumerate(sources):
        place = pl.ds(pl.multiple_of(spots_ref[number] * piece, piece), piece)
        copies.append(pltpu.make_async_copy(source, out_ref.at[place, :], sems.at[number]))
    for copy in copies:
        copy.start()
    for copy in copies:
        copy.wait()


def join(spots, near, side, mate):
    shape = (4 * near.shape[0], near.shape[1])
    any_space = pl.BlockSpec(memory_space=pl.ANY)
    return pl.pallas_call(
        join_kernel,
        out_shape=jax.ShapeDtypeStruct(shape, BF16),
        in_specs=[pl.BlockSpec(memory_space=pltpu.SMEM)] + [any_space] * 3,
        out_specs=pl.BlockSpec(memory_space=pltpu.VMEM),
        scratch_shapes=[pltpu.SemaphoreType.DMA((4,))],
        compiler_params=pltpu.CompilerParams(vmem_limit_bytes=8 * MIB),
        name="join",
    )(spots, near, side, mate)


def in_hbm(array):
    return pltpu.with_memory_space_constraint(array, pltpu.HBM)


def split_store(value, high_ref, low_ref):
    high = value.astype(BF16)
    high_ref[...] = high
    low_ref[...] = (value - high.astype(F32)).astype(BF16)


def attend_kernel(n_after, own_ref, other_ref, rows_ref, b_ref, w_ref, *refs):
    (out_ref, held, normed, q_high, q_low, k_high, k_low, values, scores, sems) = refs[n_after:]
    blocks, rows, width = own_ref.shape
    span = held.shape[2]
    loads = [pltpu.make_async_copy(w_ref.at[j], held.at[j], sems.at[j]) for j in range(3)]
    for load in loads:
        load.start()
    gain, shift = rows_ref[0:1, :], rows_ref[1:2, :]
    for half, ref in enumerate((own_ref, other_ref)):
        for block in range(blocks):
            at = (half * blocks + block) * rows
            normed[at : at + rows] = norm_rows(ref[block].astype(F32), gain, shift).astype(BF16)

    def project(j):
        loads[j].wait()
        product = jnp.dot(normed[...], held[j], preferred_element_type=F32)
        return product + b_ref[j : j + 1, :]

    split_store(project(0) * HEAD_DIM ** (-0.5), q_high, q_low)
    split_store(project(1), k_high, k_low)
    values[...] = project(2).astype(BF16)
    tiles = span // 128
    heads = span // HEAD_DIM
    size = 2 * rows
    lane = lax.broadcasted_iota(jnp.int32, (1, 256), 1)

    def window(head):
        tile = min(head * HEAD_DIM // 128, tiles - 2)
        first = head * HEAD_DIM - tile * 128
        inside = (lane >= first) & (lane < first + HEAD_DIM)
        return tile, slice(tile * 128, tile * 128 + 256), inside

    def one_block(block, carry):
        near = pl.ds(pl.multiple_of(block * rows, rows), rows)
        far = pl.ds(pl.multiple_of((blocks + block) * rows, rows), rows)

        def both(ref, columns):
            return jnp.concatenate([ref[near, columns], ref[far, columns]], axis=0)

        def times(left, right):
            return lax.dot_general(
                left, right, (((1,), (1,)), ((), ())), preferred_element_type=F32
            )

        for head in range(heads):
            _, columns, inside = window(head)
            none = jnp.zeros((), BF16)
            qh = jnp.where(inside, both(q_high, columns), none)
            ql = jnp.where(inside, both(q_low, columns), none)
            kh, kl = both(k_high, columns), both(k_low, columns)
            scores[head * size : (head + 1) * size, :] = (
                times(qh, kh) + times(qh, kl) + times(ql, kh)
            )
        value = scores[...]
        value = jnp.exp(value - jnp.max(value, axis=-1, keepdims=True))
        weights = (value * (1.0 / jnp.sum(value, axis=-1, keepdims=True))).astype(BF16)
        sums = [None] * tiles
        for head in range(heads):
            tile, columns, inside = window(head)
            mixed = jnp.dot(
                weights[head * size : (head + 1) * size, :], both(values, columns),
                preferred_element_type=F32,
            )
            mixed = jnp.where(inside, mixed, 0.0)
            for part in range(2):
                piece = mixed[:, part * 128 : part * 128 + 128]
                old = sums[tile + part]
                sums[tile + part] = piece if old is None else old + piece
        result = jnp.concatenate(sums, axis=1).astype(BF16)
        out_ref[0, block] = result[:rows]
        out_ref[1, block] = result[rows:]
        return carry

    lax.fori_loop(0, blocks, one_block, 0)


def attend(own, other, rows_params, w_qkv, b_qkv, after=()):
    blocks, rows, width = own.shape
    span = w_qkv.shape[2]
    total = 2 * blocks * rows
    vmem = pl.BlockSpec(memory_space=pltpu.VMEM)
    return pl.pallas_call(
        functools.partial(attend_kernel, len(after)),
        out_shape=jax.ShapeDtypeStruct((2, blocks, rows, span), BF16),
        in_specs=[vmem] * 4 + [pl.BlockSpec(memory_space=pl.ANY)] * (1 + len(after)),
        out_specs=vmem,
        scratch_shapes=[pltpu.VMEM((3, width, span), BF16), pltpu.VMEM((total, width), BF16)]
        + [pltpu.VMEM((total, span), BF16)] * 5
        + [
            pltpu.VMEM((2 * rows * (span // HEAD_DIM), 2 * rows), F32),
            pltpu.SemaphoreType.DMA((3,)),
        ],
        compiler_params=pltpu.CompilerParams(vmem_limit_bytes=28 * MIB),
        cost_estimate=SMALL_COST,
        name="attend",
    )(own, other, rows_params, b_qkv, in_hbm(w_qkv), *after)


UP_TILE = 512
DOWN_TILE = 256
SLOTS = 5


def mlp_kernel(n_after, own_ref, other_ref, mine_ref, theirs_ref, rows_ref, b_up_ref, w_mine, w_theirs,
               w_up, w_down, *refs):
    (keep_ref, send_ref, residual, renormed, hidden, outs, ups, downs, out_sems, up_sems,
     down_sems) = refs[n_after:]
    blocks, rows, width = own_ref.shape
    half = blocks * rows
    span = outs.shape[1]
    up_steps, down_steps = w_up.shape[1] // UP_TILE, width // DOWN_TILE

    def load_up(step):
        columns = pl.ds(pl.multiple_of(step * UP_TILE, UP_TILE), UP_TILE)
        slot = lax.rem(step, SLOTS)
        return pltpu.make_async_copy(w_up.at[:, columns], ups.at[slot], up_sems.at[slot])

    def load_down(step):
        columns = pl.ds(pl.multiple_of(step * DOWN_TILE, DOWN_TILE), DOWN_TILE)
        slot = lax.rem(step, SLOTS)
        return pltpu.make_async_copy(w_down.at[:, columns], downs.at[slot], down_sems.at[slot])

    out_loads = [
        pltpu.make_async_copy(source, outs.at[number], out_sems.at[number])
        for number, source in enumerate((w_mine, w_theirs))
    ]
    for load in out_loads:
        load.start()
    for slot in range(SLOTS):
        load_up(jnp.int32(slot)).start()
    gain, shift = rows_ref[2:3, :], rows_ref[3:4, :]
    mine = mine_ref[...].reshape(2 * half, span)
    theirs = jnp.concatenate(
        [theirs_ref[1].reshape(half, span), theirs_ref[0].reshape(half, span)], axis=0
    )
    for number, attended in enumerate((mine, theirs)):
        out_loads[number].wait()
        for column in range(0, width, DOWN_TILE):
            columns = slice(column, column + DOWN_TILE)
            part = jnp.dot(attended, outs[number, :, columns], preferred_element_type=F32)
            part = part.astype(BF16).astype(F32)
            if number == 0:
                residual[:, columns] = part + rows_ref[4:5, columns]
            else:
                residual[:, columns] += part
    for side, ref in enumerate((own_ref, other_ref)):
        for block in range(blocks):
            at = slice((side * blocks + block) * rows, (side * blocks + block + 1) * rows)
            value = ref[block].astype(F32) + residual[at]
            if side == 0:
                residual[at] = value
            renormed[at] = norm_rows(value, gain, shift).astype(BF16)

    def one_up(step, carry):
        load_up(step).wait()
        slot = lax.rem(step, SLOTS)
        for part in range(0, UP_TILE, 256):
            columns = pl.ds(pl.multiple_of(step * UP_TILE + part, 256), 256)
            raised = jnp.dot(
                renormed[...], ups[slot, :, part : part + 256], preferred_element_type=F32
            )
            raised = raised + b_up_ref[0:1, columns]
            hidden[:, columns] = jax.nn.gelu(raised, approximate=True).astype(BF16)
        ahead = step + SLOTS

        @pl.when(ahead < up_steps)
        def _():
            load_up(ahead).start()

        @pl.when((ahead >= up_steps) & (ahead < up_steps + down_steps))
        def _():
            load_down(ahead - up_steps).start()

        return carry

    lax.fori_loop(0, up_steps, one_up, 0)

    def one_down(step, carry):
        load_down(step).wait()
        columns = pl.ds(pl.multiple_of(step * DOWN_TILE, DOWN_TILE), DOWN_TILE)
        lowered = jnp.dot(
            hidden[...], downs[lax.rem(step, SLOTS)], preferred_element_type=F32
        )
        kept = residual[:half, columns] + lowered[:half] + rows_ref[5:6, columns]
        keep_ref[:, :, columns] = kept.reshape(blocks, rows, DOWN_TILE)
        send_ref[:, :, columns] = lowered[half:].astype(BF16).reshape(blocks, rows, DOWN_TILE)

        @pl.when(step + SLOTS < down_steps)
        def _():
            load_down(step + SLOTS).start()

        return carry

    lax.fori_loop(0, down_steps, one_down, 0)


def mlp(own, other, mine, theirs, rows_params, b_up, weights, after):
    blocks, rows, width = own.shape
    span = mine.shape[3]
    total = 2 * blocks * rows
    vmem = pl.BlockSpec(memory_space=pltpu.VMEM)
    hbm = pl.BlockSpec(memory_space=pl.ANY)
    w_mine, w_theirs, w_up, w_down = weights
    hidden = w_up.shape[1]
    return pl.pallas_call(
        functools.partial(mlp_kernel, len(after)),
        out_shape=(
            jax.ShapeDtypeStruct((blocks, rows, width), F32),
            jax.ShapeDtypeStruct((blocks, rows, width), BF16),
        ),
        in_specs=[vmem] * 6 + [hbm] * (4 + len(after)),
        out_specs=(vmem, vmem),
        scratch_shapes=[
            pltpu.VMEM((total, width), F32),
            pltpu.VMEM((total, width), BF16),
            pltpu.VMEM((total, hidden), BF16),
            pltpu.VMEM((2, span, width), BF16),
            pltpu.VMEM((SLOTS, width, UP_TILE), BF16),
            pltpu.VMEM((SLOTS, hidden, DOWN_TILE), BF16),
            pltpu.SemaphoreType.DMA((2,)),
            pltpu.SemaphoreType.DMA((SLOTS,)),
            pltpu.SemaphoreType.DMA((SLOTS,)),
        ],
        compiler_params=pltpu.CompilerParams(vmem_limit_bytes=46 * MIB),
        cost_estimate=pl.CostEstimate(
            flops=4 * total * width * (span + hidden),
            bytes_accessed=4 * width * (span + hidden),
            transcendentals=0,
        ),
        name="mlp",
    )(
        own, other, mine, theirs, rows_params, b_up, in_hbm(w_mine), w_theirs, in_hbm(w_up),
        in_hbm(w_down), *after,
    )


def add_kernel(n_after, keep_ref, came_ref, *refs):
    out_ref = refs[n_after]
    out_ref[...] = (keep_ref[...] + came_ref[...].astype(F32)).astype(BF16)


def add(keep, came, after):
    vmem = pl.BlockSpec(memory_space=pltpu.VMEM)
    return pl.pallas_call(
        functools.partial(add_kernel, len(after)),
        out_shape=jax.ShapeDtypeStruct(came.shape, BF16),
        in_specs=[vmem] * 2 + [pl.BlockSpec(memory_space=pl.ANY)] * len(after),
        out_specs=vmem,
        compiler_params=pltpu.CompilerParams(vmem_limit_bytes=8 * MIB),
        cost_estimate=SMALL_COST,
        name="add",
    )(keep, came, *after)


def swap(value):
    return lax.ppermute(value, "tensor", [(0, 1), (1, 0)])


def line_up_kernel(total, n_after, *refs):
    sources, out_ref, sems = refs[:total], refs[total + n_after], refs[-1]
    copies = [
        pltpu.make_async_copy(source, out_ref.at[number], sems.at[number])
        for number, source in enumerate(sources)
    ]
    for copy in copies:
        copy.start()
    for copy in copies:
        copy.wait()


def line_up(arrays, after, name):
    any_space = pl.BlockSpec(memory_space=pl.ANY)
    total = len(arrays)
    return pl.pallas_call(
        functools.partial(line_up_kernel, total, len(after)),
        out_shape=jax.ShapeDtypeStruct((total,) + arrays[0].shape, arrays[0].dtype),
        in_specs=[any_space] * (total + len(after)),
        out_specs=pl.BlockSpec(memory_space=pltpu.VMEM),
        scratch_shapes=[pltpu.SemaphoreType.DMA((total,))],
        compiler_params=pltpu.CompilerParams(vmem_limit_bytes=8 * MIB),
        cost_estimate=SMALL_COST,
        name=name,
    )(*arrays, *after)


def w_out_place(w_out):
    core = lax.axis_index("dp") & 1
    group = lax.axis_index("groups")
    return 2 * group + core, 2 * (1 - group) + core, w_out.shape[0] // 4


def piece_kernel(n_after, number_ref, w_ref, *refs):
    out_ref, sem = refs[n_after:]
    piece = out_ref.shape[0]
    rows = pl.ds(pl.multiple_of(number_ref[0] * piece, piece), piece)
    copy = pltpu.make_async_copy(w_ref.at[rows, :], out_ref, sem)
    copy.start()
    copy.wait()


def w_out_piece(w_out, after):
    number, _, piece = w_out_place(w_out)
    any_space = pl.BlockSpec(memory_space=pl.ANY)
    return pl.pallas_call(
        functools.partial(piece_kernel, len(after)),
        out_shape=jax.ShapeDtypeStruct((piece, w_out.shape[1]), BF16),
        in_specs=[pl.BlockSpec(memory_space=pltpu.SMEM)] + [any_space] * (1 + len(after)),
        out_specs=pl.BlockSpec(memory_space=pltpu.VMEM),
        scratch_shapes=[pltpu.SemaphoreType.DMA],
        compiler_params=pltpu.CompilerParams(vmem_limit_bytes=4 * MIB),
        cost_estimate=SMALL_COST,
        name="w_piece",
    )(number.astype(jnp.int32).reshape(1), in_hbm(w_out), *after)


def other_w_out(w_out, near, early, late):
    number, other, _ = w_out_place(w_out)
    dp_size = lax.axis_size("dp")
    sent = line_up([near], early, "w_near")
    side = lax.ppermute(sent, "groups", [(0, 1), (1, 0)])[0]
    both = line_up([near, side], late, "w_both")
    mate = lax.ppermute(both, "dp", [(d, d ^ 1) for d in range(dp_size)])
    spots = jnp.stack([number, other, number ^ 1, other ^ 1]).astype(jnp.int32)
    return join(spots, near, side, mate)


def attend_rows(projected):
    row_total, count_blocks, width = (projected.shape[0], projected.shape[1], projected.shape[3])
    head_count = width // HEAD_DIM
    queries = projected[:, :, 0].reshape(row_total, count_blocks, head_count, HEAD_DIM)
    key_rows = projected[:, :, 1].reshape(row_total, count_blocks, head_count, HEAD_DIM)
    values = projected[:, :, 2].astype(BF16).reshape(row_total, count_blocks, head_count, HEAD_DIM)
    scores = jnp.einsum(
        "qnhd,snhd->nhqs", queries, key_rows, precision=lax.Precision.HIGHEST
    ) * HEAD_DIM ** (-0.5)
    weights = jax.nn.softmax(scores, axis=-1).astype(BF16)
    attended = jnp.einsum("nhqs,snhd->qnhd", weights, values, preferred_element_type=F32)
    return attended.astype(BF16).reshape(row_total, count_blocks, width)


def encode_split(own, params):
    (pre_gain, pre_shift, w_qkv, b_qkv, w_out, b_out, mlp_gain, mlp_shift, w_up, b_up, w_down,
     b_down) = params
    block_rows = jnp.swapaxes(own, 0, 1)
    rows_dev = block_rows.shape[0]
    gathered = lax.all_gather(block_rows, "tensor", axis=0, tiled=True)
    normed = norm_rows(gathered.astype(F32), pre_gain, pre_shift).astype(BF16)
    attended = attend_rows(
        jnp.einsum("qnd,jde->qnje", normed, w_qkv, preferred_element_type=F32) + b_qkv[None, None]
    )
    partial_value = jnp.einsum("qne,ed->qnd", attended, w_out, preferred_element_type=F32)
    summed = lax.psum(partial_value.astype(BF16), "tensor").astype(F32)
    residual_all = gathered.astype(F32) + summed + b_out
    renormed = norm_rows(residual_all, mlp_gain, mlp_shift).astype(BF16)
    raised = jnp.einsum("qnd,df->qnf", renormed, w_up, preferred_element_type=F32) + b_up
    hidden = jax.nn.gelu(raised, approximate=True).astype(BF16)
    residual = lax.dynamic_slice_in_dim(
        residual_all, lax.axis_index("tensor") * rows_dev, rows_dev, 0
    )
    mlp_out = lax.psum_scatter(
        jnp.einsum("qnf,fd->qnd", hidden, w_down, preferred_element_type=F32).astype(BF16),
        "tensor", scatter_dimension=0, tiled=True,
    ).astype(F32)
    return jnp.swapaxes((residual + mlp_out + b_down).astype(BF16), 0, 1)


def per_device(paired, patches, kept_count, keep_list, *params):
    home = in_hbm(patches[0])
    keep_row = in_hbm(keep_list[0])
    kept_count = in_hbm(kept_count)
    dp_size = lax.axis_size("dp")
    device = lax.axis_index("dp").astype(jnp.int32).reshape(1)
    mates = [(d, d ^ 1) for d in range(dp_size)]
    rightwards = [(d, d + 2) for d in range(dp_size - 2)]
    leftwards = [(d + 2, d) for d in range(dp_size - 2)]

    def to_mate(value):
        return lax.ppermute(value, "dp", mates)

    def to_right(value):
        return lax.ppermute(value, "dp", rightwards)

    def to_left(value):
        return lax.ppermute(value, "dp", leftwards)

    mine, for_mate = pack(device, kept_count, keep_row, home)
    from_mate = to_mate(for_mate)
    table = make_plan(device, kept_count)
    short = table[AT_SHORT : AT_SHORT + 1].astype(F32)
    if paired:
        short = short + lax.ppermute(short, "groups", [(0, 1), (1, 0)])
    else:
        short = lax.pmax(short, "groups")
    short = short[0] > 0

    parts = tuple(zip(STARTS, CHUNKS))
    sends = [(AT_RIGHT + at, size) for at, size in parts] + [(AT_LEFT + at, size) for at, size in parts]
    going = choose(table, sends, [mine, from_mate], "send")
    came_right = [to_right(value) for value in going[: len(parts)]]
    came_left = [to_left(value) for value in going[len(parts) :]]

    def deal_fast(chunk, after):
        right = [came_right[min(part, chunk)] for part in range(len(parts))]
        left = [came_left[min(part, chunk)] for part in range(len(parts))]
        at, size = parts[chunk]
        sources = [mine, from_mate] + right + left
        return choose(table, [(AT_DEALT + at, size)], sources, "deal_%d" % chunk, after)[0]

    def deal_slow(chunk):
        chips = dp_size // 2
        (picked,) = choose(table, [(AT_SLOW_SEND, ROOM * chips)], [mine, from_mate], "deal_slow")
        picked = picked.reshape((chips, ROOM) + picked.shape[1:])
        spread = jnp.repeat(picked, 2, axis=0)
        arrived = lax.all_to_all(spread, "dp", split_axis=0, concat_axis=0, tiled=True)
        at, size = parts[chunk]
        return jnp.stack(
            [
                arrived[table[AT_SLOW_SOURCE + j], table[AT_SLOW_PLACE + j]]
                for j in range(at, at + size)
            ]
        )

    def deal(chunk, after=()):
        return lax.cond(short, lambda: deal_slow(chunk), lambda: deal_fast(chunk, after))

    if paired:
        (pre_gain, pre_shift, w_qkv, b_qkv, w_out, b_out, mlp_gain, mlp_shift, w_up, b_up, w_down,
         b_down) = params
        rows_params = jnp.stack([pre_gain, pre_shift, mlp_gain, mlp_shift, b_out, b_down])
        b_up = b_up.reshape(1, -1)
        w_near = swap(w_out_piece(w_out, [going[0]]))

        def start(own, after):
            other = swap(own)
            mine = attend(own, other, rows_params, w_qkv, b_qkv, after)
            return own, other, mine, swap(mine)

        def finish(state, after):
            keep, send = mlp(*state, rows_params, b_up, weights, after)
            return keep, swap(send)

        state_0 = start(deal(0), [])
        state_1 = start(deal(1), [])
        w_theirs = other_w_out(
            w_out, w_near, [state_0[1], came_right[1], came_left[1]], [state_0[2], state_1[0]]
        )
        weights = (w_out, w_theirs, w_up, w_down)
        done_0 = finish(state_0, [state_1[2]])
        done_1 = finish(state_1, [done_0[0]])
        results, from_right, from_left = [], [], []
        for done, beside in ((done_0, done_1[:1]), (done_1, ())):
            results.append(add(*done, list(beside) + from_right[-1:] + from_left[-1:]))
            from_right.append(to_left(results[-1]))
            from_left.append(to_right(results[-1]))
    else:
        results = [encode_split(deal(chunk), params) for chunk in range(len(parts))]
        from_right = [to_left(value) for value in results]
        from_left = [to_right(value) for value in results]

    back = results + from_right + from_left
    back = back + [to_mate(value) for value in back]

    def home_slow():
        spread = lax.all_gather(jnp.concatenate(results), "dp", axis=0, tiled=True)
        places = table[AT_SLOW_HOME : AT_SLOW_HOME + 2 * PAGE_HALF]
        return (
            jnp.take(spread, places[:PAGE_HALF], axis=0),
            jnp.take(spread, places[PAGE_HALF:], axis=0),
        )

    found = lax.cond(short, home_slow, lambda: (mine, from_mate))
    slow = short.astype(jnp.int32).reshape(1)
    return merge(device, kept_count, keep_row, table, slow, home, back + list(found))[None]


def solution(mesh):
    in_specs = (
        P(("groups", "dp"), "tensor", None, None),
        P("groups"),
        P(("groups", "dp"), None),
        P(),
        P(),
        P(None, None, "tensor"),
        P(None, "tensor"),
        P("tensor", None),
        P(),
        P(),
        P(),
        P(None, "tensor"),
        P("tensor"),
        P("tensor", None),
        P(),
    )
    out_specs = P(("groups", "dp"), "tensor", None, None)
    paired = mesh.shape["tensor"] == 2 and mesh.shape["groups"] == 2
    return jax.shard_map(
        functools.partial(per_device, paired), mesh=mesh, in_specs=in_specs, out_specs=out_specs,
        check_vma=False,
    )
```

```python
import functools

import jax
import jax.numpy as jnp
from jax import lax
from jax.experimental import pallas as pl
from jax.experimental.pallas import tpu as pltpu
from jax.sharding import PartitionSpec as P

HEAD_DIM = 112
CHUNKS = (3, 2)
STARTS = (0, 3)
ROOM = 5
PAGE_HALF = 8
GROUP_ROWS = 16
F32 = jnp.float32
BF16 = jnp.bfloat16
MIB = 1 << 20
SMALL_COST = pl.CostEstimate(flops=1000, bytes_accessed=1000, transcendentals=0)


def norm_rows(inputs, gain, shift):
    average = jnp.mean(inputs, axis=-1, keepdims=True)
    centred = inputs - average
    variance = jnp.mean(centred * centred, axis=-1, keepdims=True)
    return centred * lax.rsqrt(variance + 1e-06) * gain + shift


def pick_at(values, index):
    total = jnp.int32(0)
    for place, value in enumerate(values):
        total = total + jnp.where(index == place, value, 0)
    return total


def page_ends_of(count_ref, pages):
    ends = [jnp.int32(0)]
    for page in range(pages):
        ends.append(ends[-1] + count_ref[page])
    return ends


def chunk_of(slot):
    number, start = jnp.int32(0), jnp.int32(0)
    for chunk in range(1, len(CHUNKS)):
        number = jnp.where(slot >= STARTS[chunk], chunk, number)
        start = jnp.where(slot >= STARTS[chunk], STARTS[chunk], start)
    return number, slot - start


def line_plan(ends, chips, core):
    held = [(ends[2 * chip] + 1 - core) >> 1 for chip in range(chips + 1)]
    total = held[chips]
    wanted = [
        jnp.clip(held[i], jnp.maximum(total - ROOM * (chips - i), 0), jnp.minimum(total, ROOM * i))
        for i in range(chips + 1)
    ]
    below, above = list(wanted), list(wanted)
    for i in range(1, chips + 1):
        below[i] = jnp.minimum(below[i], below[i - 1] + ROOM)
    for i in range(chips - 1, -1, -1):
        above[i] = jnp.maximum(above[i], above[i + 1] - ROOM)
    dealt = [(low + high) >> 1 for low, high in zip(below, above)]
    short = jnp.int32(0)
    for cut in range(1, chips):
        right = held[cut] - dealt[cut]
        most_right = jnp.minimum(held[cut] - held[cut - 1], ROOM)
        most_left = jnp.minimum(held[cut + 1] - held[cut], ROOM)
        short = short + jnp.where((right > most_right) | (-right > most_left), 1, 0)
    return held, dealt, short


AT_PAIR = 0
AT_NEXT = AT_PAIR + ROOM
AT_DEALT = AT_NEXT + ROOM
AT_HOME = AT_DEALT + ROOM
AT_SHORT = AT_HOME + 2 * PAGE_HALF
AT_SLOW_SOURCE = AT_SHORT + 1
AT_SLOW_PLACE = AT_SLOW_SOURCE + ROOM
AT_SLOW_HOME = AT_SLOW_PLACE + ROOM
AT_IN_ORDER = AT_SLOW_HOME + 2 * PAGE_HALF
AT_SLOW_SEND = AT_IN_ORDER + 2 * PAGE_HALF


def plan_kernel(pages, device_ref, count_ref, table_ref):
    chips = pages // 2
    device = device_ref[0]
    core, chip = device & 1, device >> 1
    ends = page_ends_of(count_ref, pages)
    held, dealt, short = line_plan(ends, chips, core)
    held_mate, dealt_mate, short_mate = line_plan(ends, chips, 1 - core)
    table_ref[AT_SHORT] = jnp.where(short + short_mate > 0, 1, 0)
    falls, falls_mate = (
        [jnp.where(ranks[i] - ranks_dealt[i] > 2, 1, 0) for i in range(chips)]
        for ranks, ranks_dealt in ((held, dealt), (held_mate, dealt_mate))
    )

    low, high = pick_at(held, chip), pick_at(held, chip + 1)
    first, end = pick_at(dealt, chip), pick_at(dealt, chip + 1)
    falls_here = pick_at(falls, chip)
    own_start, own_end = pick_at(ends, device), pick_at(ends, device + 1)
    mate_start = pick_at(ends, device ^ 1)

    def turned(offset, falling):
        return jnp.where(falling > 0, ROOM - 1 - offset, offset)

    def local_code(rank):
        position = 2 * rank + core
        own = (position >= own_start) & (position < own_end)
        return jnp.where(own, (position - own_start) >> 1, 16 + ((position - mate_start) >> 1))

    def part_code(count, source):
        number, place = chunk_of(count)
        return (source + number) * 16 + place

    sides = len(CHUNKS)
    odd = chip & 1
    right_side, left_side = sides * odd, sides * (1 - odd)

    for slot in range(ROOM):
        rightwards, leftwards = local_code(high - 1 - slot), local_code(low + slot)
        table_ref[AT_PAIR + slot] = jnp.where(odd > 0, leftwards, rightwards)
        table_ref[AT_NEXT + slot] = jnp.where(odd > 0, rightwards, leftwards)
        offset = turned(jnp.int32(slot), falls_here)
        rank = first + offset
        code = jnp.where(rank < low, part_code(low - 1 - rank, 2 + left_side), local_code(rank))
        code = jnp.where(rank >= high, part_code(rank - high, 2 + right_side), code)
        table_ref[AT_DEALT + slot] = code
        node = jnp.int32(0)
        for place in range(1, chips):
            node = node + jnp.where(held[place] <= rank, 1, 0)
        table_ref[AT_SLOW_SOURCE + slot] = 2 * node + core
        table_ref[AT_SLOW_PLACE + slot] = offset
    for half, (ranks_dealt, turns) in enumerate(((dealt, falls), (dealt_mate, falls_mate))):
        lane = core ^ half
        here, there = pick_at(ranks_dealt, chip), pick_at(ranks_dealt, chip + 1)
        before = pick_at(ranks_dealt, chip - 1)
        turns_here, turns_right, turns_left = (pick_at(turns, chip + i) for i in (0, 1, -1))
        for slot in range(PAGE_HALF):
            rank = (own_start + ((own_start + lane) & 1) + 2 * slot - lane) >> 1
            at = half * PAGE_HALF + slot
            base = 3 * sides * half
            code = part_code(turned(rank - here, turns_here), base)
            right = part_code(turned(rank - there, turns_right), base + sides + right_side)
            left = part_code(turned(rank - before, turns_left), base + sides + left_side)
            code = jnp.where(rank >= there, right, code)
            table_ref[AT_HOME + at] = jnp.where(rank < here, left, code)
            node, start_there, turns_there = jnp.int32(0), jnp.int32(0), turns[0]
            for place in range(1, chips):
                beyond = ranks_dealt[place] <= rank
                node = node + jnp.where(beyond, 1, 0)
                start_there = jnp.where(beyond, ranks_dealt[place], start_there)
                turns_there = jnp.where(beyond, turns[place], turns_there)
            slow = (2 * node + lane) * ROOM + turned(rank - start_there, turns_there)
            table_ref[AT_SLOW_HOME + at] = jnp.clip(slow, 0, pages * ROOM - 1)
            table_ref[AT_IN_ORDER + at] = jnp.int32((6 * sides + half) * 16 + slot)
    for node in range(chips):
        for slot in range(ROOM):
            code = local_code(dealt[node] + slot)
            table_ref[AT_SLOW_SEND + node * ROOM + slot] = jnp.clip(code, 0, 31)


def make_plan(device, kept_count):
    pages = kept_count.shape[0]
    size = AT_SLOW_SEND + ROOM * (pages // 2)
    return pl.pallas_call(
        functools.partial(plan_kernel, pages),
        out_shape=jax.ShapeDtypeStruct((size,), jnp.int32),
        in_specs=[pl.BlockSpec(memory_space=pltpu.SMEM)] * 2,
        out_specs=pl.BlockSpec(memory_space=pltpu.SMEM),
        compiler_params=pltpu.CompilerParams(vmem_limit_bytes=MIB),
        cost_estimate=SMALL_COST,
        name="plan",
    )(device, kept_count)


def kept_blocks(device_ref, count_ref, keep_ref, pages):
    device = device_ref[0]
    start, count = jnp.int32(0), jnp.int32(0)
    for page in range(pages):
        start = start + jnp.where(page < device, count_ref[page], 0)
        count = count + jnp.where(page == device, count_ref[page], 0)
    blocks = []
    for half in range(2):
        offset = (start + device + half) & 1
        for slot in range(PAGE_HALF):
            index = 2 * slot + offset
            block = keep_ref[jnp.minimum(index, 2 * PAGE_HALF - 1)]
            blocks.append(jnp.where(index < count, block, -1))
    return blocks


def kept_blocks_once(device_ref, count_ref, keep_ref, pages, held):
    @pl.when(pl.program_id(0) == 0)
    def _():
        for slot, block in enumerate(kept_blocks(device_ref, count_ref, keep_ref, pages)):
            held[slot] = block

    return [held[slot] for slot in range(2 * PAGE_HALF)]


def pack_kernel(pages, device_ref, count_ref, keep_ref, home_ref, mine_ref, mate_ref, held):
    page_blocks, width = home_ref.shape[1], home_ref.shape[2]
    blocks = kept_blocks_once(device_ref, count_ref, keep_ref, pages, held)
    span = GROUP_ROWS * page_blocks
    row = lax.broadcasted_iota(jnp.int32, (GROUP_ROWS, span), 0)
    column = lax.broadcasted_iota(jnp.int32, (GROUP_ROWS, span), 1)
    chosen = jnp.concatenate(
        [jnp.where(column == row * page_blocks + block, 1.0, 0.0).astype(BF16) for block in blocks],
        axis=0,
    )
    packed = jnp.dot(
        chosen, home_ref[...].reshape(span, width), preferred_element_type=F32
    ).astype(BF16)
    half = PAGE_HALF * GROUP_ROWS
    mine_ref[...] = packed[:half].reshape(PAGE_HALF, GROUP_ROWS, width)
    mate_ref[...] = packed[half:].reshape(PAGE_HALF, GROUP_ROWS, width)


def pack(device, kept_count, keep_row, home):
    rows, page_blocks, width = home.shape
    shape = jax.ShapeDtypeStruct((PAGE_HALF, rows, width), BF16)
    place = pl.BlockSpec((PAGE_HALF, GROUP_ROWS, width), lambda step, *_: (0, step, 0))
    return pl.pallas_call(
        functools.partial(pack_kernel, kept_count.shape[0]),
        out_shape=(shape, shape),
        grid_spec=pltpu.PrefetchScalarGridSpec(
            num_scalar_prefetch=3,
            grid=(rows // GROUP_ROWS,),
            in_specs=[
                pl.BlockSpec((GROUP_ROWS, page_blocks, width), lambda step, *_: (step, 0, 0))
            ],
            out_specs=(place, place),
            scratch_shapes=[pltpu.SMEM((2 * PAGE_HALF,), jnp.int32)],
        ),
        compiler_params=pltpu.CompilerParams(vmem_limit_bytes=16 * MIB),
        name="pack",
    )(device, kept_count, keep_row, home)


def merge_kernel(pages, total, device_ref, count_ref, keep_ref, table_ref, slow_ref, home_ref, *refs):
    sources = refs[:total]
    out_ref, held, landed, sems = refs[total:]
    page_blocks, width = home_ref.shape[1], home_ref.shape[2]
    step = pl.program_id(0)
    slots = 2 * PAGE_HALF

    @pl.when(step == 0)
    def _():
        at = jnp.where(slow_ref[0] > 0, AT_IN_ORDER, AT_HOME)
        start_copies(
            sources,
            [(table_ref[at + slot], landed.at[slot], sems.at[slot]) for slot in range(slots)],
        )

    blocks = kept_blocks_once(device_ref, count_ref, keep_ref, pages, held)
    span = GROUP_ROWS * page_blocks
    depth = slots * GROUP_ROWS
    row = lax.broadcasted_iota(jnp.int32, (span, depth), 0)
    column = lax.broadcasted_iota(jnp.int32, (span, depth), 1)
    slot_id = lax.broadcasted_iota(jnp.int32, (1, depth), 1) // GROUP_ROWS
    block_id = lax.broadcasted_iota(jnp.int32, (span, 1), 0) % page_blocks
    wanted = jnp.full((1, depth), -1, jnp.int32)
    kept = jnp.zeros((span, 1), jnp.int32)
    for place, block in enumerate(blocks):
        wanted = jnp.where(slot_id == place, block, wanted)
        kept = kept + jnp.where(block_id == block, 1, 0)
    chosen = jnp.where(
        (row // page_blocks == column % GROUP_ROWS) & (row % page_blocks == wanted), 1.0, 0.0
    ).astype(BF16)

    @pl.when(step == 0)
    def _():
        for slot in range(slots):
            pltpu.make_async_copy(sources[0].at[0], landed.at[slot], sems.at[slot]).wait()

    rows = pl.ds(pl.multiple_of(step * GROUP_ROWS, GROUP_ROWS), GROUP_ROWS)
    source = landed[:, rows, :].reshape(depth, width)
    result = jnp.dot(chosen, source, preferred_element_type=F32)
    home = home_ref[...].reshape(span, width).astype(F32)
    merged = jnp.where(kept > 0, result, home).astype(BF16)
    out_ref[...] = merged.reshape(GROUP_ROWS, page_blocks, width)


def merge(device, kept_count, keep_row, table, slow, home, sources):
    rows, page_blocks, width = home.shape
    page = pl.BlockSpec((GROUP_ROWS, page_blocks, width), lambda step, *_: (step, 0, 0))
    slots = 2 * PAGE_HALF
    return pl.pallas_call(
        functools.partial(merge_kernel, kept_count.shape[0], len(sources)),
        out_shape=jax.ShapeDtypeStruct(home.shape, BF16),
        grid_spec=pltpu.PrefetchScalarGridSpec(
            num_scalar_prefetch=5,
            grid=(rows // GROUP_ROWS,),
            in_specs=[page] + [pl.BlockSpec(memory_space=pl.ANY)] * len(sources),
            out_specs=page,
            scratch_shapes=[
                pltpu.SMEM((slots,), jnp.int32),
                pltpu.VMEM((slots, rows, width), BF16),
                pltpu.SemaphoreType.DMA((slots,)),
            ],
        ),
        compiler_params=pltpu.CompilerParams(vmem_limit_bytes=20 * MIB),
        cost_estimate=SMALL_COST,
        name="merge",
    )(device, kept_count, keep_row, table, slow, home, *sources)


def start_copies(sources, wanted):
    for code, target, sem in wanted:
        which, place = code >> 4, code & 15
        for index, source in enumerate(sources):
            if len(sources) == 1:
                here = which > -(1 << 20)
            elif index == 0:
                here = which <= 0
            elif index == len(sources) - 1:
                here = which >= index
            else:
                here = which == index

            @pl.when(here)
            def _(source=source, place=place, target=target, sem=sem):
                inside = jnp.minimum(place, source.shape[0] - 1)
                pltpu.make_async_copy(source.at[inside], target, sem).start()


def choose_kernel(parts, n_sources, table_ref, *refs):
    sources, outs, sems = refs[:n_sources], refs[-1 - len(parts) : -1], refs[-1]
    targets = [
        (at + slot, out_ref.at[slot])
        for (at, total), out_ref in zip(parts, outs)
        for slot in range(total)
    ]
    start_copies(
        sources,
        [(table_ref[at], target, sems.at[number]) for number, (at, target) in enumerate(targets)],
    )
    for number, (_, target) in enumerate(targets):
        pltpu.make_async_copy(sources[0].at[0], target, sems.at[number]).wait()


def choose(table, parts, sources, name, after=()):
    block = sources[0].shape[1:]
    total = sum(count for _, count in parts)
    return pl.pallas_call(
        functools.partial(choose_kernel, parts, len(sources)),
        out_shape=tuple(jax.ShapeDtypeStruct((count,) + block, BF16) for _, count in parts),
        in_specs=[pl.BlockSpec(memory_space=pltpu.SMEM)]
        + [pl.BlockSpec(memory_space=pl.ANY)] * (len(sources) + len(after)),
        out_specs=tuple(pl.BlockSpec(memory_space=pltpu.VMEM) for _ in parts),
        scratch_shapes=[pltpu.SemaphoreType.DMA((total,))],
        compiler_params=pltpu.CompilerParams(vmem_limit_bytes=8 * MIB),
        cost_estimate=SMALL_COST,
        name=name,
    )(table, *sources, *after)


def join_kernel(spots_ref, near, side, mate, out_ref, sems):
    piece = near.shape[0]
    sources = (near, side, mate.at[0], mate.at[1])
    copies = []
    for number, source in enumerate(sources):
        place = pl.ds(pl.multiple_of(spots_ref[number] * piece, piece), piece)
        copies.append(pltpu.make_async_copy(source, out_ref.at[place, :], sems.at[number]))
    for copy in copies:
        copy.start()
    for copy in copies:
        copy.wait()


def join(spots, near, side, mate):
    shape = (4 * near.shape[0], near.shape[1])
    any_space = pl.BlockSpec(memory_space=pl.ANY)
    return pl.pallas_call(
        join_kernel,
        out_shape=jax.ShapeDtypeStruct(shape, BF16),
        in_specs=[pl.BlockSpec(memory_space=pltpu.SMEM)] + [any_space] * 3,
        out_specs=pl.BlockSpec(memory_space=pltpu.VMEM),
        scratch_shapes=[pltpu.SemaphoreType.DMA((4,))],
        compiler_params=pltpu.CompilerParams(vmem_limit_bytes=8 * MIB),
        name="join",
    )(spots, near, side, mate)


def in_hbm(array):
    return pltpu.with_memory_space_constraint(array, pltpu.HBM)


def split_store(value, high_ref, low_ref):
    high = value.astype(BF16)
    high_ref[...] = high
    low_ref[...] = (value - high.astype(F32)).astype(BF16)


def attend_kernel(n_after, own_ref, other_ref, rows_ref, b_ref, w_ref, *refs):
    (out_ref, held, normed, q_high, q_low, k_high, k_low, values, scores, sems) = refs[n_after:]
    blocks, rows, width = own_ref.shape
    span = held.shape[2]
    loads = [pltpu.make_async_copy(w_ref.at[j], held.at[j], sems.at[j]) for j in range(3)]
    for load in loads:
        load.start()
    gain, shift = rows_ref[0:1, :], rows_ref[1:2, :]
    for half, ref in enumerate((own_ref, other_ref)):
        for block in range(blocks):
            at = (half * blocks + block) * rows
            normed[at : at + rows] = norm_rows(ref[block].astype(F32), gain, shift).astype(BF16)

    def project(j):
        loads[j].wait()
        product = jnp.dot(normed[...], held[j], preferred_element_type=F32)
        return product + b_ref[j : j + 1, :]

    split_store(project(0) * HEAD_DIM ** (-0.5), q_high, q_low)
    split_store(project(1), k_high, k_low)
    values[...] = project(2).astype(BF16)
    tiles = span // 128
    heads = span // HEAD_DIM
    size = 2 * rows
    lane = lax.broadcasted_iota(jnp.int32, (1, 256), 1)

    def window(head):
        tile = min(head * HEAD_DIM // 128, tiles - 2)
        first = head * HEAD_DIM - tile * 128
        inside = (lane >= first) & (lane < first + HEAD_DIM)
        return tile, slice(tile * 128, tile * 128 + 256), inside

    def one_block(block, carry):
        near = pl.ds(pl.multiple_of(block * rows, rows), rows)
        far = pl.ds(pl.multiple_of((blocks + block) * rows, rows), rows)

        def both(ref, columns):
            return jnp.concatenate([ref[near, columns], ref[far, columns]], axis=0)

        def times(left, right):
            return lax.dot_general(
                left, right, (((1,), (1,)), ((), ())), preferred_element_type=F32
            )

        for head in range(heads):
            _, columns, inside = window(head)
            none = jnp.zeros((), BF16)
            qh = jnp.where(inside, both(q_high, columns), none)
            ql = jnp.where(inside, both(q_low, columns), none)
            kh, kl = both(k_high, columns), both(k_low, columns)
            scores[head * size : (head + 1) * size, :] = (
                times(qh, kh) + times(qh, kl) + times(ql, kh)
            )
        value = scores[...]
        value = jnp.exp(value - jnp.max(value, axis=-1, keepdims=True))
        weights = (value * (1.0 / jnp.sum(value, axis=-1, keepdims=True))).astype(BF16)
        sums = [None] * tiles
        for head in range(heads):
            tile, columns, inside = window(head)
            mixed = jnp.dot(
                weights[head * size : (head + 1) * size, :], both(values, columns),
                preferred_element_type=F32,
            )
            mixed = jnp.where(inside, mixed, 0.0)
            for part in range(2):
                piece = mixed[:, part * 128 : part * 128 + 128]
                old = sums[tile + part]
                sums[tile + part] = piece if old is None else old + piece
        result = jnp.concatenate(sums, axis=1).astype(BF16)
        out_ref[0, block] = result[:rows]
        out_ref[1, block] = result[rows:]
        return carry

    lax.fori_loop(0, blocks, one_block, 0)


def attend(own, other, rows_params, w_qkv, b_qkv, after=()):
    blocks, rows, width = own.shape
    span = w_qkv.shape[2]
    total = 2 * blocks * rows
    vmem = pl.BlockSpec(memory_space=pltpu.VMEM)
    return pl.pallas_call(
        functools.partial(attend_kernel, len(after)),
        out_shape=jax.ShapeDtypeStruct((2, blocks, rows, span), BF16),
        in_specs=[vmem] * 4 + [pl.BlockSpec(memory_space=pl.ANY)] * (1 + len(after)),
        out_specs=vmem,
        scratch_shapes=[pltpu.VMEM((3, width, span), BF16), pltpu.VMEM((total, width), BF16)]
        + [pltpu.VMEM((total, span), BF16)] * 5
        + [
            pltpu.VMEM((2 * rows * (span // HEAD_DIM), 2 * rows), F32),
            pltpu.SemaphoreType.DMA((3,)),
        ],
        compiler_params=pltpu.CompilerParams(vmem_limit_bytes=28 * MIB),
        cost_estimate=pl.CostEstimate(
            flops=24 * total * width * span, bytes_accessed=6 * width * span, transcendentals=0
        ),
        name="attend",
    )(own, other, rows_params, b_qkv, in_hbm(w_qkv), *after)


UP_TILE = 512
DOWN_TILE = 256
SLOTS = 5


def mlp_kernel(n_after, own_ref, other_ref, mine_ref, theirs_ref, rows_ref, b_up_ref, w_mine, w_theirs,
               w_up, w_down, *refs):
    (keep_ref, send_ref, residual, renormed, hidden, outs, ups, downs, out_sems, up_sems,
     down_sems) = refs[n_after:]
    blocks, rows, width = own_ref.shape
    half = blocks * rows
    span = outs.shape[1]
    up_steps, down_steps = w_up.shape[1] // UP_TILE, width // DOWN_TILE

    def load_up(step):
        columns = pl.ds(pl.multiple_of(step * UP_TILE, UP_TILE), UP_TILE)
        slot = lax.rem(step, SLOTS)
        return pltpu.make_async_copy(w_up.at[:, columns], ups.at[slot], up_sems.at[slot])

    def load_down(step):
        columns = pl.ds(pl.multiple_of(step * DOWN_TILE, DOWN_TILE), DOWN_TILE)
        slot = lax.rem(step, SLOTS)
        return pltpu.make_async_copy(w_down.at[:, columns], downs.at[slot], down_sems.at[slot])

    out_loads = [
        pltpu.make_async_copy(source, outs.at[number], out_sems.at[number])
        for number, source in enumerate((w_mine, w_theirs))
    ]
    for load in out_loads:
        load.start()
    for slot in range(SLOTS):
        load_up(jnp.int32(slot)).start()
    gain, shift = rows_ref[2:3, :], rows_ref[3:4, :]
    mine = mine_ref[...].reshape(2 * half, span)
    theirs = jnp.concatenate(
        [theirs_ref[1].reshape(half, span), theirs_ref[0].reshape(half, span)], axis=0
    )
    for number, attended in enumerate((mine, theirs)):
        out_loads[number].wait()
        for column in range(0, width, DOWN_TILE):
            columns = slice(column, column + DOWN_TILE)
            part = jnp.dot(attended, outs[number, :, columns], preferred_element_type=F32)
            part = part.astype(BF16).astype(F32)
            if number == 0:
                residual[:, columns] = part + rows_ref[4:5, columns]
            else:
                residual[:, columns] += part
    for side, ref in enumerate((own_ref, other_ref)):
        for block in range(blocks):
            at = slice((side * blocks + block) * rows, (side * blocks + block + 1) * rows)
            value = ref[block].astype(F32) + residual[at]
            if side == 0:
                residual[at] = value
            renormed[at] = norm_rows(value, gain, shift).astype(BF16)

    def one_up(step, carry):
        load_up(step).wait()
        slot = lax.rem(step, SLOTS)
        for part in range(0, UP_TILE, 256):
            columns = pl.ds(pl.multiple_of(step * UP_TILE + part, 256), 256)
            raised = jnp.dot(
                renormed[...], ups[slot, :, part : part + 256], preferred_element_type=F32
            )
            raised = raised + b_up_ref[0:1, columns]
            hidden[:, columns] = jax.nn.gelu(raised, approximate=True).astype(BF16)
        ahead = step + SLOTS

        @pl.when(ahead < up_steps)
        def _():
            load_up(ahead).start()

        @pl.when((ahead >= up_steps) & (ahead < up_steps + down_steps))
        def _():
            load_down(ahead - up_steps).start()

        return carry

    lax.fori_loop(0, up_steps, one_up, 0)

    def one_down(step, carry):
        load_down(step).wait()
        columns = pl.ds(pl.multiple_of(step * DOWN_TILE, DOWN_TILE), DOWN_TILE)
        lowered = jnp.dot(
            hidden[...], downs[lax.rem(step, SLOTS)], preferred_element_type=F32
        )
        kept = residual[:half, columns] + lowered[:half] + rows_ref[5:6, columns]
        keep_ref[:, :, columns] = kept.reshape(blocks, rows, DOWN_TILE)
        send_ref[:, :, columns] = lowered[half:].astype(BF16).reshape(blocks, rows, DOWN_TILE)

        @pl.when(step + SLOTS < down_steps)
        def _():
            load_down(step + SLOTS).start()

        return carry

    lax.fori_loop(0, down_steps, one_down, 0)


def mlp(own, other, mine, theirs, rows_params, b_up, weights, after):
    blocks, rows, width = own.shape
    span = mine.shape[3]
    total = 2 * blocks * rows
    vmem = pl.BlockSpec(memory_space=pltpu.VMEM)
    hbm = pl.BlockSpec(memory_space=pl.ANY)
    w_mine, w_theirs, w_up, w_down = weights
    hidden = w_up.shape[1]
    return pl.pallas_call(
        functools.partial(mlp_kernel, len(after)),
        out_shape=(
            jax.ShapeDtypeStruct((blocks, rows, width), F32),
            jax.ShapeDtypeStruct((blocks, rows, width), BF16),
        ),
        in_specs=[vmem] * 6 + [hbm] * (4 + len(after)),
        out_specs=(vmem, vmem),
        scratch_shapes=[
            pltpu.VMEM((total, width), F32),
            pltpu.VMEM((total, width), BF16),
            pltpu.VMEM((total, hidden), BF16),
            pltpu.VMEM((2, span, width), BF16),
            pltpu.VMEM((SLOTS, width, UP_TILE), BF16),
            pltpu.VMEM((SLOTS, hidden, DOWN_TILE), BF16),
            pltpu.SemaphoreType.DMA((2,)),
            pltpu.SemaphoreType.DMA((SLOTS,)),
            pltpu.SemaphoreType.DMA((SLOTS,)),
        ],
        compiler_params=pltpu.CompilerParams(vmem_limit_bytes=46 * MIB),
        cost_estimate=pl.CostEstimate(
            flops=8 * total * width * (span + hidden),
            bytes_accessed=4 * width * (span + hidden),
            transcendentals=0,
        ),
        name="mlp",
    )(
        own, other, mine, theirs, rows_params, b_up, in_hbm(w_mine), w_theirs, in_hbm(w_up),
        in_hbm(w_down), *after,
    )


def add_kernel(n_after, keep_ref, came_ref, *refs):
    out_ref = refs[n_after]
    out_ref[...] = (keep_ref[...] + came_ref[...].astype(F32)).astype(BF16)


def add(keep, came, after):
    vmem = pl.BlockSpec(memory_space=pltpu.VMEM)
    return pl.pallas_call(
        functools.partial(add_kernel, len(after)),
        out_shape=jax.ShapeDtypeStruct(came.shape, BF16),
        in_specs=[vmem] * 2 + [pl.BlockSpec(memory_space=pl.ANY)] * len(after),
        out_specs=vmem,
        compiler_params=pltpu.CompilerParams(vmem_limit_bytes=8 * MIB),
        cost_estimate=SMALL_COST,
        name="add",
    )(keep, came, *after)


def swap(value):
    return lax.ppermute(value, "tensor", [(0, 1), (1, 0)])


def line_up_kernel(total, n_after, *refs):
    sources, out_ref, sems = refs[:total], refs[total + n_after], refs[-1]
    copies = [
        pltpu.make_async_copy(source, out_ref.at[number], sems.at[number])
        for number, source in enumerate(sources)
    ]
    for copy in copies:
        copy.start()
    for copy in copies:
        copy.wait()


def line_up(arrays, after, name):
    any_space = pl.BlockSpec(memory_space=pl.ANY)
    total = len(arrays)
    return pl.pallas_call(
        functools.partial(line_up_kernel, total, len(after)),
        out_shape=jax.ShapeDtypeStruct((total,) + arrays[0].shape, arrays[0].dtype),
        in_specs=[any_space] * (total + len(after)),
        out_specs=pl.BlockSpec(memory_space=pltpu.VMEM),
        scratch_shapes=[pltpu.SemaphoreType.DMA((total,))],
        compiler_params=pltpu.CompilerParams(vmem_limit_bytes=8 * MIB),
        cost_estimate=SMALL_COST,
        name=name,
    )(*arrays, *after)


def w_out_place(w_out):
    core = lax.axis_index("dp") & 1
    group = lax.axis_index("groups")
    return 2 * group + core, 2 * (1 - group) + core, w_out.shape[0] // 4


def piece_kernel(n_after, number_ref, w_ref, *refs):
    out_ref, sem = refs[n_after:]
    piece = out_ref.shape[0]
    rows = pl.ds(pl.multiple_of(number_ref[0] * piece, piece), piece)
    copy = pltpu.make_async_copy(w_ref.at[rows, :], out_ref, sem)
    copy.start()
    copy.wait()


def w_out_piece(w_out, after):
    number, _, piece = w_out_place(w_out)
    any_space = pl.BlockSpec(memory_space=pl.ANY)
    return pl.pallas_call(
        functools.partial(piece_kernel, len(after)),
        out_shape=jax.ShapeDtypeStruct((piece, w_out.shape[1]), BF16),
        in_specs=[pl.BlockSpec(memory_space=pltpu.SMEM)] + [any_space] * (1 + len(after)),
        out_specs=pl.BlockSpec(memory_space=pltpu.VMEM),
        scratch_shapes=[pltpu.SemaphoreType.DMA],
        compiler_params=pltpu.CompilerParams(vmem_limit_bytes=4 * MIB),
        cost_estimate=SMALL_COST,
        name="w_piece",
    )(number.astype(jnp.int32).reshape(1), in_hbm(w_out), *after)


def other_w_out(w_out, near, early, late):
    number, other, _ = w_out_place(w_out)
    dp_size = lax.axis_size("dp")
    sent = line_up([near], early, "w_near")
    side = lax.ppermute(sent, "groups", [(0, 1), (1, 0)])[0]
    both = line_up([near, side], late, "w_both")
    mate = lax.ppermute(both, "dp", [(d, d ^ 1) for d in range(dp_size)])
    spots = jnp.stack([number, other, number ^ 1, other ^ 1]).astype(jnp.int32)
    return join(spots, near, side, mate)


def attend_rows(projected):
    row_total, count_blocks, width = (projected.shape[0], projected.shape[1], projected.shape[3])
    head_count = width // HEAD_DIM
    queries = projected[:, :, 0].reshape(row_total, count_blocks, head_count, HEAD_DIM)
    key_rows = projected[:, :, 1].reshape(row_total, count_blocks, head_count, HEAD_DIM)
    values = projected[:, :, 2].astype(BF16).reshape(row_total, count_blocks, head_count, HEAD_DIM)
    scores = jnp.einsum(
        "qnhd,snhd->nhqs", queries, key_rows, precision=lax.Precision.HIGHEST
    ) * HEAD_DIM ** (-0.5)
    weights = jax.nn.softmax(scores, axis=-1).astype(BF16)
    attended = jnp.einsum("nhqs,snhd->qnhd", weights, values, preferred_element_type=F32)
    return attended.astype(BF16).reshape(row_total, count_blocks, width)


def encode_split(own, params):
    (pre_gain, pre_shift, w_qkv, b_qkv, w_out, b_out, mlp_gain, mlp_shift, w_up, b_up, w_down,
     b_down) = params
    block_rows = jnp.swapaxes(own, 0, 1)
    rows_dev = block_rows.shape[0]
    gathered = lax.all_gather(block_rows, "tensor", axis=0, tiled=True)
    normed = norm_rows(gathered.astype(F32), pre_gain, pre_shift).astype(BF16)
    attended = attend_rows(
        jnp.einsum("qnd,jde->qnje", normed, w_qkv, preferred_element_type=F32) + b_qkv[None, None]
    )
    partial_value = jnp.einsum("qne,ed->qnd", attended, w_out, preferred_element_type=F32)
    summed = lax.psum(partial_value.astype(BF16), "tensor").astype(F32)
    residual_all = gathered.astype(F32) + summed + b_out
    renormed = norm_rows(residual_all, mlp_gain, mlp_shift).astype(BF16)
    raised = jnp.einsum("qnd,df->qnf", renormed, w_up, preferred_element_type=F32) + b_up
    hidden = jax.nn.gelu(raised, approximate=True).astype(BF16)
    residual = lax.dynamic_slice_in_dim(
        residual_all, lax.axis_index("tensor") * rows_dev, rows_dev, 0
    )
    mlp_out = lax.psum_scatter(
        jnp.einsum("qnf,fd->qnd", hidden, w_down, preferred_element_type=F32).astype(BF16),
        "tensor", scatter_dimension=0, tiled=True,
    ).astype(F32)
    return jnp.swapaxes((residual + mlp_out + b_down).astype(BF16), 0, 1)


def per_device(paired, patches, kept_count, keep_list, *params):
    home = in_hbm(patches[0])
    keep_row = in_hbm(keep_list[0])
    kept_count = in_hbm(kept_count)
    dp_size = lax.axis_size("dp")
    device = lax.axis_index("dp").astype(jnp.int32).reshape(1)
    mates = [(d, d ^ 1) for d in range(dp_size)]
    pairs = [(d, d ^ 2) for d in range(dp_size)]
    nexts = [(d, min(max(((d + 2) ^ 2) - 2, d & 1), dp_size - 2 + (d & 1))) for d in range(dp_size)]

    def to_mate(value):
        return lax.ppermute(value, "dp", mates)

    def to_pair(value):
        return lax.ppermute(value, "dp", pairs)

    def to_next(value):
        return lax.ppermute(value, "dp", nexts)

    mine, for_mate = pack(device, kept_count, keep_row, home)
    from_mate = to_mate(for_mate)
    table = make_plan(device, kept_count)
    short = table[AT_SHORT : AT_SHORT + 1].astype(F32)
    if paired:
        short = short + lax.ppermute(short, "groups", [(0, 1), (1, 0)])
    else:
        short = lax.pmax(short, "groups")
    short = short[0] > 0

    parts = tuple(zip(STARTS, CHUNKS))
    sends = [(AT_PAIR + at, size) for at, size in parts] + [(AT_NEXT + at, size) for at, size in parts]
    going = choose(table, sends, [mine, from_mate], "send")
    came_pair = [to_pair(value) for value in going[: len(parts)]]
    came_next = [to_next(value) for value in going[len(parts) :]]

    def deal_fast(chunk, after):
        came = [came_pair[min(part, chunk)] for part in range(len(parts))]
        came = came + [came_next[min(part, chunk)] for part in range(len(parts))]
        at, size = parts[chunk]
        sources = [mine, from_mate] + came
        return choose(table, [(AT_DEALT + at, size)], sources, "deal_%d" % chunk, after)[0]

    def deal_slow(chunk):
        chips = dp_size // 2
        (picked,) = choose(table, [(AT_SLOW_SEND, ROOM * chips)], [mine, from_mate], "deal_slow")
        picked = picked.reshape((chips, ROOM) + picked.shape[1:])
        spread = jnp.repeat(picked, 2, axis=0)
        arrived = lax.all_to_all(spread, "dp", split_axis=0, concat_axis=0, tiled=True)
        at, size = parts[chunk]
        return jnp.stack(
            [
                arrived[table[AT_SLOW_SOURCE + j], table[AT_SLOW_PLACE + j]]
                for j in range(at, at + size)
            ]
        )

    def deal(chunk, after=()):
        return lax.cond(short, lambda: deal_slow(chunk), lambda: deal_fast(chunk, after))

    if paired:
        (pre_gain, pre_shift, w_qkv, b_qkv, w_out, b_out, mlp_gain, mlp_shift, w_up, b_up, w_down,
         b_down) = params
        rows_params = jnp.stack([pre_gain, pre_shift, mlp_gain, mlp_shift, b_out, b_down])
        b_up = b_up.reshape(1, -1)
        w_near = swap(w_out_piece(w_out, [going[0]]))

        def start(own, after):
            other = swap(own)
            mine = attend(own, other, rows_params, w_qkv, b_qkv, after)
            return own, other, mine, swap(mine)

        def finish(state, after):
            keep, send = mlp(*state, rows_params, b_up, weights, after)
            return keep, swap(send)

        state_0 = start(deal(0), [])
        state_1 = start(deal(1), [])
        w_theirs = other_w_out(
            w_out, w_near, [state_0[0]], [state_0[2], state_1[0]]
        )
        weights = (w_out, w_theirs, w_up, w_down)
        done_0 = finish(state_0, [state_1[2]])
        done_1 = finish(state_1, [done_0[0]])
        results, from_pair, from_next = [], [], []
        for done, beside in ((done_0, done_1[:1]), (done_1, ())):
            results.append(add(*done, list(beside) + from_pair[-1:] + from_next[-1:]))
            from_pair.append(to_pair(results[-1]))
            from_next.append(to_next(results[-1]))
    else:
        results = [encode_split(deal(chunk), params) for chunk in range(len(parts))]
        from_pair = [to_pair(value) for value in results]
        from_next = [to_next(value) for value in results]

    back = results + from_pair + from_next
    back = back + [to_mate(value) for value in back]

    def home_slow():
        spread = lax.all_gather(jnp.concatenate(results), "dp", axis=0, tiled=True)
        places = table[AT_SLOW_HOME : AT_SLOW_HOME + 2 * PAGE_HALF]
        return (
            jnp.take(spread, places[:PAGE_HALF], axis=0),
            jnp.take(spread, places[PAGE_HALF:], axis=0),
        )

    found = lax.cond(short, home_slow, lambda: (mine, from_mate))
    slow = short.astype(jnp.int32).reshape(1)
    return merge(device, kept_count, keep_row, table, slow, home, back + list(found))[None]


def solution(mesh):
    in_specs = (
        P(("groups", "dp"), "tensor", None, None),
        P("groups"),
        P(("groups", "dp"), None),
        P(),
        P(),
        P(None, None, "tensor"),
        P(None, "tensor"),
        P("tensor", None),
        P(),
        P(),
        P(),
        P(None, "tensor"),
        P("tensor"),
        P("tensor", None),
        P(),
    )
    out_specs = P(("groups", "dp"), "tensor", None, None)
    paired = mesh.shape["tensor"] == 2 and mesh.shape["groups"] == 2
    return jax.shard_map(
        functools.partial(per_device, paired), mesh=mesh, in_specs=in_specs, out_specs=out_specs,
        check_vma=False,
    )
```

```python
import functools

import jax
import jax.numpy as jnp
from jax import lax
from jax.experimental import pallas as pl
from jax.experimental.pallas import tpu as pltpu
from jax.sharding import PartitionSpec as P

HEAD_DIM = 112
CHUNKS = (3, 2)
STARTS = (0, 3)
ROOM = 5
PAGE_HALF = 8
GROUP_ROWS = 16
F32 = jnp.float32
BF16 = jnp.bfloat16
MIB = 1 << 20
SMALL_COST = pl.CostEstimate(flops=1000, bytes_accessed=1000, transcendentals=0)


def norm_rows(inputs, gain, shift):
    average = jnp.mean(inputs, axis=-1, keepdims=True)
    centred = inputs - average
    variance = jnp.mean(centred * centred, axis=-1, keepdims=True)
    return centred * lax.rsqrt(variance + 1e-06) * gain + shift


def pick_at(values, index):
    total = jnp.int32(0)
    for place, value in enumerate(values):
        total = total + jnp.where(index == place, value, 0)
    return total


def page_ends_of(count_ref, pages):
    ends = [jnp.int32(0)]
    for page in range(pages):
        ends.append(ends[-1] + count_ref[page])
    return ends


def chunk_of(slot):
    number, start = jnp.int32(0), jnp.int32(0)
    for chunk in range(1, len(CHUNKS)):
        number = jnp.where(slot >= STARTS[chunk], chunk, number)
        start = jnp.where(slot >= STARTS[chunk], STARTS[chunk], start)
    return number, slot - start


def line_plan(ends, chips, core):
    held = [(ends[2 * chip] + 1 - core) >> 1 for chip in range(chips + 1)]
    total = held[chips]
    wanted = [
        jnp.clip(held[i], jnp.maximum(total - ROOM * (chips - i), 0), jnp.minimum(total, ROOM * i))
        for i in range(chips + 1)
    ]
    below, above = list(wanted), list(wanted)
    for i in range(1, chips + 1):
        below[i] = jnp.minimum(below[i], below[i - 1] + ROOM)
    for i in range(chips - 1, -1, -1):
        above[i] = jnp.maximum(above[i], above[i + 1] - ROOM)
    dealt = [(low + high) >> 1 for low, high in zip(below, above)]
    short = jnp.int32(0)
    for cut in range(1, chips):
        right = held[cut] - dealt[cut]
        most_right = jnp.minimum(held[cut] - held[cut - 1], ROOM)
        most_left = jnp.minimum(held[cut + 1] - held[cut], ROOM)
        short = short + jnp.where((right > most_right) | (-right > most_left), 1, 0)
    return held, dealt, short


AT_PAIR = 0
AT_NEXT = AT_PAIR + ROOM
AT_DEALT = AT_NEXT + ROOM
AT_HOME = AT_DEALT + ROOM
AT_SHORT = AT_HOME + 2 * PAGE_HALF
AT_SLOW_SOURCE = AT_SHORT + 1
AT_SLOW_PLACE = AT_SLOW_SOURCE + ROOM
AT_SLOW_HOME = AT_SLOW_PLACE + ROOM
AT_IN_ORDER = AT_SLOW_HOME + 2 * PAGE_HALF
AT_SLOW_SEND = AT_IN_ORDER + 2 * PAGE_HALF


def plan_kernel(pages, device_ref, count_ref, table_ref):
    chips = pages // 2
    device = device_ref[0]
    core, chip = device & 1, device >> 1
    ends = page_ends_of(count_ref, pages)
    held, dealt, short = line_plan(ends, chips, core)
    held_mate, dealt_mate, short_mate = line_plan(ends, chips, 1 - core)
    table_ref[AT_SHORT] = jnp.where(short + short_mate > 0, 1, 0)
    falls, falls_mate = (
        [jnp.where(ranks[i] - ranks_dealt[i] > 2, 1, 0) for i in range(chips)]
        for ranks, ranks_dealt in ((held, dealt), (held_mate, dealt_mate))
    )

    low, high = pick_at(held, chip), pick_at(held, chip + 1)
    first, end = pick_at(dealt, chip), pick_at(dealt, chip + 1)
    falls_here = pick_at(falls, chip)
    own_start, own_end = pick_at(ends, device), pick_at(ends, device + 1)
    mate_start = pick_at(ends, device ^ 1)

    def turned(offset, falling):
        return jnp.where(falling > 0, ROOM - 1 - offset, offset)

    def local_code(rank):
        position = 2 * rank + core
        own = (position >= own_start) & (position < own_end)
        return jnp.where(own, (position - own_start) >> 1, 16 + ((position - mate_start) >> 1))

    def part_code(count, source):
        number, place = chunk_of(count)
        return (source + number) * 16 + place

    sides = len(CHUNKS)
    odd = chip & 1
    right_side, left_side = sides * odd, sides * (1 - odd)

    for slot in range(ROOM):
        rightwards, leftwards = local_code(high - 1 - slot), local_code(low + slot)
        table_ref[AT_PAIR + slot] = jnp.where(odd > 0, leftwards, rightwards)
        table_ref[AT_NEXT + slot] = jnp.where(odd > 0, rightwards, leftwards)
        offset = turned(jnp.int32(slot), falls_here)
        rank = first + offset
        code = jnp.where(rank < low, part_code(low - 1 - rank, 2 + left_side), local_code(rank))
        code = jnp.where(rank >= high, part_code(rank - high, 2 + right_side), code)
        table_ref[AT_DEALT + slot] = code
        node = jnp.int32(0)
        for place in range(1, chips):
            node = node + jnp.where(held[place] <= rank, 1, 0)
        table_ref[AT_SLOW_SOURCE + slot] = 2 * node + core
        table_ref[AT_SLOW_PLACE + slot] = offset
    for half, (ranks_dealt, turns) in enumerate(((dealt, falls), (dealt_mate, falls_mate))):
        lane = core ^ half
        here, there = pick_at(ranks_dealt, chip), pick_at(ranks_dealt, chip + 1)
        before = pick_at(ranks_dealt, chip - 1)
        turns_here, turns_right, turns_left = (pick_at(turns, chip + i) for i in (0, 1, -1))
        for slot in range(PAGE_HALF):
            rank = (own_start + ((own_start + lane) & 1) + 2 * slot - lane) >> 1
            at = half * PAGE_HALF + slot
            base = 3 * sides * half
            code = part_code(turned(rank - here, turns_here), base)
            right = part_code(turned(rank - there, turns_right), base + sides + right_side)
            left = part_code(turned(rank - before, turns_left), base + sides + left_side)
            code = jnp.where(rank >= there, right, code)
            table_ref[AT_HOME + at] = jnp.where(rank < here, left, code)
            node, start_there, turns_there = jnp.int32(0), jnp.int32(0), turns[0]
            for place in range(1, chips):
                beyond = ranks_dealt[place] <= rank
                node = node + jnp.where(beyond, 1, 0)
                start_there = jnp.where(beyond, ranks_dealt[place], start_there)
                turns_there = jnp.where(beyond, turns[place], turns_there)
            slow = (2 * node + lane) * ROOM + turned(rank - start_there, turns_there)
            table_ref[AT_SLOW_HOME + at] = jnp.clip(slow, 0, pages * ROOM - 1)
            table_ref[AT_IN_ORDER + at] = jnp.int32((6 * sides + half) * 16 + slot)
    for node in range(chips):
        for slot in range(ROOM):
            code = local_code(dealt[node] + slot)
            table_ref[AT_SLOW_SEND + node * ROOM + slot] = jnp.clip(code, 0, 31)


def make_plan(device, kept_count):
    pages = kept_count.shape[0]
    size = AT_SLOW_SEND + ROOM * (pages // 2)
    return pl.pallas_call(
        functools.partial(plan_kernel, pages),
        out_shape=jax.ShapeDtypeStruct((size,), jnp.int32),
        in_specs=[pl.BlockSpec(memory_space=pltpu.SMEM)] * 2,
        out_specs=pl.BlockSpec(memory_space=pltpu.SMEM),
        compiler_params=pltpu.CompilerParams(vmem_limit_bytes=MIB),
        cost_estimate=SMALL_COST,
        name="plan",
    )(device, kept_count)


def kept_blocks(device_ref, count_ref, keep_ref, pages):
    device = device_ref[0]
    start, count = jnp.int32(0), jnp.int32(0)
    for page in range(pages):
        start = start + jnp.where(page < device, count_ref[page], 0)
        count = count + jnp.where(page == device, count_ref[page], 0)
    blocks = []
    for half in range(2):
        offset = (start + device + half) & 1
        for slot in range(PAGE_HALF):
            index = 2 * slot + offset
            block = keep_ref[jnp.minimum(index, 2 * PAGE_HALF - 1)]
            blocks.append(jnp.where(index < count, block, -1))
    return blocks


def kept_blocks_once(device_ref, count_ref, keep_ref, pages, held):
    @pl.when(pl.program_id(0) == 0)
    def _():
        for slot, block in enumerate(kept_blocks(device_ref, count_ref, keep_ref, pages)):
            held[slot] = block

    return [held[slot] for slot in range(2 * PAGE_HALF)]


def pack_kernel(pages, device_ref, count_ref, keep_ref, home_ref, mine_ref, mate_ref, held):
    page_blocks, width = home_ref.shape[1], home_ref.shape[2]
    blocks = kept_blocks_once(device_ref, count_ref, keep_ref, pages, held)
    span = GROUP_ROWS * page_blocks
    row = lax.broadcasted_iota(jnp.int32, (GROUP_ROWS, span), 0)
    column = lax.broadcasted_iota(jnp.int32, (GROUP_ROWS, span), 1)
    chosen = jnp.concatenate(
        [jnp.where(column == row * page_blocks + block, 1.0, 0.0).astype(BF16) for block in blocks],
        axis=0,
    )
    packed = jnp.dot(
        chosen, home_ref[...].reshape(span, width), preferred_element_type=F32
    ).astype(BF16)
    half = PAGE_HALF * GROUP_ROWS
    mine_ref[...] = packed[:half].reshape(PAGE_HALF, GROUP_ROWS, width)
    mate_ref[...] = packed[half:].reshape(PAGE_HALF, GROUP_ROWS, width)


def pack(device, kept_count, keep_row, home):
    rows, page_blocks, width = home.shape
    shape = jax.ShapeDtypeStruct((PAGE_HALF, rows, width), BF16)
    place = pl.BlockSpec((PAGE_HALF, GROUP_ROWS, width), lambda step, *_: (0, step, 0))
    return pl.pallas_call(
        functools.partial(pack_kernel, kept_count.shape[0]),
        out_shape=(shape, shape),
        grid_spec=pltpu.PrefetchScalarGridSpec(
            num_scalar_prefetch=3,
            grid=(rows // GROUP_ROWS,),
            in_specs=[
                pl.BlockSpec((GROUP_ROWS, page_blocks, width), lambda step, *_: (step, 0, 0))
            ],
            out_specs=(place, place),
            scratch_shapes=[pltpu.SMEM((2 * PAGE_HALF,), jnp.int32)],
        ),
        compiler_params=pltpu.CompilerParams(vmem_limit_bytes=16 * MIB),
        name="pack",
    )(device, kept_count, keep_row, home)


def merge_kernel(pages, total, device_ref, count_ref, keep_ref, table_ref, slow_ref, home_ref, *refs):
    sources = refs[:total]
    out_ref, held, landed, sems = refs[total:]
    page_blocks, width = home_ref.shape[1], home_ref.shape[2]
    step = pl.program_id(0)
    slots = 2 * PAGE_HALF

    @pl.when(step == 0)
    def _():
        at = jnp.where(slow_ref[0] > 0, AT_IN_ORDER, AT_HOME)
        start_copies(
            sources,
            [(table_ref[at + slot], landed.at[slot], sems.at[slot]) for slot in range(slots)],
            landed.shape[1] // GROUP_ROWS,
        )

    blocks = kept_blocks_once(device_ref, count_ref, keep_ref, pages, held)
    span = GROUP_ROWS * page_blocks
    depth = slots * GROUP_ROWS
    row = lax.broadcasted_iota(jnp.int32, (span, depth), 0)
    column = lax.broadcasted_iota(jnp.int32, (span, depth), 1)
    slot_id = lax.broadcasted_iota(jnp.int32, (1, depth), 1) // GROUP_ROWS
    block_id = lax.broadcasted_iota(jnp.int32, (span, 1), 0) % page_blocks
    wanted = jnp.full((1, depth), -1, jnp.int32)
    kept = jnp.zeros((span, 1), jnp.int32)
    for place, block in enumerate(blocks):
        wanted = jnp.where(slot_id == place, block, wanted)
        kept = kept + jnp.where(block_id == block, 1, 0)
    chosen = jnp.where(
        (row // page_blocks == column % GROUP_ROWS) & (row % page_blocks == wanted), 1.0, 0.0
    ).astype(BF16)

    same = lax.broadcasted_iota(jnp.int32, (span, span), 0) == lax.broadcasted_iota(
        jnp.int32, (span, span), 1
    )
    stays = jnp.where(same & (kept == 0), 1.0, 0.0).astype(BF16)
    rows = pl.ds(pl.multiple_of(step * GROUP_ROWS, GROUP_ROWS), GROUP_ROWS)
    for slot in range(slots):
        pltpu.make_async_copy(
            sources[0].at[0, rows, :], landed.at[slot, rows, :], sems.at[slot, step]
        ).wait()
    source = landed[:, rows, :].reshape(depth, width)
    result = jnp.dot(chosen, source, preferred_element_type=F32)
    result += jnp.dot(stays, home_ref[...].reshape(span, width), preferred_element_type=F32)
    out_ref[...] = result.astype(BF16).reshape(GROUP_ROWS, page_blocks, width)


def merge(device, kept_count, keep_row, table, slow, home, sources):
    rows, page_blocks, width = home.shape
    page = pl.BlockSpec((GROUP_ROWS, page_blocks, width), lambda step, *_: (step, 0, 0))
    slots = 2 * PAGE_HALF
    return pl.pallas_call(
        functools.partial(merge_kernel, kept_count.shape[0], len(sources)),
        out_shape=jax.ShapeDtypeStruct(home.shape, BF16),
        grid_spec=pltpu.PrefetchScalarGridSpec(
            num_scalar_prefetch=5,
            grid=(rows // GROUP_ROWS,),
            in_specs=[page] + [pl.BlockSpec(memory_space=pl.ANY)] * len(sources),
            out_specs=page,
            scratch_shapes=[
                pltpu.SMEM((slots,), jnp.int32),
                pltpu.VMEM((slots, rows, width), BF16),
                pltpu.SemaphoreType.DMA((slots, rows // GROUP_ROWS)),
            ],
        ),
        compiler_params=pltpu.CompilerParams(vmem_limit_bytes=20 * MIB),
        cost_estimate=SMALL_COST,
        name="merge",
    )(device, kept_count, keep_row, table, slow, home, *sources)


def start_copies(sources, wanted, groups=0):
    for code, target, sem in wanted:
        which, place = code >> 4, code & 15
        for index, source in enumerate(sources):
            if len(sources) == 1:
                here = which > -(1 << 20)
            elif index == 0:
                here = which <= 0
            elif index == len(sources) - 1:
                here = which >= index
            else:
                here = which == index

            @pl.when(here)
            def _(source=source, place=place, target=target, sem=sem):
                inside = jnp.minimum(place, source.shape[0] - 1)
                if groups == 0:
                    pltpu.make_async_copy(source.at[inside], target, sem).start()
                    return
                size = source.shape[1] // groups
                for group in range(groups):
                    rows = pl.ds(group * size, size)
                    pltpu.make_async_copy(
                        source.at[inside, rows, :], target.at[rows, :], sem.at[group]
                    ).start()


def choose_kernel(parts, n_sources, table_ref, *refs):
    sources, outs, sems = refs[:n_sources], refs[-1 - len(parts) : -1], refs[-1]
    targets = [
        (at + slot, out_ref.at[slot])
        for (at, total), out_ref in zip(parts, outs)
        for slot in range(total)
    ]
    start_copies(
        sources,
        [(table_ref[at], target, sems.at[number]) for number, (at, target) in enumerate(targets)],
    )
    for number, (_, target) in enumerate(targets):
        pltpu.make_async_copy(sources[0].at[0], target, sems.at[number]).wait()


def choose(table, parts, sources, name, after=()):
    block = sources[0].shape[1:]
    total = sum(count for _, count in parts)
    return pl.pallas_call(
        functools.partial(choose_kernel, parts, len(sources)),
        out_shape=tuple(jax.ShapeDtypeStruct((count,) + block, BF16) for _, count in parts),
        in_specs=[pl.BlockSpec(memory_space=pltpu.SMEM)]
        + [pl.BlockSpec(memory_space=pl.ANY)] * (len(sources) + len(after)),
        out_specs=tuple(pl.BlockSpec(memory_space=pltpu.VMEM) for _ in parts),
        scratch_shapes=[pltpu.SemaphoreType.DMA((total,))],
        compiler_params=pltpu.CompilerParams(vmem_limit_bytes=8 * MIB),
        cost_estimate=SMALL_COST,
        name=name,
    )(table, *sources, *after)


def join_kernel(spots_ref, near, side, mate, out_ref, sems):
    piece = near.shape[0]
    sources = (near, side, mate.at[0], mate.at[1])
    copies = []
    for number, source in enumerate(sources):
        place = pl.ds(pl.multiple_of(spots_ref[number] * piece, piece), piece)
        copies.append(pltpu.make_async_copy(source, out_ref.at[place, :], sems.at[number]))
    for copy in copies:
        copy.start()
    for copy in copies:
        copy.wait()


def join(spots, near, side, mate):
    shape = (4 * near.shape[0], near.shape[1])
    any_space = pl.BlockSpec(memory_space=pl.ANY)
    return pl.pallas_call(
        join_kernel,
        out_shape=jax.ShapeDtypeStruct(shape, BF16),
        in_specs=[pl.BlockSpec(memory_space=pltpu.SMEM)] + [any_space] * 3,
        out_specs=pl.BlockSpec(memory_space=pltpu.VMEM),
        scratch_shapes=[pltpu.SemaphoreType.DMA((4,))],
        compiler_params=pltpu.CompilerParams(vmem_limit_bytes=8 * MIB),
        name="join",
    )(spots, near, side, mate)


def in_hbm(array):
    return pltpu.with_memory_space_constraint(array, pltpu.HBM)


def split_store(value, high_ref, low_ref):
    high = value.astype(BF16)
    high_ref[...] = high
    low_ref[...] = (value - high.astype(F32)).astype(BF16)


def attend_kernel(n_after, own_ref, other_ref, rows_ref, b_ref, w_ref, *refs):
    (out_ref, held, normed, q_high, q_low, k_high, k_low, values, scores, sems) = refs[n_after:]
    blocks, rows, width = own_ref.shape
    span = held.shape[2]
    loads = [pltpu.make_async_copy(w_ref.at[j], held.at[j], sems.at[j]) for j in range(3)]
    for load in loads:
        load.start()
    gain, shift = rows_ref[0:1, :], rows_ref[1:2, :]
    for half, ref in enumerate((own_ref, other_ref)):
        for block in range(blocks):
            at = (half * blocks + block) * rows
            normed[at : at + rows] = norm_rows(ref[block].astype(F32), gain, shift).astype(BF16)

    def project(j):
        loads[j].wait()
        product = jnp.dot(normed[...], held[j], preferred_element_type=F32)
        return product + b_ref[j : j + 1, :]

    split_store(project(0) * HEAD_DIM ** (-0.5), q_high, q_low)
    split_store(project(1), k_high, k_low)
    values[...] = project(2).astype(BF16)
    tiles = span // 128
    heads = span // HEAD_DIM
    size = 2 * rows
    lane = lax.broadcasted_iota(jnp.int32, (1, 256), 1)

    def window(head):
        tile = min(head * HEAD_DIM // 128, tiles - 2)
        first = head * HEAD_DIM - tile * 128
        inside = (lane >= first) & (lane < first + HEAD_DIM)
        return tile, slice(tile * 128, tile * 128 + 256), inside

    def one_block(block, carry):
        near = pl.ds(pl.multiple_of(block * rows, rows), rows)
        far = pl.ds(pl.multiple_of((blocks + block) * rows, rows), rows)

        def both(ref, columns):
            return jnp.concatenate([ref[near, columns], ref[far, columns]], axis=0)

        def times(left, right):
            return lax.dot_general(
                left, right, (((1,), (1,)), ((), ())), preferred_element_type=F32
            )

        for head in range(heads):
            _, columns, inside = window(head)
            none = jnp.zeros((), BF16)
            qh = jnp.where(inside, both(q_high, columns), none)
            ql = jnp.where(inside, both(q_low, columns), none)
            kh, kl = both(k_high, columns), both(k_low, columns)
            scores[head * size : (head + 1) * size, :] = (
                times(qh, kh) + times(qh, kl) + times(ql, kh)
            )
        value = scores[...]
        value = jnp.exp(value - jnp.max(value, axis=-1, keepdims=True))
        weights = (value * (1.0 / jnp.sum(value, axis=-1, keepdims=True))).astype(BF16)
        sums = [None] * tiles
        for head in range(heads):
            tile, columns, inside = window(head)
            mixed = jnp.dot(
                weights[head * size : (head + 1) * size, :], both(values, columns),
                preferred_element_type=F32,
            )
            mixed = jnp.where(inside, mixed, 0.0)
            for part in range(2):
                piece = mixed[:, part * 128 : part * 128 + 128]
                old = sums[tile + part]
                sums[tile + part] = piece if old is None else old + piece
        result = jnp.concatenate(sums, axis=1).astype(BF16)
        out_ref[0, block] = result[:rows]
        out_ref[1, block] = result[rows:]
        return carry

    lax.fori_loop(0, blocks, one_block, 0)


def attend(own, other, rows_params, w_qkv, b_qkv, after=()):
    blocks, rows, width = own.shape
    span = w_qkv.shape[2]
    total = 2 * blocks * rows
    vmem = pl.BlockSpec(memory_space=pltpu.VMEM)
    return pl.pallas_call(
        functools.partial(attend_kernel, len(after)),
        out_shape=jax.ShapeDtypeStruct((2, blocks, rows, span), BF16),
        in_specs=[vmem] * 4 + [pl.BlockSpec(memory_space=pl.ANY)] * (1 + len(after)),
        out_specs=vmem,
        scratch_shapes=[pltpu.VMEM((3, width, span), BF16), pltpu.VMEM((total, width), BF16)]
        + [pltpu.VMEM((total, span), BF16)] * 5
        + [
            pltpu.VMEM((2 * rows * (span // HEAD_DIM), 2 * rows), F32),
            pltpu.SemaphoreType.DMA((3,)),
        ],
        compiler_params=pltpu.CompilerParams(vmem_limit_bytes=28 * MIB),
        cost_estimate=pl.CostEstimate(
            flops=24 * total * width * span, bytes_accessed=6 * width * span, transcendentals=0
        ),
        name="attend",
    )(own, other, rows_params, b_qkv, in_hbm(w_qkv), *after)


UP_TILE = 512
DOWN_TILE = 256
SLOTS = 5


def mlp_kernel(n_after, own_ref, other_ref, mine_ref, theirs_ref, rows_ref, b_up_ref, w_mine, w_theirs,
               w_up, w_down, *refs):
    (keep_ref, send_ref, residual, renormed, hidden, outs, ups, downs, out_sems, up_sems,
     down_sems) = refs[n_after:]
    blocks, rows, width = own_ref.shape
    half = blocks * rows
    span = outs.shape[1]
    up_steps, down_steps = w_up.shape[1] // UP_TILE, width // DOWN_TILE

    def load_up(step):
        columns = pl.ds(pl.multiple_of(step * UP_TILE, UP_TILE), UP_TILE)
        slot = lax.rem(step, SLOTS)
        return pltpu.make_async_copy(w_up.at[:, columns], ups.at[slot], up_sems.at[slot])

    def load_down(step):
        columns = pl.ds(pl.multiple_of(step * DOWN_TILE, DOWN_TILE), DOWN_TILE)
        slot = lax.rem(step, SLOTS)
        return pltpu.make_async_copy(w_down.at[:, columns], downs.at[slot], down_sems.at[slot])

    out_loads = [
        pltpu.make_async_copy(source, outs.at[number], out_sems.at[number])
        for number, source in enumerate((w_mine, w_theirs))
    ]
    for load in out_loads:
        load.start()
    load_up(jnp.int32(0)).start()
    gain, shift = rows_ref[2:3, :], rows_ref[3:4, :]
    mine = mine_ref[...].reshape(2 * half, span)
    theirs = jnp.concatenate(
        [theirs_ref[1].reshape(half, span), theirs_ref[0].reshape(half, span)], axis=0
    )
    for number, attended in enumerate((mine, theirs)):
        out_loads[number].wait()
        for slot in (range(1, 3), range(3, SLOTS))[number]:
            load_up(jnp.int32(slot)).start()
        for column in range(0, width, DOWN_TILE):
            columns = slice(column, column + DOWN_TILE)
            part = jnp.dot(attended, outs[number, :, columns], preferred_element_type=F32)
            part = part.astype(BF16).astype(F32)
            if number == 0:
                residual[:, columns] = part + rows_ref[4:5, columns]
            else:
                residual[:, columns] += part
    for side, ref in enumerate((own_ref, other_ref)):
        for block in range(blocks):
            at = slice((side * blocks + block) * rows, (side * blocks + block + 1) * rows)
            value = ref[block].astype(F32) + residual[at]
            if side == 0:
                residual[at] = value
            renormed[at] = norm_rows(value, gain, shift).astype(BF16)

    def one_up(step, carry):
        load_up(step).wait()
        slot = lax.rem(step, SLOTS)
        for part in range(0, UP_TILE, 256):
            columns = pl.ds(pl.multiple_of(step * UP_TILE + part, 256), 256)
            raised = jnp.dot(
                renormed[...], ups[slot, :, part : part + 256], preferred_element_type=F32
            )
            raised = raised + b_up_ref[0:1, columns]
            hidden[:, columns] = jax.nn.gelu(raised, approximate=True).astype(BF16)
        ahead = step + SLOTS

        @pl.when(ahead < up_steps)
        def _():
            load_up(ahead).start()

        @pl.when((ahead >= up_steps) & (ahead < up_steps + down_steps))
        def _():
            load_down(ahead - up_steps).start()

        return carry

    lax.fori_loop(0, up_steps, one_up, 0)

    def one_down(step, carry):
        load_down(step).wait()
        columns = pl.ds(pl.multiple_of(step * DOWN_TILE, DOWN_TILE), DOWN_TILE)
        lowered = jnp.dot(
            hidden[...], downs[lax.rem(step, SLOTS)], preferred_element_type=F32
        )
        kept = residual[:half, columns] + lowered[:half] + rows_ref[5:6, columns]
        keep_ref[:, :, columns] = kept.reshape(blocks, rows, DOWN_TILE)
        send_ref[:, :, columns] = lowered[half:].astype(BF16).reshape(blocks, rows, DOWN_TILE)

        @pl.when(step + SLOTS < down_steps)
        def _():
            load_down(step + SLOTS).start()

        return carry

    lax.fori_loop(0, down_steps, one_down, 0)


def mlp(own, other, mine, theirs, rows_params, b_up, weights, after):
    blocks, rows, width = own.shape
    span = mine.shape[3]
    total = 2 * blocks * rows
    vmem = pl.BlockSpec(memory_space=pltpu.VMEM)
    hbm = pl.BlockSpec(memory_space=pl.ANY)
    w_mine, w_theirs, w_up, w_down = weights
    hidden = w_up.shape[1]
    return pl.pallas_call(
        functools.partial(mlp_kernel, len(after)),
        out_shape=(
            jax.ShapeDtypeStruct((blocks, rows, width), F32),
            jax.ShapeDtypeStruct((blocks, rows, width), BF16),
        ),
        in_specs=[vmem] * 6 + [hbm] * (4 + len(after)),
        out_specs=(vmem, vmem),
        scratch_shapes=[
            pltpu.VMEM((total, width), F32),
            pltpu.VMEM((total, width), BF16),
            pltpu.VMEM((total, hidden), BF16),
            pltpu.VMEM((2, span, width), BF16),
            pltpu.VMEM((SLOTS, width, UP_TILE), BF16),
            pltpu.VMEM((SLOTS, hidden, DOWN_TILE), BF16),
            pltpu.SemaphoreType.DMA((2,)),
            pltpu.SemaphoreType.DMA((SLOTS,)),
            pltpu.SemaphoreType.DMA((SLOTS,)),
        ],
        compiler_params=pltpu.CompilerParams(vmem_limit_bytes=46 * MIB),
        cost_estimate=pl.CostEstimate(
            flops=8 * total * width * (span + hidden),
            bytes_accessed=4 * width * (span + hidden),
            transcendentals=0,
        ),
        name="mlp",
    )(
        own, other, mine, theirs, rows_params, b_up, in_hbm(w_mine), w_theirs, in_hbm(w_up),
        in_hbm(w_down), *after,
    )


def add_kernel(n_after, keep_ref, came_ref, *refs):
    out_ref = refs[n_after]
    out_ref[...] = (keep_ref[...] + came_ref[...].astype(F32)).astype(BF16)


def add(keep, came, after):
    vmem = pl.BlockSpec(memory_space=pltpu.VMEM)
    return pl.pallas_call(
        functools.partial(add_kernel, len(after)),
        out_shape=jax.ShapeDtypeStruct(came.shape, BF16),
        in_specs=[vmem] * 2 + [pl.BlockSpec(memory_space=pl.ANY)] * len(after),
        out_specs=vmem,
        compiler_params=pltpu.CompilerParams(vmem_limit_bytes=8 * MIB),
        cost_estimate=SMALL_COST,
        name="add",
    )(keep, came, *after)


def swap(value):
    return lax.ppermute(value, "tensor", [(0, 1), (1, 0)])


def line_up_kernel(total, n_after, *refs):
    sources, out_ref, sems = refs[:total], refs[total + n_after], refs[-1]
    copies = [
        pltpu.make_async_copy(source, out_ref.at[number], sems.at[number])
        for number, source in enumerate(sources)
    ]
    for copy in copies:
        copy.start()
    for copy in copies:
        copy.wait()


def line_up(arrays, after, name):
    any_space = pl.BlockSpec(memory_space=pl.ANY)
    total = len(arrays)
    return pl.pallas_call(
        functools.partial(line_up_kernel, total, len(after)),
        out_shape=jax.ShapeDtypeStruct((total,) + arrays[0].shape, arrays[0].dtype),
        in_specs=[any_space] * (total + len(after)),
        out_specs=pl.BlockSpec(memory_space=pltpu.VMEM),
        scratch_shapes=[pltpu.SemaphoreType.DMA((total,))],
        compiler_params=pltpu.CompilerParams(vmem_limit_bytes=8 * MIB),
        cost_estimate=SMALL_COST,
        name=name,
    )(*arrays, *after)


def w_out_place(w_out):
    core = lax.axis_index("dp") & 1
    group = lax.axis_index("groups")
    return 2 * group + core, 2 * (1 - group) + core, w_out.shape[0] // 4


def piece_kernel(n_after, number_ref, w_ref, *refs):
    out_ref, sem = refs[n_after:]
    piece = out_ref.shape[0]
    rows = pl.ds(pl.multiple_of(number_ref[0] * piece, piece), piece)
    copy = pltpu.make_async_copy(w_ref.at[rows, :], out_ref, sem)
    copy.start()
    copy.wait()


def w_out_piece(w_out, after):
    number, _, piece = w_out_place(w_out)
    any_space = pl.BlockSpec(memory_space=pl.ANY)
    return pl.pallas_call(
        functools.partial(piece_kernel, len(after)),
        out_shape=jax.ShapeDtypeStruct((piece, w_out.shape[1]), BF16),
        in_specs=[pl.BlockSpec(memory_space=pltpu.SMEM)] + [any_space] * (1 + len(after)),
        out_specs=pl.BlockSpec(memory_space=pltpu.VMEM),
        scratch_shapes=[pltpu.SemaphoreType.DMA],
        compiler_params=pltpu.CompilerParams(vmem_limit_bytes=4 * MIB),
        cost_estimate=SMALL_COST,
        name="w_piece",
    )(number.astype(jnp.int32).reshape(1), in_hbm(w_out), *after)


def other_w_out(w_out, near, side, after):
    number, other, _ = w_out_place(w_out)
    dp_size = lax.axis_size("dp")
    both = line_up([near, side], after, "w_both")
    mate = lax.ppermute(both, "dp", [(d, d ^ 1) for d in range(dp_size)])
    spots = jnp.stack([number, other, number ^ 1, other ^ 1]).astype(jnp.int32)
    return join(spots, near, side, mate)


def attend_rows(projected):
    row_total, count_blocks, width = (projected.shape[0], projected.shape[1], projected.shape[3])
    head_count = width // HEAD_DIM
    queries = projected[:, :, 0].reshape(row_total, count_blocks, head_count, HEAD_DIM)
    key_rows = projected[:, :, 1].reshape(row_total, count_blocks, head_count, HEAD_DIM)
    values = projected[:, :, 2].astype(BF16).reshape(row_total, count_blocks, head_count, HEAD_DIM)
    scores = jnp.einsum(
        "qnhd,snhd->nhqs", queries, key_rows, precision=lax.Precision.HIGHEST
    ) * HEAD_DIM ** (-0.5)
    weights = jax.nn.softmax(scores, axis=-1).astype(BF16)
    attended = jnp.einsum("nhqs,snhd->qnhd", weights, values, preferred_element_type=F32)
    return attended.astype(BF16).reshape(row_total, count_blocks, width)


def encode_split(own, params):
    (pre_gain, pre_shift, w_qkv, b_qkv, w_out, b_out, mlp_gain, mlp_shift, w_up, b_up, w_down,
     b_down) = params
    block_rows = jnp.swapaxes(own, 0, 1)
    rows_dev = block_rows.shape[0]
    gathered = lax.all_gather(block_rows, "tensor", axis=0, tiled=True)
    normed = norm_rows(gathered.astype(F32), pre_gain, pre_shift).astype(BF16)
    attended = attend_rows(
        jnp.einsum("qnd,jde->qnje", normed, w_qkv, preferred_element_type=F32) + b_qkv[None, None]
    )
    partial_value = jnp.einsum("qne,ed->qnd", attended, w_out, preferred_element_type=F32)
    summed = lax.psum(partial_value.astype(BF16), "tensor").astype(F32)
    residual_all = gathered.astype(F32) + summed + b_out
    renormed = norm_rows(residual_all, mlp_gain, mlp_shift).astype(BF16)
    raised = jnp.einsum("qnd,df->qnf", renormed, w_up, preferred_element_type=F32) + b_up
    hidden = jax.nn.gelu(raised, approximate=True).astype(BF16)
    residual = lax.dynamic_slice_in_dim(
        residual_all, lax.axis_index("tensor") * rows_dev, rows_dev, 0
    )
    mlp_out = lax.psum_scatter(
        jnp.einsum("qnf,fd->qnd", hidden, w_down, preferred_element_type=F32).astype(BF16),
        "tensor", scatter_dimension=0, tiled=True,
    ).astype(F32)
    return jnp.swapaxes((residual + mlp_out + b_down).astype(BF16), 0, 1)


def per_device(paired, patches, kept_count, keep_list, *params):
    home = in_hbm(patches[0])
    keep_row = in_hbm(keep_list[0])
    kept_count = in_hbm(kept_count)
    dp_size = lax.axis_size("dp")
    device = lax.axis_index("dp").astype(jnp.int32).reshape(1)
    mates = [(d, d ^ 1) for d in range(dp_size)]
    pairs = [(d, d ^ 2) for d in range(dp_size)]
    nexts = [(d, min(max(((d + 2) ^ 2) - 2, d & 1), dp_size - 2 + (d & 1))) for d in range(dp_size)]

    def to_mate(value):
        return lax.ppermute(value, "dp", mates)

    def to_pair(value):
        return lax.ppermute(value, "dp", pairs)

    def to_next(value):
        return lax.ppermute(value, "dp", nexts)

    mine, for_mate = pack(device, kept_count, keep_row, home)
    from_mate = to_mate(for_mate)
    table = make_plan(device, kept_count)
    short = table[AT_SHORT : AT_SHORT + 1].astype(F32)
    if paired:
        short = short + lax.ppermute(short, "groups", [(0, 1), (1, 0)])
    else:
        short = lax.pmax(short, "groups")
    short = short[0] > 0

    parts = tuple(zip(STARTS, CHUNKS))
    sends = [(AT_PAIR + at, size) for at, size in parts] + [(AT_NEXT + at, size) for at, size in parts]
    going = choose(table, sends, [mine, from_mate], "send")
    came_pair = [to_pair(value) for value in going[: len(parts)]]
    came_next = [to_next(value) for value in going[len(parts) :]]

    def deal_fast(chunk, after):
        came = [came_pair[min(part, chunk)] for part in range(len(parts))]
        came = came + [came_next[min(part, chunk)] for part in range(len(parts))]
        at, size = parts[chunk]
        sources = [mine, from_mate] + came
        return choose(table, [(AT_DEALT + at, size)], sources, "deal_%d" % chunk, after)[0]

    def deal_slow(chunk):
        chips = dp_size // 2
        (picked,) = choose(table, [(AT_SLOW_SEND, ROOM * chips)], [mine, from_mate], "deal_slow")
        picked = picked.reshape((chips, ROOM) + picked.shape[1:])
        spread = jnp.repeat(picked, 2, axis=0)
        arrived = lax.all_to_all(spread, "dp", split_axis=0, concat_axis=0, tiled=True)
        at, size = parts[chunk]
        return jnp.stack(
            [
                arrived[table[AT_SLOW_SOURCE + j], table[AT_SLOW_PLACE + j]]
                for j in range(at, at + size)
            ]
        )

    def deal(chunk, after=()):
        return lax.cond(short, lambda: deal_slow(chunk), lambda: deal_fast(chunk, after))

    if paired:
        (pre_gain, pre_shift, w_qkv, b_qkv, w_out, b_out, mlp_gain, mlp_shift, w_up, b_up, w_down,
         b_down) = params
        rows_params = jnp.stack([pre_gain, pre_shift, mlp_gain, mlp_shift, b_out, b_down])
        b_up = b_up.reshape(1, -1)
        w_near = swap(w_out_piece(w_out, [for_mate]))

        def start(own, after):
            other = swap(own)
            mine = attend(own, other, rows_params, w_qkv, b_qkv, after)
            return own, other, mine, swap(mine)

        def finish(state, after):
            keep, send = mlp(*state, rows_params, b_up, weights, after)
            return keep, swap(send)

        blocks_0 = deal(0)
        state_0 = start(blocks_0, [])
        w_sent = line_up([w_near], [blocks_0], "w_near")
        blocks_1 = deal(1, [w_sent])
        state_1 = start(blocks_1, [])
        w_side = lax.ppermute(w_sent, "groups", [(0, 1), (1, 0)])[0]
        w_theirs = other_w_out(w_out, w_near, w_side, [blocks_1])
        weights = (w_out, w_theirs, w_up, w_down)
        done_0 = finish(state_0, [state_1[2]])
        done_1 = finish(state_1, [done_0[0]])
        results, from_pair, from_next = [], [], []
        for done, beside in ((done_0, done_1[:1]), (done_1, ())):
            results.append(add(*done, list(beside) + from_pair[-1:] + from_next[-1:]))
            from_pair.append(to_pair(results[-1]))
            from_next.append(to_next(results[-1]))
    else:
        results = [encode_split(deal(chunk), params) for chunk in range(len(parts))]
        from_pair = [to_pair(value) for value in results]
        from_next = [to_next(value) for value in results]

    back = results + from_pair + from_next
    back = back + [to_mate(value) for value in back]

    def home_slow():
        spread = lax.all_gather(jnp.concatenate(results), "dp", axis=0, tiled=True)
        places = table[AT_SLOW_HOME : AT_SLOW_HOME + 2 * PAGE_HALF]
        return (
            jnp.take(spread, places[:PAGE_HALF], axis=0),
            jnp.take(spread, places[PAGE_HALF:], axis=0),
        )

    found = lax.cond(short, home_slow, lambda: (mine, from_mate))
    slow = short.astype(jnp.int32).reshape(1)
    return merge(device, kept_count, keep_row, table, slow, home, back + list(found))[None]


def solution(mesh):
    in_specs = (
        P(("groups", "dp"), "tensor", None, None),
        P("groups"),
        P(("groups", "dp"), None),
        P(),
        P(),
        P(None, None, "tensor"),
        P(None, "tensor"),
        P("tensor", None),
        P(),
        P(),
        P(),
        P(None, "tensor"),
        P("tensor"),
        P("tensor", None),
        P(),
    )
    out_specs = P(("groups", "dp"), "tensor", None, None)
    paired = mesh.shape["tensor"] == 2 and mesh.shape["groups"] == 2
    return jax.shard_map(
        functools.partial(per_device, paired), mesh=mesh, in_specs=in_specs, out_specs=out_specs,
        check_vma=False,
    )
```

```python
import functools

import jax
import jax.numpy as jnp
from jax import lax
from jax.experimental import pallas as pl
from jax.experimental.pallas import tpu as pltpu
from jax.sharding import PartitionSpec as P

HEAD_DIM = 112
CHUNKS = (3, 2)
STARTS = (0, 3)
ROOM = 5
PAGE_HALF = 8
GROUP_ROWS = 16
F32 = jnp.float32
BF16 = jnp.bfloat16
MIB = 1 << 20
SMALL_COST = pl.CostEstimate(flops=1000, bytes_accessed=1000, transcendentals=0)


def norm_rows(inputs, gain, shift):
    average = jnp.mean(inputs, axis=-1, keepdims=True)
    centred = inputs - average
    variance = jnp.mean(centred * centred, axis=-1, keepdims=True)
    return centred * lax.rsqrt(variance + 1e-06) * gain + shift


def pick_at(values, index):
    total = jnp.int32(0)
    for place, value in enumerate(values):
        total = total + jnp.where(index == place, value, 0)
    return total


def page_ends_of(count_ref, pages):
    ends = [jnp.int32(0)]
    for page in range(pages):
        ends.append(ends[-1] + count_ref[page])
    return ends


def chunk_of(slot):
    number, start = jnp.int32(0), jnp.int32(0)
    for chunk in range(1, len(CHUNKS)):
        number = jnp.where(slot >= STARTS[chunk], chunk, number)
        start = jnp.where(slot >= STARTS[chunk], STARTS[chunk], start)
    return number, slot - start


def line_plan(ends, chips, core):
    held = [(ends[2 * chip] + 1 - core) >> 1 for chip in range(chips + 1)]
    total = held[chips]
    wanted = [
        jnp.clip(held[i], jnp.maximum(total - ROOM * (chips - i), 0), jnp.minimum(total, ROOM * i))
        for i in range(chips + 1)
    ]
    below, above = list(wanted), list(wanted)
    for i in range(1, chips + 1):
        below[i] = jnp.minimum(below[i], below[i - 1] + ROOM)
    for i in range(chips - 1, -1, -1):
        above[i] = jnp.maximum(above[i], above[i + 1] - ROOM)
    dealt = [(low + high) >> 1 for low, high in zip(below, above)]
    short = jnp.int32(0)
    for cut in range(1, chips):
        right = held[cut] - dealt[cut]
        most_right = jnp.minimum(held[cut] - held[cut - 1], ROOM)
        most_left = jnp.minimum(held[cut + 1] - held[cut], ROOM)
        short = short + jnp.where((right > most_right) | (-right > most_left), 1, 0)
    return held, dealt, short


AT_PAIR = 0
AT_NEXT = AT_PAIR + ROOM
AT_DEALT = AT_NEXT + ROOM
AT_HOME = AT_DEALT + ROOM
AT_SHORT = AT_HOME + 2 * PAGE_HALF
AT_SLOW_SOURCE = AT_SHORT + 1
AT_SLOW_PLACE = AT_SLOW_SOURCE + ROOM
AT_SLOW_HOME = AT_SLOW_PLACE + ROOM
AT_IN_ORDER = AT_SLOW_HOME + 2 * PAGE_HALF
AT_SLOW_SEND = AT_IN_ORDER + 2 * PAGE_HALF


def plan_kernel(pages, device_ref, count_ref, table_ref):
    chips = pages // 2
    device = device_ref[0]
    core, chip = device & 1, device >> 1
    ends = page_ends_of(count_ref, pages)
    held, dealt, short = line_plan(ends, chips, core)
    held_mate, dealt_mate, short_mate = line_plan(ends, chips, 1 - core)
    table_ref[AT_SHORT] = jnp.where(short + short_mate > 0, 1, 0)
    falls, falls_mate = (
        [jnp.where(ranks[i] - ranks_dealt[i] > 2, 1, 0) for i in range(chips)]
        for ranks, ranks_dealt in ((held, dealt), (held_mate, dealt_mate))
    )

    low, high = pick_at(held, chip), pick_at(held, chip + 1)
    first, end = pick_at(dealt, chip), pick_at(dealt, chip + 1)
    falls_here = pick_at(falls, chip)
    own_start, own_end = pick_at(ends, device), pick_at(ends, device + 1)
    mate_start = pick_at(ends, device ^ 1)

    def turned(offset, falling):
        return jnp.where(falling > 0, ROOM - 1 - offset, offset)

    def local_code(rank):
        position = 2 * rank + core
        own = (position >= own_start) & (position < own_end)
        return jnp.where(own, (position - own_start) >> 1, 16 + ((position - mate_start) >> 1))

    def part_code(count, source):
        number, place = chunk_of(count)
        return (source + number) * 16 + place

    sides = len(CHUNKS)
    odd = chip & 1
    right_side, left_side = sides * odd, sides * (1 - odd)

    for slot in range(ROOM):
        rightwards, leftwards = local_code(high - 1 - slot), local_code(low + slot)
        table_ref[AT_PAIR + slot] = jnp.where(odd > 0, leftwards, rightwards)
        table_ref[AT_NEXT + slot] = jnp.where(odd > 0, rightwards, leftwards)
        offset = turned(jnp.int32(slot), falls_here)
        rank = first + offset
        code = jnp.where(rank < low, part_code(low - 1 - rank, 2 + left_side), local_code(rank))
        code = jnp.where(rank >= high, part_code(rank - high, 2 + right_side), code)
        table_ref[AT_DEALT + slot] = code
        node = jnp.int32(0)
        for place in range(1, chips):
            node = node + jnp.where(held[place] <= rank, 1, 0)
        table_ref[AT_SLOW_SOURCE + slot] = 2 * node + core
        table_ref[AT_SLOW_PLACE + slot] = offset
    for half, (ranks_dealt, turns) in enumerate(((dealt, falls), (dealt_mate, falls_mate))):
        lane = core ^ half
        here, there = pick_at(ranks_dealt, chip), pick_at(ranks_dealt, chip + 1)
        before = pick_at(ranks_dealt, chip - 1)
        turns_here, turns_right, turns_left = (pick_at(turns, chip + i) for i in (0, 1, -1))
        for slot in range(PAGE_HALF):
            rank = (own_start + ((own_start + lane) & 1) + 2 * slot - lane) >> 1
            at = half * PAGE_HALF + slot
            base = 3 * sides * half
            code = part_code(turned(rank - here, turns_here), base)
            right = part_code(turned(rank - there, turns_right), base + sides + right_side)
            left = part_code(turned(rank - before, turns_left), base + sides + left_side)
            code = jnp.where(rank >= there, right, code)
            table_ref[AT_HOME + at] = jnp.where(rank < here, left, code)
            node, start_there, turns_there = jnp.int32(0), jnp.int32(0), turns[0]
            for place in range(1, chips):
                beyond = ranks_dealt[place] <= rank
                node = node + jnp.where(beyond, 1, 0)
                start_there = jnp.where(beyond, ranks_dealt[place], start_there)
                turns_there = jnp.where(beyond, turns[place], turns_there)
            slow = (2 * node + lane) * ROOM + turned(rank - start_there, turns_there)
            table_ref[AT_SLOW_HOME + at] = jnp.clip(slow, 0, pages * ROOM - 1)
            table_ref[AT_IN_ORDER + at] = jnp.int32((6 * sides + half) * 16 + slot)
    for node in range(chips):
        for slot in range(ROOM):
            code = local_code(dealt[node] + slot)
            table_ref[AT_SLOW_SEND + node * ROOM + slot] = jnp.clip(code, 0, 31)


def make_plan(device, kept_count):
    pages = kept_count.shape[0]
    size = AT_SLOW_SEND + ROOM * (pages // 2)
    return pl.pallas_call(
        functools.partial(plan_kernel, pages),
        out_shape=jax.ShapeDtypeStruct((size,), jnp.int32),
        in_specs=[pl.BlockSpec(memory_space=pltpu.SMEM)] * 2,
        out_specs=pl.BlockSpec(memory_space=pltpu.SMEM),
        compiler_params=pltpu.CompilerParams(vmem_limit_bytes=MIB),
        cost_estimate=SMALL_COST,
        name="plan",
    )(device, kept_count)


def kept_blocks(device_ref, count_ref, keep_ref, pages):
    device = device_ref[0]
    start, count = jnp.int32(0), jnp.int32(0)
    for page in range(pages):
        start = start + jnp.where(page < device, count_ref[page], 0)
        count = count + jnp.where(page == device, count_ref[page], 0)
    blocks = []
    for half in range(2):
        offset = (start + device + half) & 1
        for slot in range(PAGE_HALF):
            index = 2 * slot + offset
            block = keep_ref[jnp.minimum(index, 2 * PAGE_HALF - 1)]
            blocks.append(jnp.where(index < count, block, -1))
    return blocks


def kept_blocks_once(device_ref, count_ref, keep_ref, pages, held):
    @pl.when(pl.program_id(0) == 0)
    def _():
        for slot, block in enumerate(kept_blocks(device_ref, count_ref, keep_ref, pages)):
            held[slot] = block

    return [held[slot] for slot in range(2 * PAGE_HALF)]


def pack_kernel(pages, device_ref, count_ref, keep_ref, home_ref, mine_ref, mate_ref, held):
    page_blocks, width = home_ref.shape[1], home_ref.shape[2]
    blocks = kept_blocks_once(device_ref, count_ref, keep_ref, pages, held)
    span = GROUP_ROWS * page_blocks
    row = lax.broadcasted_iota(jnp.int32, (GROUP_ROWS, span), 0)
    column = lax.broadcasted_iota(jnp.int32, (GROUP_ROWS, span), 1)
    chosen = jnp.concatenate(
        [jnp.where(column == row * page_blocks + block, 1.0, 0.0).astype(BF16) for block in blocks],
        axis=0,
    )
    packed = jnp.dot(
        chosen, home_ref[...].reshape(span, width), preferred_element_type=F32
    ).astype(BF16)
    half = PAGE_HALF * GROUP_ROWS
    mine_ref[...] = packed[:half].reshape(PAGE_HALF, GROUP_ROWS, width)
    mate_ref[...] = packed[half:].reshape(PAGE_HALF, GROUP_ROWS, width)


def pack(device, kept_count, keep_row, home):
    rows, page_blocks, width = home.shape
    shape = jax.ShapeDtypeStruct((PAGE_HALF, rows, width), BF16)
    place = pl.BlockSpec((PAGE_HALF, GROUP_ROWS, width), lambda step, *_: (0, step, 0))
    return pl.pallas_call(
        functools.partial(pack_kernel, kept_count.shape[0]),
        out_shape=(shape, shape),
        grid_spec=pltpu.PrefetchScalarGridSpec(
            num_scalar_prefetch=3,
            grid=(rows // GROUP_ROWS,),
            in_specs=[
                pl.BlockSpec((GROUP_ROWS, page_blocks, width), lambda step, *_: (step, 0, 0))
            ],
            out_specs=(place, place),
            scratch_shapes=[pltpu.SMEM((2 * PAGE_HALF,), jnp.int32)],
        ),
        compiler_params=pltpu.CompilerParams(vmem_limit_bytes=16 * MIB),
        name="pack",
    )(device, kept_count, keep_row, home)


LATE = (3, 5, 9, 11)


def merge_kernel(pages, device_ref, count_ref, keep_ref, code_ref, home_ref, found_ref, *refs):
    late, out_ref, held = refs[:-2], refs[-2], refs[-1]
    page_blocks, width = home_ref.shape[1], home_ref.shape[2]
    slots, size = 2 * PAGE_HALF, CHUNKS[-1]
    places = slots + size * len(LATE)

    @pl.when(pl.program_id(0) == 0)
    def _():
        blocks = kept_blocks(device_ref, count_ref, keep_ref, pages)
        spots = []
        for slot in range(slots):
            code = code_ref[slot]
            spot = jnp.int32(slot)
            for number, source in enumerate(LATE):
                spot = jnp.where(code >> 4 == source, slots + number * size + (code & 15), spot)
            spots.append(jnp.where(blocks[slot] >= 0, spot, -1))
        for place in range(places):
            block = jnp.int32(-1)
            for slot in range(slots) if place >= slots else (place,):
                block = jnp.where(spots[slot] == place, blocks[slot], block)
            held[place] = block

    span = GROUP_ROWS * page_blocks
    depth = places * GROUP_ROWS
    row = lax.broadcasted_iota(jnp.int32, (span, depth), 0)
    column = lax.broadcasted_iota(jnp.int32, (span, depth), 1)
    place_id = lax.broadcasted_iota(jnp.int32, (1, depth), 1) // GROUP_ROWS
    block_id = lax.broadcasted_iota(jnp.int32, (span, 1), 0) % page_blocks
    wanted = jnp.full((1, depth), -1, jnp.int32)
    kept = jnp.zeros((span, 1), jnp.int32)
    for place in range(places):
        block = held[place]
        wanted = jnp.where(place_id == place, block, wanted)
        kept = kept + jnp.where(block_id == block, 1, 0)
    chosen = jnp.where(
        (row // page_blocks == column % GROUP_ROWS) & (row % page_blocks == wanted), 1.0, 0.0
    ).astype(BF16)
    source = jnp.concatenate(
        [ref[...].reshape(-1, width) for ref in (found_ref,) + tuple(late)], axis=0
    )
    landed = jnp.dot(chosen, source, preferred_element_type=F32)
    home = home_ref[...].reshape(span, width).astype(F32)
    merged = jnp.where(kept > 0, landed, home).astype(BF16)
    out_ref[...] = merged.reshape(GROUP_ROWS, page_blocks, width)


def merge(device, kept_count, keep_row, codes, home, found, late):
    rows, page_blocks, width = home.shape
    page = pl.BlockSpec((GROUP_ROWS, page_blocks, width), lambda step, *_: (step, 0, 0))

    def some(array):
        return pl.BlockSpec((array.shape[0], GROUP_ROWS, width), lambda step, *_: (0, step, 0))

    return pl.pallas_call(
        functools.partial(merge_kernel, kept_count.shape[0]),
        out_shape=jax.ShapeDtypeStruct(home.shape, BF16),
        grid_spec=pltpu.PrefetchScalarGridSpec(
            num_scalar_prefetch=4,
            grid=(rows // GROUP_ROWS,),
            in_specs=[page, some(found)] + [some(array) for array in late],
            out_specs=page,
            scratch_shapes=[
                pltpu.SMEM((found.shape[0] + CHUNKS[-1] * len(LATE),), jnp.int32)
            ],
        ),
        compiler_params=pltpu.CompilerParams(vmem_limit_bytes=20 * MIB),
        cost_estimate=SMALL_COST,
        name="merge",
    )(device, kept_count, keep_row, codes, home, found, *late)


def start_copies(sources, wanted):
    for code, target, sem in wanted:
        which, place = code >> 4, code & 15
        for index, source in enumerate(sources):
            if len(sources) == 1:
                here = which > -(1 << 20)
            elif index == 0:
                here = which <= 0
            elif index == len(sources) - 1:
                here = which >= index
            else:
                here = which == index

            @pl.when(here)
            def _(source=source, place=place, target=target, sem=sem):
                inside = jnp.minimum(place, source.shape[0] - 1)
                pltpu.make_async_copy(source.at[inside], target, sem).start()


def choose_kernel(parts, n_sources, table_ref, *refs):
    sources, outs, sems = refs[:n_sources], refs[-1 - len(parts) : -1], refs[-1]
    targets = [
        (at + slot, out_ref.at[slot])
        for (at, total), out_ref in zip(parts, outs)
        for slot in range(total)
    ]
    start_copies(
        sources,
        [(table_ref[at], target, sems.at[number]) for number, (at, target) in enumerate(targets)],
    )
    for number, (_, target) in enumerate(targets):
        pltpu.make_async_copy(sources[0].at[0], target, sems.at[number]).wait()


def choose(table, parts, sources, name, after=()):
    block = sources[0].shape[1:]
    total = sum(count for _, count in parts)
    return pl.pallas_call(
        functools.partial(choose_kernel, parts, len(sources)),
        out_shape=tuple(jax.ShapeDtypeStruct((count,) + block, BF16) for _, count in parts),
        in_specs=[pl.BlockSpec(memory_space=pltpu.SMEM)]
        + [pl.BlockSpec(memory_space=pl.ANY)] * (len(sources) + len(after)),
        out_specs=tuple(pl.BlockSpec(memory_space=pltpu.VMEM) for _ in parts),
        scratch_shapes=[pltpu.SemaphoreType.DMA((total,))],
        compiler_params=pltpu.CompilerParams(vmem_limit_bytes=8 * MIB),
        cost_estimate=SMALL_COST,
        name=name,
    )(table, *sources, *after)


def join_kernel(spots_ref, near, side, mate, out_ref, sems):
    piece = near.shape[0]
    sources = (near, side, mate.at[0], mate.at[1])
    copies = []
    for number, source in enumerate(sources):
        place = pl.ds(pl.multiple_of(spots_ref[number] * piece, piece), piece)
        copies.append(pltpu.make_async_copy(source, out_ref.at[place, :], sems.at[number]))
    for copy in copies:
        copy.start()
    for copy in copies:
        copy.wait()


def join(spots, near, side, mate):
    shape = (4 * near.shape[0], near.shape[1])
    any_space = pl.BlockSpec(memory_space=pl.ANY)
    return pl.pallas_call(
        join_kernel,
        out_shape=jax.ShapeDtypeStruct(shape, BF16),
        in_specs=[pl.BlockSpec(memory_space=pltpu.SMEM)] + [any_space] * 3,
        out_specs=pl.BlockSpec(memory_space=pltpu.VMEM),
        scratch_shapes=[pltpu.SemaphoreType.DMA((4,))],
        compiler_params=pltpu.CompilerParams(vmem_limit_bytes=8 * MIB),
        name="join",
    )(spots, near, side, mate)


def in_hbm(array):
    return pltpu.with_memory_space_constraint(array, pltpu.HBM)


def split_store(value, high_ref, low_ref):
    high = value.astype(BF16)
    high_ref[...] = high
    low_ref[...] = (value - high.astype(F32)).astype(BF16)


def attend_kernel(n_after, own_ref, other_ref, rows_ref, b_ref, w_ref, *refs):
    (out_ref, held, normed, q_high, q_low, k_high, k_low, values, scores, sems) = refs[n_after:]
    blocks, rows, width = own_ref.shape
    span = held.shape[2]
    loads = [pltpu.make_async_copy(w_ref.at[j], held.at[j], sems.at[j]) for j in range(3)]
    for load in loads:
        load.start()
    gain, shift = rows_ref[0:1, :], rows_ref[1:2, :]
    for half, ref in enumerate((own_ref, other_ref)):
        for block in range(blocks):
            at = (half * blocks + block) * rows
            normed[at : at + rows] = norm_rows(ref[block].astype(F32), gain, shift).astype(BF16)

    def project(j):
        loads[j].wait()
        product = jnp.dot(normed[...], held[j], preferred_element_type=F32)
        return product + b_ref[j : j + 1, :]

    split_store(project(0) * HEAD_DIM ** (-0.5), q_high, q_low)
    split_store(project(1), k_high, k_low)
    values[...] = project(2).astype(BF16)
    tiles = span // 128
    heads = span // HEAD_DIM
    size = 2 * rows
    lane = lax.broadcasted_iota(jnp.int32, (1, 256), 1)

    def window(head):
        tile = min(head * HEAD_DIM // 128, tiles - 2)
        first = head * HEAD_DIM - tile * 128
        inside = (lane >= first) & (lane < first + HEAD_DIM)
        return tile, slice(tile * 128, tile * 128 + 256), inside

    def one_block(block, carry):
        near = pl.ds(pl.multiple_of(block * rows, rows), rows)
        far = pl.ds(pl.multiple_of((blocks + block) * rows, rows), rows)

        def both(ref, columns):
            return jnp.concatenate([ref[near, columns], ref[far, columns]], axis=0)

        def times(left, right):
            return lax.dot_general(
                left, right, (((1,), (1,)), ((), ())), preferred_element_type=F32
            )

        for head in range(heads):
            _, columns, inside = window(head)
            none = jnp.zeros((), BF16)
            qh = jnp.where(inside, both(q_high, columns), none)
            ql = jnp.where(inside, both(q_low, columns), none)
            kh, kl = both(k_high, columns), both(k_low, columns)
            scores[head * size : (head + 1) * size, :] = (
                times(qh, kh) + times(qh, kl) + times(ql, kh)
            )
        value = scores[...]
        value = jnp.exp(value - jnp.max(value, axis=-1, keepdims=True))
        weights = (value * (1.0 / jnp.sum(value, axis=-1, keepdims=True))).astype(BF16)
        sums = [None] * tiles
        for head in range(heads):
            tile, columns, inside = window(head)
            mixed = jnp.dot(
                weights[head * size : (head + 1) * size, :], both(values, columns),
                preferred_element_type=F32,
            )
            mixed = jnp.where(inside, mixed, 0.0)
            for part in range(2):
                piece = mixed[:, part * 128 : part * 128 + 128]
                old = sums[tile + part]
                sums[tile + part] = piece if old is None else old + piece
        result = jnp.concatenate(sums, axis=1).astype(BF16)
        out_ref[0, block] = result[:rows]
        out_ref[1, block] = result[rows:]
        return carry

    lax.fori_loop(0, blocks, one_block, 0)


def attend(own, other, rows_params, w_qkv, b_qkv, after=()):
    blocks, rows, width = own.shape
    span = w_qkv.shape[2]
    total = 2 * blocks * rows
    vmem = pl.BlockSpec(memory_space=pltpu.VMEM)
    return pl.pallas_call(
        functools.partial(attend_kernel, len(after)),
        out_shape=jax.ShapeDtypeStruct((2, blocks, rows, span), BF16),
        in_specs=[vmem] * 4 + [pl.BlockSpec(memory_space=pl.ANY)] * (1 + len(after)),
        out_specs=vmem,
        scratch_shapes=[pltpu.VMEM((3, width, span), BF16), pltpu.VMEM((total, width), BF16)]
        + [pltpu.VMEM((total, span), BF16)] * 5
        + [
            pltpu.VMEM((2 * rows * (span // HEAD_DIM), 2 * rows), F32),
            pltpu.SemaphoreType.DMA((3,)),
        ],
        compiler_params=pltpu.CompilerParams(vmem_limit_bytes=28 * MIB),
        cost_estimate=pl.CostEstimate(
            flops=24 * total * width * span, bytes_accessed=6 * width * span, transcendentals=0
        ),
        name="attend",
    )(own, other, rows_params, b_qkv, in_hbm(w_qkv), *after)


UP_TILE = 768
DOWN_TILE = 256
SLOTS = 4


def mlp_kernel(n_after, own_ref, other_ref, mine_ref, theirs_ref, rows_ref, b_up_ref, w_mine, w_theirs,
               w_up, w_down, *refs):
    (keep_ref, send_ref, residual, renormed, hidden, outs, ups, downs, out_sems, up_sems,
     down_sems) = refs[n_after:]
    blocks, rows, width = own_ref.shape
    half = blocks * rows
    span = outs.shape[1]
    up_steps, down_steps = w_up.shape[1] // UP_TILE, width // DOWN_TILE

    def load_up(step):
        columns = pl.ds(pl.multiple_of(step * UP_TILE, UP_TILE), UP_TILE)
        slot = lax.rem(step, SLOTS)
        return pltpu.make_async_copy(w_up.at[:, columns], ups.at[slot], up_sems.at[slot])

    def load_down(step):
        columns = pl.ds(pl.multiple_of(step * DOWN_TILE, DOWN_TILE), DOWN_TILE)
        slot = lax.rem(step, SLOTS)
        return pltpu.make_async_copy(w_down.at[:, columns], downs.at[slot], down_sems.at[slot])

    out_loads = [
        pltpu.make_async_copy(source, outs.at[number], out_sems.at[number])
        for number, source in enumerate((w_mine, w_theirs))
    ]
    for load in out_loads:
        load.start()
    load_up(jnp.int32(0)).start()
    gain, shift = rows_ref[2:3, :], rows_ref[3:4, :]
    mine = mine_ref[...].reshape(2 * half, span)
    theirs = jnp.concatenate(
        [theirs_ref[1].reshape(half, span), theirs_ref[0].reshape(half, span)], axis=0
    )
    for number, attended in enumerate((mine, theirs)):
        out_loads[number].wait()
        for slot in (range(1, 3), range(3, SLOTS))[number]:
            load_up(jnp.int32(slot)).start()
        for column in range(0, width, DOWN_TILE):
            columns = slice(column, column + DOWN_TILE)
            part = jnp.dot(attended, outs[number, :, columns], preferred_element_type=F32)
            part = part.astype(BF16).astype(F32)
            if number == 0:
                residual[:, columns] = part + rows_ref[4:5, columns]
            else:
                residual[:, columns] += part
    for side, ref in enumerate((own_ref, other_ref)):
        for block in range(blocks):
            at = slice((side * blocks + block) * rows, (side * blocks + block + 1) * rows)
            value = ref[block].astype(F32) + residual[at]
            if side == 0:
                residual[at] = value
            renormed[at] = norm_rows(value, gain, shift).astype(BF16)

    def one_up(step, carry):
        load_up(step).wait()
        slot = lax.rem(step, SLOTS)
        for part in range(0, UP_TILE, 256):
            columns = pl.ds(pl.multiple_of(step * UP_TILE + part, 256), 256)
            raised = jnp.dot(
                renormed[...], ups[slot, :, part : part + 256], preferred_element_type=F32
            )
            raised = raised + b_up_ref[0:1, columns]
            hidden[:, columns] = jax.nn.gelu(raised, approximate=True).astype(BF16)
        ahead = step + SLOTS

        @pl.when(ahead < up_steps)
        def _():
            load_up(ahead).start()

        @pl.when((ahead >= up_steps) & (ahead < up_steps + down_steps))
        def _():
            load_down(ahead - up_steps).start()

        return carry

    lax.fori_loop(0, up_steps, one_up, 0)

    def one_down(step, carry):
        load_down(step).wait()
        columns = pl.ds(pl.multiple_of(step * DOWN_TILE, DOWN_TILE), DOWN_TILE)
        lowered = jnp.dot(
            hidden[...], downs[lax.rem(step, SLOTS)], preferred_element_type=F32
        )
        kept = residual[:half, columns] + lowered[:half] + rows_ref[5:6, columns]
        keep_ref[:, :, columns] = kept.reshape(blocks, rows, DOWN_TILE)
        send_ref[:, :, columns] = lowered[half:].astype(BF16).reshape(blocks, rows, DOWN_TILE)

        @pl.when(step + SLOTS < down_steps)
        def _():
            load_down(step + SLOTS).start()

        return carry

    lax.fori_loop(0, down_steps, one_down, 0)


def mlp(own, other, mine, theirs, rows_params, b_up, weights, after):
    blocks, rows, width = own.shape
    span = mine.shape[3]
    total = 2 * blocks * rows
    vmem = pl.BlockSpec(memory_space=pltpu.VMEM)
    hbm = pl.BlockSpec(memory_space=pl.ANY)
    w_mine, w_theirs, w_up, w_down = weights
    hidden = w_up.shape[1]
    return pl.pallas_call(
        functools.partial(mlp_kernel, len(after)),
        out_shape=(
            jax.ShapeDtypeStruct((blocks, rows, width), F32),
            jax.ShapeDtypeStruct((blocks, rows, width), BF16),
        ),
        in_specs=[vmem] * 6 + [hbm] * (4 + len(after)),
        out_specs=(vmem, vmem),
        scratch_shapes=[
            pltpu.VMEM((total, width), F32),
            pltpu.VMEM((total, width), BF16),
            pltpu.VMEM((total, hidden), BF16),
            pltpu.VMEM((2, span, width), BF16),
            pltpu.VMEM((SLOTS, width, UP_TILE), BF16),
            pltpu.VMEM((SLOTS, hidden, DOWN_TILE), BF16),
            pltpu.SemaphoreType.DMA((2,)),
            pltpu.SemaphoreType.DMA((SLOTS,)),
            pltpu.SemaphoreType.DMA((SLOTS,)),
        ],
        compiler_params=pltpu.CompilerParams(vmem_limit_bytes=46 * MIB),
        cost_estimate=pl.CostEstimate(
            flops=8 * total * width * (span + hidden),
            bytes_accessed=4 * width * (span + hidden),
            transcendentals=0,
        ),
        name="mlp",
    )(
        own, other, mine, theirs, rows_params, b_up, in_hbm(w_mine), w_theirs, in_hbm(w_up),
        in_hbm(w_down), *after,
    )


def add_kernel(n_after, keep_ref, came_ref, *refs):
    out_ref = refs[n_after]
    out_ref[...] = (keep_ref[...] + came_ref[...].astype(F32)).astype(BF16)


def add(keep, came, after):
    vmem = pl.BlockSpec(memory_space=pltpu.VMEM)
    return pl.pallas_call(
        functools.partial(add_kernel, len(after)),
        out_shape=jax.ShapeDtypeStruct(came.shape, BF16),
        in_specs=[vmem] * 2 + [pl.BlockSpec(memory_space=pl.ANY)] * len(after),
        out_specs=vmem,
        compiler_params=pltpu.CompilerParams(vmem_limit_bytes=8 * MIB),
        cost_estimate=SMALL_COST,
        name="add",
    )(keep, came, *after)


def swap(value):
    return lax.ppermute(value, "tensor", [(0, 1), (1, 0)])


def line_up_kernel(total, n_after, *refs):
    sources, out_ref, sems = refs[:total], refs[total + n_after], refs[-1]
    copies = [
        pltpu.make_async_copy(source, out_ref.at[number], sems.at[number])
        for number, source in enumerate(sources)
    ]
    for copy in copies:
        copy.start()
    for copy in copies:
        copy.wait()


def line_up(arrays, after, name):
    any_space = pl.BlockSpec(memory_space=pl.ANY)
    total = len(arrays)
    return pl.pallas_call(
        functools.partial(line_up_kernel, total, len(after)),
        out_shape=jax.ShapeDtypeStruct((total,) + arrays[0].shape, arrays[0].dtype),
        in_specs=[any_space] * (total + len(after)),
        out_specs=pl.BlockSpec(memory_space=pltpu.VMEM),
        scratch_shapes=[pltpu.SemaphoreType.DMA((total,))],
        compiler_params=pltpu.CompilerParams(vmem_limit_bytes=8 * MIB),
        cost_estimate=SMALL_COST,
        name=name,
    )(*arrays, *after)


def w_out_place(w_out):
    core = lax.axis_index("dp") & 1
    group = lax.axis_index("groups")
    return 2 * group + core, 2 * (1 - group) + core, w_out.shape[0] // 4


def piece_kernel(n_after, number_ref, w_ref, *refs):
    out_ref, sem = refs[n_after:]
    piece = out_ref.shape[0]
    rows = pl.ds(pl.multiple_of(number_ref[0] * piece, piece), piece)
    copy = pltpu.make_async_copy(w_ref.at[rows, :], out_ref, sem)
    copy.start()
    copy.wait()


def w_out_piece(w_out, after):
    number, _, piece = w_out_place(w_out)
    any_space = pl.BlockSpec(memory_space=pl.ANY)
    return pl.pallas_call(
        functools.partial(piece_kernel, len(after)),
        out_shape=jax.ShapeDtypeStruct((piece, w_out.shape[1]), BF16),
        in_specs=[pl.BlockSpec(memory_space=pltpu.SMEM)] + [any_space] * (1 + len(after)),
        out_specs=pl.BlockSpec(memory_space=pltpu.VMEM),
        scratch_shapes=[pltpu.SemaphoreType.DMA],
        compiler_params=pltpu.CompilerParams(vmem_limit_bytes=4 * MIB),
        cost_estimate=SMALL_COST,
        name="w_piece",
    )(number.astype(jnp.int32).reshape(1), in_hbm(w_out), *after)


def other_w_out(w_out, near, side, after):
    number, other, _ = w_out_place(w_out)
    dp_size = lax.axis_size("dp")
    both = line_up([near, side], after, "w_both")
    mate = lax.ppermute(both, "dp", [(d, d ^ 1) for d in range(dp_size)])
    spots = jnp.stack([number, other, number ^ 1, other ^ 1]).astype(jnp.int32)
    return join(spots, near, side, mate)


def attend_rows(projected):
    row_total, count_blocks, width = (projected.shape[0], projected.shape[1], projected.shape[3])
    head_count = width // HEAD_DIM
    queries = projected[:, :, 0].reshape(row_total, count_blocks, head_count, HEAD_DIM)
    key_rows = projected[:, :, 1].reshape(row_total, count_blocks, head_count, HEAD_DIM)
    values = projected[:, :, 2].astype(BF16).reshape(row_total, count_blocks, head_count, HEAD_DIM)
    scores = jnp.einsum(
        "qnhd,snhd->nhqs", queries, key_rows, precision=lax.Precision.HIGHEST
    ) * HEAD_DIM ** (-0.5)
    weights = jax.nn.softmax(scores, axis=-1).astype(BF16)
    attended = jnp.einsum("nhqs,snhd->qnhd", weights, values, preferred_element_type=F32)
    return attended.astype(BF16).reshape(row_total, count_blocks, width)


def encode_split(own, params):
    (pre_gain, pre_shift, w_qkv, b_qkv, w_out, b_out, mlp_gain, mlp_shift, w_up, b_up, w_down,
     b_down) = params
    block_rows = jnp.swapaxes(own, 0, 1)
    rows_dev = block_rows.shape[0]
    gathered = lax.all_gather(block_rows, "tensor", axis=0, tiled=True)
    normed = norm_rows(gathered.astype(F32), pre_gain, pre_shift).astype(BF16)
    attended = attend_rows(
        jnp.einsum("qnd,jde->qnje", normed, w_qkv, preferred_element_type=F32) + b_qkv[None, None]
    )
    partial_value = jnp.einsum("qne,ed->qnd", attended, w_out, preferred_element_type=F32)
    summed = lax.psum(partial_value.astype(BF16), "tensor").astype(F32)
    residual_all = gathered.astype(F32) + summed + b_out
    renormed = norm_rows(residual_all, mlp_gain, mlp_shift).astype(BF16)
    raised = jnp.einsum("qnd,df->qnf", renormed, w_up, preferred_element_type=F32) + b_up
    hidden = jax.nn.gelu(raised, approximate=True).astype(BF16)
    residual = lax.dynamic_slice_in_dim(
        residual_all, lax.axis_index("tensor") * rows_dev, rows_dev, 0
    )
    mlp_out = lax.psum_scatter(
        jnp.einsum("qnf,fd->qnd", hidden, w_down, preferred_element_type=F32).astype(BF16),
        "tensor", scatter_dimension=0, tiled=True,
    ).astype(F32)
    return jnp.swapaxes((residual + mlp_out + b_down).astype(BF16), 0, 1)


def per_device(paired, patches, kept_count, keep_list, *params):
    home = in_hbm(patches[0])
    keep_row = in_hbm(keep_list[0])
    kept_count = in_hbm(kept_count)
    dp_size = lax.axis_size("dp")
    device = lax.axis_index("dp").astype(jnp.int32).reshape(1)
    mates = [(d, d ^ 1) for d in range(dp_size)]
    pairs = [(d, d ^ 2) for d in range(dp_size)]
    nexts = [
        (d, d ^ 1 if d < 2 or d >= dp_size - 2 else ((d + 2) ^ 2) - 2) for d in range(dp_size)
    ]

    def to_mate(value):
        return lax.ppermute(value, "dp", mates)

    def to_pair(value):
        return lax.ppermute(value, "dp", pairs)

    def to_next(value):
        return lax.ppermute(value, "dp", nexts)

    mine, for_mate = pack(device, kept_count, keep_row, home)
    from_mate = to_mate(for_mate)
    table = make_plan(device, kept_count)
    short = table[AT_SHORT : AT_SHORT + 1].astype(F32)
    if paired:
        short = short + lax.ppermute(short, "groups", [(0, 1), (1, 0)])
    else:
        short = lax.pmax(short, "groups")
    short = short[0] > 0

    parts = tuple(zip(STARTS, CHUNKS))
    sends = [(AT_PAIR + at, size) for at, size in parts] + [(AT_NEXT + at, size) for at, size in parts]
    going = choose(table, sends, [mine, from_mate], "send")
    came_pair = [to_pair(value) for value in going[: len(parts)]]
    came_next = [to_next(value) for value in going[len(parts) :]]

    def deal_fast(chunk, after):
        came = [came_pair[min(part, chunk)] for part in range(len(parts))]
        came = came + [came_next[min(part, chunk)] for part in range(len(parts))]
        at, size = parts[chunk]
        sources = [mine, from_mate] + came
        return choose(table, [(AT_DEALT + at, size)], sources, "deal_%d" % chunk, after)[0]

    def deal_slow(chunk):
        chips = dp_size // 2
        (picked,) = choose(table, [(AT_SLOW_SEND, ROOM * chips)], [mine, from_mate], "deal_slow")
        picked = picked.reshape((chips, ROOM) + picked.shape[1:])
        spread = jnp.repeat(picked, 2, axis=0)
        arrived = lax.all_to_all(spread, "dp", split_axis=0, concat_axis=0, tiled=True)
        at, size = parts[chunk]
        return jnp.stack(
            [
                arrived[table[AT_SLOW_SOURCE + j], table[AT_SLOW_PLACE + j]]
                for j in range(at, at + size)
            ]
        )

    def deal(chunk, after=()):
        return lax.cond(short, lambda: deal_slow(chunk), lambda: deal_fast(chunk, after))

    if paired:
        (pre_gain, pre_shift, w_qkv, b_qkv, w_out, b_out, mlp_gain, mlp_shift, w_up, b_up, w_down,
         b_down) = params
        rows_params = jnp.stack([pre_gain, pre_shift, mlp_gain, mlp_shift, b_out, b_down])
        b_up = b_up.reshape(1, -1)
        w_near = swap(w_out_piece(w_out, [for_mate]))

        def start(own, after):
            other = swap(own)
            mine = attend(own, other, rows_params, w_qkv, b_qkv, after)
            return own, other, mine, swap(mine)

        def finish(state, after):
            keep, send = mlp(*state, rows_params, b_up, weights, after)
            return keep, swap(send)

        blocks_0 = deal(0)
        state_0 = start(blocks_0, [])
        w_sent = line_up([w_near], [blocks_0], "w_near")
        blocks_1 = deal(1, [w_sent])
        state_1 = start(blocks_1, [])
        w_side = lax.ppermute(w_sent, "groups", [(0, 1), (1, 0)])[0]
        w_theirs = other_w_out(w_out, w_near, w_side, [blocks_1])
        weights = (w_out, w_theirs, w_up, w_down)
        done_0 = finish(state_0, [state_1[2]])
        done_1 = finish(state_1, [done_0[0]])
        results, from_pair, from_next = [], [], []
        for done, beside in ((done_0, done_1[:1]), (done_1, ())):
            results.append(add(*done, list(beside) + from_pair[-1:] + from_next[-1:]))
            from_pair.append(to_pair(results[-1]))
            from_next.append(to_next(results[-1]))
    else:
        results = [encode_split(deal(chunk), params) for chunk in range(len(parts))]
        from_pair = [to_pair(value) for value in results]
        from_next = [to_next(value) for value in results]

    back = results + from_pair + from_next
    last = len(parts) - 1
    back = back + [
        back[place] if place + len(back) in LATE else to_mate(value)
        for place, value in enumerate(back)
    ]

    def home_slow():
        spread = lax.all_gather(jnp.concatenate(results), "dp", axis=0, tiled=True)
        places = table[AT_SLOW_HOME : AT_SLOW_HOME + 2 * PAGE_HALF]
        return (
            jnp.take(spread, places[:PAGE_HALF], axis=0),
            jnp.take(spread, places[PAGE_HALF:], axis=0),
        )

    found = lax.cond(short, home_slow, lambda: (mine, from_mate))
    slots = 2 * PAGE_HALF
    codes = jnp.where(
        short, table[AT_IN_ORDER : AT_IN_ORDER + slots], table[AT_HOME : AT_HOME + slots]
    )
    early = [results[0] if place in LATE else value for place, value in enumerate(back)]
    (gathered,) = choose(codes, [(0, slots)], early + list(found), "gather")
    late = [from_pair[last], from_next[last]]
    mates_late = to_mate(line_up(late, [gathered], "late"))
    late.append(mates_late.reshape((-1,) + mates_late.shape[2:]))
    return merge(device, kept_count, keep_row, codes, home, gathered, late)[None]


def solution(mesh):
    in_specs = (
        P(("groups", "dp"), "tensor", None, None),
        P("groups"),
        P(("groups", "dp"), None),
        P(),
        P(),
        P(None, None, "tensor"),
        P(None, "tensor"),
        P("tensor", None),
        P(),
        P(),
        P(),
        P(None, "tensor"),
        P("tensor"),
        P("tensor", None),
        P(),
    )
    out_specs = P(("groups", "dp"), "tensor", None, None)
    paired = mesh.shape["tensor"] == 2 and mesh.shape["groups"] == 2
    return jax.shard_map(
        functools.partial(per_device, paired), mesh=mesh, in_specs=in_specs, out_specs=out_specs,
        check_vma=False,
    )
```

```python
import functools

import jax
import jax.numpy as jnp
from jax import lax
from jax.experimental import pallas as pl
from jax.experimental.pallas import tpu as pltpu
from jax.sharding import PartitionSpec as P

HEAD_DIM = 112
CHUNKS = (3, 2)
STARTS = (0, 3)
ROOM = 5
PAGE_HALF = 8
GROUP_ROWS = 16
F32 = jnp.float32
BF16 = jnp.bfloat16
MIB = 1 << 20
SMALL_COST = pl.CostEstimate(flops=1000, bytes_accessed=1000, transcendentals=0)


def norm_rows(inputs, gain, shift):
    average = jnp.mean(inputs, axis=-1, keepdims=True)
    centred = inputs - average
    variance = jnp.mean(centred * centred, axis=-1, keepdims=True)
    return centred * lax.rsqrt(variance + 1e-06) * gain + shift


def pick_at(values, index):
    total = jnp.int32(0)
    for place, value in enumerate(values):
        total = total + jnp.where(index == place, value, 0)
    return total


def page_ends_of(count_ref, pages):
    ends = [jnp.int32(0)]
    for page in range(pages):
        ends.append(ends[-1] + count_ref[page])
    return ends


def chunk_of(slot):
    number, start = jnp.int32(0), jnp.int32(0)
    for chunk in range(1, len(CHUNKS)):
        number = jnp.where(slot >= STARTS[chunk], chunk, number)
        start = jnp.where(slot >= STARTS[chunk], STARTS[chunk], start)
    return number, slot - start


def line_plan(ends, chips, core):
    held = [(ends[2 * chip] + 1 - core) >> 1 for chip in range(chips + 1)]
    total = held[chips]
    wanted = [
        jnp.clip(held[i], jnp.maximum(total - ROOM * (chips - i), 0), jnp.minimum(total, ROOM * i))
        for i in range(chips + 1)
    ]
    below, above = list(wanted), list(wanted)
    for i in range(1, chips + 1):
        below[i] = jnp.minimum(below[i], below[i - 1] + ROOM)
    for i in range(chips - 1, -1, -1):
        above[i] = jnp.maximum(above[i], above[i + 1] - ROOM)
    dealt = [(low + high) >> 1 for low, high in zip(below, above)]
    short = jnp.int32(0)
    for cut in range(1, chips):
        right = held[cut] - dealt[cut]
        most_right = jnp.minimum(held[cut] - held[cut - 1], ROOM)
        most_left = jnp.minimum(held[cut + 1] - held[cut], ROOM)
        short = short + jnp.where((right > most_right) | (-right > most_left), 1, 0)
    return held, dealt, short


AT_PAIR = 0
AT_NEXT = AT_PAIR + ROOM
AT_DEALT = AT_NEXT + ROOM
AT_HOME = AT_DEALT + ROOM
AT_SHORT = AT_HOME + 2 * PAGE_HALF
AT_SLOW_SOURCE = AT_SHORT + 1
AT_SLOW_PLACE = AT_SLOW_SOURCE + ROOM
AT_SLOW_HOME = AT_SLOW_PLACE + ROOM
AT_IN_ORDER = AT_SLOW_HOME + 2 * PAGE_HALF
AT_SLOW_SEND = AT_IN_ORDER + 2 * PAGE_HALF


def plan_kernel(pages, device_ref, count_ref, table_ref):
    chips = pages // 2
    device = device_ref[0]
    core, chip = device & 1, device >> 1
    ends = page_ends_of(count_ref, pages)
    held, dealt, short = line_plan(ends, chips, core)
    held_mate, dealt_mate, short_mate = line_plan(ends, chips, 1 - core)
    table_ref[AT_SHORT] = jnp.where(short + short_mate > 0, 1, 0)
    falls, falls_mate = (
        [jnp.where(ranks[i] - ranks_dealt[i] > 2, 1, 0) for i in range(chips)]
        for ranks, ranks_dealt in ((held, dealt), (held_mate, dealt_mate))
    )

    low, high = pick_at(held, chip), pick_at(held, chip + 1)
    first, end = pick_at(dealt, chip), pick_at(dealt, chip + 1)
    falls_here = pick_at(falls, chip)
    own_start, own_end = pick_at(ends, device), pick_at(ends, device + 1)
    mate_start = pick_at(ends, device ^ 1)

    def turned(offset, falling):
        return jnp.where(falling > 0, ROOM - 1 - offset, offset)

    def local_code(rank):
        position = 2 * rank + core
        own = (position >= own_start) & (position < own_end)
        return jnp.where(own, (position - own_start) >> 1, 16 + ((position - mate_start) >> 1))

    def part_code(count, source):
        number, place = chunk_of(count)
        return (source + number) * 16 + place

    sides = len(CHUNKS)
    odd = chip & 1
    right_side, left_side = sides * odd, sides * (1 - odd)

    for slot in range(ROOM):
        rightwards, leftwards = local_code(high - 1 - slot), local_code(low + slot)
        table_ref[AT_PAIR + slot] = jnp.where(odd > 0, leftwards, rightwards)
        table_ref[AT_NEXT + slot] = jnp.where(odd > 0, rightwards, leftwards)
        offset = turned(jnp.int32(slot), falls_here)
        rank = first + offset
        code = jnp.where(rank < low, part_code(low - 1 - rank, 2 + left_side), local_code(rank))
        code = jnp.where(rank >= high, part_code(rank - high, 2 + right_side), code)
        table_ref[AT_DEALT + slot] = code
        node = jnp.int32(0)
        for place in range(1, chips):
            node = node + jnp.where(held[place] <= rank, 1, 0)
        table_ref[AT_SLOW_SOURCE + slot] = 2 * node + core
        table_ref[AT_SLOW_PLACE + slot] = offset
    for half, (ranks_dealt, turns) in enumerate(((dealt, falls), (dealt_mate, falls_mate))):
        lane = core ^ half
        here, there = pick_at(ranks_dealt, chip), pick_at(ranks_dealt, chip + 1)
        before = pick_at(ranks_dealt, chip - 1)
        turns_here, turns_right, turns_left = (pick_at(turns, chip + i) for i in (0, 1, -1))
        for slot in range(PAGE_HALF):
            rank = (own_start + ((own_start + lane) & 1) + 2 * slot - lane) >> 1
            at = half * PAGE_HALF + slot
            base = 3 * sides * half
            code = part_code(turned(rank - here, turns_here), base)
            right = part_code(turned(rank - there, turns_right), base + sides + right_side)
            left = part_code(turned(rank - before, turns_left), base + sides + left_side)
            code = jnp.where(rank >= there, right, code)
            table_ref[AT_HOME + at] = jnp.where(rank < here, left, code)
            node, start_there, turns_there = jnp.int32(0), jnp.int32(0), turns[0]
            for place in range(1, chips):
                beyond = ranks_dealt[place] <= rank
                node = node + jnp.where(beyond, 1, 0)
                start_there = jnp.where(beyond, ranks_dealt[place], start_there)
                turns_there = jnp.where(beyond, turns[place], turns_there)
            slow = (2 * node + lane) * ROOM + turned(rank - start_there, turns_there)
            table_ref[AT_SLOW_HOME + at] = jnp.clip(slow, 0, pages * ROOM - 1)
            table_ref[AT_IN_ORDER + at] = jnp.int32((6 * sides + half) * 16 + slot)
    for node in range(chips):
        for slot in range(ROOM):
            code = local_code(dealt[node] + slot)
            table_ref[AT_SLOW_SEND + node * ROOM + slot] = jnp.clip(code, 0, 31)


def make_plan(device, kept_count):
    pages = kept_count.shape[0]
    size = AT_SLOW_SEND + ROOM * (pages // 2)
    return pl.pallas_call(
        functools.partial(plan_kernel, pages),
        out_shape=jax.ShapeDtypeStruct((size,), jnp.int32),
        in_specs=[pl.BlockSpec(memory_space=pltpu.SMEM)] * 2,
        out_specs=pl.BlockSpec(memory_space=pltpu.SMEM),
        compiler_params=pltpu.CompilerParams(vmem_limit_bytes=MIB),
        cost_estimate=SMALL_COST,
        name="plan",
    )(device, kept_count)


def kept_blocks(device_ref, count_ref, keep_ref, pages):
    device = device_ref[0]
    start, count = jnp.int32(0), jnp.int32(0)
    for page in range(pages):
        start = start + jnp.where(page < device, count_ref[page], 0)
        count = count + jnp.where(page == device, count_ref[page], 0)
    blocks = []
    for half in range(2):
        offset = (start + device + half) & 1
        for slot in range(PAGE_HALF):
            index = 2 * slot + offset
            block = keep_ref[jnp.minimum(index, 2 * PAGE_HALF - 1)]
            blocks.append(jnp.where(index < count, block, -1))
    return blocks


def kept_blocks_once(device_ref, count_ref, keep_ref, pages, held):
    @pl.when(pl.program_id(0) == 0)
    def _():
        for slot, block in enumerate(kept_blocks(device_ref, count_ref, keep_ref, pages)):
            held[slot] = block

    return [held[slot] for slot in range(2 * PAGE_HALF)]


def pack_kernel(pages, device_ref, count_ref, keep_ref, home_ref, mine_ref, mate_ref, held):
    page_blocks, width = home_ref.shape[1], home_ref.shape[2]
    blocks = kept_blocks_once(device_ref, count_ref, keep_ref, pages, held)
    span = GROUP_ROWS * page_blocks
    row = lax.broadcasted_iota(jnp.int32, (GROUP_ROWS, span), 0)
    column = lax.broadcasted_iota(jnp.int32, (GROUP_ROWS, span), 1)
    chosen = jnp.concatenate(
        [jnp.where(column == row * page_blocks + block, 1.0, 0.0).astype(BF16) for block in blocks],
        axis=0,
    )
    packed = jnp.dot(
        chosen, home_ref[...].reshape(span, width), preferred_element_type=F32
    ).astype(BF16)
    half = PAGE_HALF * GROUP_ROWS
    mine_ref[...] = packed[:half].reshape(PAGE_HALF, GROUP_ROWS, width)
    mate_ref[...] = packed[half:].reshape(PAGE_HALF, GROUP_ROWS, width)


def pack(device, kept_count, keep_row, home):
    rows, page_blocks, width = home.shape
    shape = jax.ShapeDtypeStruct((PAGE_HALF, rows, width), BF16)
    place = pl.BlockSpec((PAGE_HALF, GROUP_ROWS, width), lambda step, *_: (0, step, 0))
    return pl.pallas_call(
        functools.partial(pack_kernel, kept_count.shape[0]),
        out_shape=(shape, shape),
        grid_spec=pltpu.PrefetchScalarGridSpec(
            num_scalar_prefetch=3,
            grid=(rows // GROUP_ROWS,),
            in_specs=[
                pl.BlockSpec((GROUP_ROWS, page_blocks, width), lambda step, *_: (step, 0, 0))
            ],
            out_specs=(place, place),
            scratch_shapes=[pltpu.SMEM((2 * PAGE_HALF,), jnp.int32)],
        ),
        compiler_params=pltpu.CompilerParams(vmem_limit_bytes=16 * MIB),
        name="pack",
    )(device, kept_count, keep_row, home)


LATE = (3, 5, 9, 11)


def merge_kernel(pages, device_ref, count_ref, keep_ref, code_ref, home_ref, found_ref, *refs):
    late, out_ref, held = refs[:-2], refs[-2], refs[-1]
    page_blocks, width = home_ref.shape[1], home_ref.shape[2]
    slots, size = 2 * PAGE_HALF, CHUNKS[-1]
    places = slots + size * len(LATE)

    @pl.when(pl.program_id(0) == 0)
    def _():
        blocks = kept_blocks(device_ref, count_ref, keep_ref, pages)
        spots = []
        for slot in range(slots):
            code = code_ref[slot]
            spot = jnp.int32(slot)
            for number, source in enumerate(LATE):
                spot = jnp.where(code >> 4 == source, slots + number * size + (code & 15), spot)
            spots.append(jnp.where(blocks[slot] >= 0, spot, -1))
        for place in range(places):
            block = jnp.int32(-1)
            for slot in range(slots) if place >= slots else (place,):
                block = jnp.where(spots[slot] == place, blocks[slot], block)
            held[place] = block

    span = GROUP_ROWS * page_blocks
    depth = places * GROUP_ROWS
    row = lax.broadcasted_iota(jnp.int32, (span, depth), 0)
    column = lax.broadcasted_iota(jnp.int32, (span, depth), 1)
    place_id = lax.broadcasted_iota(jnp.int32, (1, depth), 1) // GROUP_ROWS
    block_id = lax.broadcasted_iota(jnp.int32, (span, 1), 0) % page_blocks
    wanted = jnp.full((1, depth), -1, jnp.int32)
    kept = jnp.zeros((span, 1), jnp.int32)
    for place in range(places):
        block = held[place]
        wanted = jnp.where(place_id == place, block, wanted)
        kept = kept + jnp.where(block_id == block, 1, 0)
    chosen = jnp.where(
        (row // page_blocks == column % GROUP_ROWS) & (row % page_blocks == wanted), 1.0, 0.0
    ).astype(BF16)
    source = jnp.concatenate(
        [ref[...].reshape(-1, width) for ref in (found_ref,) + tuple(late)], axis=0
    )
    landed = jnp.dot(chosen, source, preferred_element_type=F32)
    home = home_ref[...].reshape(span, width).astype(F32)
    merged = jnp.where(kept > 0, landed, home).astype(BF16)
    out_ref[...] = merged.reshape(GROUP_ROWS, page_blocks, width)


def merge(device, kept_count, keep_row, codes, home, found, late):
    rows, page_blocks, width = home.shape
    page = pl.BlockSpec((GROUP_ROWS, page_blocks, width), lambda step, *_: (step, 0, 0))

    def some(array):
        return pl.BlockSpec((array.shape[0], GROUP_ROWS, width), lambda step, *_: (0, step, 0))

    return pl.pallas_call(
        functools.partial(merge_kernel, kept_count.shape[0]),
        out_shape=jax.ShapeDtypeStruct(home.shape, BF16),
        grid_spec=pltpu.PrefetchScalarGridSpec(
            num_scalar_prefetch=4,
            grid=(rows // GROUP_ROWS,),
            in_specs=[page, some(found)] + [some(array) for array in late],
            out_specs=page,
            scratch_shapes=[
                pltpu.SMEM((found.shape[0] + CHUNKS[-1] * len(LATE),), jnp.int32)
            ],
        ),
        compiler_params=pltpu.CompilerParams(vmem_limit_bytes=20 * MIB),
        cost_estimate=SMALL_COST,
        name="merge",
    )(device, kept_count, keep_row, codes, home, found, *late)


def start_copies(sources, wanted):
    for code, target, sem in wanted:
        which, place = code >> 4, code & 15
        for index, source in enumerate(sources):
            if len(sources) == 1:
                here = which > -(1 << 20)
            elif index == 0:
                here = which <= 0
            elif index == len(sources) - 1:
                here = which >= index
            else:
                here = which == index

            @pl.when(here)
            def _(source=source, place=place, target=target, sem=sem):
                inside = jnp.minimum(place, source.shape[0] - 1)
                pltpu.make_async_copy(source.at[inside], target, sem).start()


def choose_kernel(parts, n_sources, table_ref, *refs):
    sources, outs, sems = refs[:n_sources], refs[-1 - len(parts) : -1], refs[-1]
    targets = [
        (at + slot, out_ref.at[slot])
        for (at, total), out_ref in zip(parts, outs)
        for slot in range(total)
    ]
    start_copies(
        sources,
        [(table_ref[at], target, sems.at[number]) for number, (at, target) in enumerate(targets)],
    )
    for number, (_, target) in enumerate(targets):
        pltpu.make_async_copy(sources[0].at[0], target, sems.at[number]).wait()


def choose(table, parts, sources, name, after=()):
    block = sources[0].shape[1:]
    total = sum(count for _, count in parts)
    return pl.pallas_call(
        functools.partial(choose_kernel, parts, len(sources)),
        out_shape=tuple(jax.ShapeDtypeStruct((count,) + block, BF16) for _, count in parts),
        in_specs=[pl.BlockSpec(memory_space=pltpu.SMEM)]
        + [pl.BlockSpec(memory_space=pl.ANY)] * (len(sources) + len(after)),
        out_specs=tuple(pl.BlockSpec(memory_space=pltpu.VMEM) for _ in parts),
        scratch_shapes=[pltpu.SemaphoreType.DMA((total,))],
        compiler_params=pltpu.CompilerParams(vmem_limit_bytes=8 * MIB),
        cost_estimate=SMALL_COST,
        name=name,
    )(table, *sources, *after)


def join_kernel(spots_ref, near, side, mate, out_ref, sems):
    piece = near.shape[0]
    sources = (near, side, mate.at[0], mate.at[1])
    copies = []
    for number, source in enumerate(sources):
        place = pl.ds(pl.multiple_of(spots_ref[number] * piece, piece), piece)
        copies.append(pltpu.make_async_copy(source, out_ref.at[place, :], sems.at[number]))
    for copy in copies:
        copy.start()
    for copy in copies:
        copy.wait()


def join(spots, near, side, mate):
    shape = (4 * near.shape[0], near.shape[1])
    any_space = pl.BlockSpec(memory_space=pl.ANY)
    return pl.pallas_call(
        join_kernel,
        out_shape=jax.ShapeDtypeStruct(shape, BF16),
        in_specs=[pl.BlockSpec(memory_space=pltpu.SMEM)] + [any_space] * 3,
        out_specs=pl.BlockSpec(memory_space=pltpu.VMEM),
        scratch_shapes=[pltpu.SemaphoreType.DMA((4,))],
        compiler_params=pltpu.CompilerParams(vmem_limit_bytes=8 * MIB),
        name="join",
    )(spots, near, side, mate)


def in_hbm(array):
    return pltpu.with_memory_space_constraint(array, pltpu.HBM)


def split_store(value, high_ref, low_ref):
    high = value.astype(BF16)
    high_ref[...] = high
    low_ref[...] = (value - high.astype(F32)).astype(BF16)


def attend_kernel(n_after, own_ref, other_ref, rows_ref, b_ref, w_ref, *refs):
    (out_ref, held, normed, q_high, q_low, k_high, k_low, values, scores, sems) = refs[n_after:]
    blocks, rows, width = own_ref.shape
    span = held.shape[2]
    loads = [pltpu.make_async_copy(w_ref.at[j], held.at[j], sems.at[j]) for j in range(3)]
    for load in loads:
        load.start()
    gain, shift = rows_ref[0:1, :], rows_ref[1:2, :]
    for half, ref in enumerate((own_ref, other_ref)):
        for block in range(blocks):
            at = (half * blocks + block) * rows
            normed[at : at + rows] = norm_rows(ref[block].astype(F32), gain, shift).astype(BF16)

    def project(j):
        loads[j].wait()
        product = jnp.dot(normed[...], held[j], preferred_element_type=F32)
        return product + b_ref[j : j + 1, :]

    split_store(project(0) * HEAD_DIM ** (-0.5), q_high, q_low)
    split_store(project(1), k_high, k_low)
    values[...] = project(2).astype(BF16)
    tiles = span // 128
    heads = span // HEAD_DIM
    size = 2 * rows
    lane = lax.broadcasted_iota(jnp.int32, (1, 256), 1)

    def window(head):
        tile = min(head * HEAD_DIM // 128, tiles - 2)
        first = head * HEAD_DIM - tile * 128
        inside = (lane >= first) & (lane < first + HEAD_DIM)
        return tile, slice(tile * 128, tile * 128 + 256), inside

    def one_block(block, carry):
        near = pl.ds(pl.multiple_of(block * rows, rows), rows)
        far = pl.ds(pl.multiple_of((blocks + block) * rows, rows), rows)

        def both(ref, columns):
            return jnp.concatenate([ref[near, columns], ref[far, columns]], axis=0)

        def times(left, right):
            return lax.dot_general(
                left, right, (((1,), (1,)), ((), ())), preferred_element_type=F32
            )

        for head in range(heads):
            _, columns, inside = window(head)
            none = jnp.zeros((), BF16)
            qh = jnp.where(inside, both(q_high, columns), none)
            ql = jnp.where(inside, both(q_low, columns), none)
            kh, kl = both(k_high, columns), both(k_low, columns)
            scores[head * size : (head + 1) * size, :] = (
                times(qh, kh) + times(qh, kl) + times(ql, kh)
            )
        value = scores[...]
        value = jnp.exp(value - jnp.max(value, axis=-1, keepdims=True))
        weights = (value * (1.0 / jnp.sum(value, axis=-1, keepdims=True))).astype(BF16)
        sums = [None] * tiles
        for head in range(heads):
            tile, columns, inside = window(head)
            mixed = jnp.dot(
                weights[head * size : (head + 1) * size, :], both(values, columns),
                preferred_element_type=F32,
            )
            mixed = jnp.where(inside, mixed, 0.0)
            for part in range(2):
                piece = mixed[:, part * 128 : part * 128 + 128]
                old = sums[tile + part]
                sums[tile + part] = piece if old is None else old + piece
        result = jnp.concatenate(sums, axis=1).astype(BF16)
        out_ref[0, block] = result[:rows]
        out_ref[1, block] = result[rows:]
        return carry

    lax.fori_loop(0, blocks, one_block, 0)


def attend(own, other, rows_params, w_qkv, b_qkv, after=()):
    blocks, rows, width = own.shape
    span = w_qkv.shape[2]
    total = 2 * blocks * rows
    vmem = pl.BlockSpec(memory_space=pltpu.VMEM)
    return pl.pallas_call(
        functools.partial(attend_kernel, len(after)),
        out_shape=jax.ShapeDtypeStruct((2, blocks, rows, span), BF16),
        in_specs=[vmem] * 4 + [pl.BlockSpec(memory_space=pl.ANY)] * (1 + len(after)),
        out_specs=vmem,
        scratch_shapes=[pltpu.VMEM((3, width, span), BF16), pltpu.VMEM((total, width), BF16)]
        + [pltpu.VMEM((total, span), BF16)] * 5
        + [
            pltpu.VMEM((2 * rows * (span // HEAD_DIM), 2 * rows), F32),
            pltpu.SemaphoreType.DMA((3,)),
        ],
        compiler_params=pltpu.CompilerParams(vmem_limit_bytes=28 * MIB),
        cost_estimate=pl.CostEstimate(
            flops=24 * total * width * span, bytes_accessed=6 * width * span, transcendentals=0
        ),
        name="attend",
    )(own, other, rows_params, b_qkv, in_hbm(w_qkv), *after)


def project_kernel(n_after, attended_ref, w_ref, *refs):
    out_ref, held, sems = refs[n_after:]
    sides, blocks, rows, span = attended_ref.shape
    width = held.shape[1]
    half = span // 2
    loads = [
        pltpu.make_async_copy(
            w_ref.at[pl.ds(part * half, half), :], held.at[pl.ds(part * half, half), :], sems.at[part]
        )
        for part in range(2)
    ]
    for load in loads:
        load.start()
    for load in loads:
        load.wait()
    attended = attended_ref[...].reshape(sides * blocks * rows, span)
    for column in range(0, width, 256):
        columns = slice(column, column + 256)
        part = jnp.dot(attended, held[:, columns], preferred_element_type=F32)
        out_ref[:, :, :, columns] = part.astype(BF16).reshape(sides, blocks, rows, 256)


def project(attended, w_out, after=()):
    sides, blocks, rows, span = attended.shape
    width = w_out.shape[1]
    vmem = pl.BlockSpec(memory_space=pltpu.VMEM)
    return pl.pallas_call(
        functools.partial(project_kernel, len(after)),
        out_shape=jax.ShapeDtypeStruct((sides, blocks, rows, width), BF16),
        in_specs=[vmem] + [pl.BlockSpec(memory_space=pl.ANY)] * (1 + len(after)),
        out_specs=vmem,
        scratch_shapes=[pltpu.VMEM((span, width), BF16), pltpu.SemaphoreType.DMA((2,))],
        compiler_params=pltpu.CompilerParams(vmem_limit_bytes=16 * MIB),
        cost_estimate=SMALL_COST,
        name="project",
    )(attended, in_hbm(w_out), *after)


UP_TILE = 768
DOWN_TILE = 256
SLOTS = 4


def mlp_kernel(n_after, given, own_ref, other_ref, mine_ref, theirs_ref, rows_ref, b_up_ref, w_mine, w_theirs,
               w_up, w_down, *refs):
    (keep_ref, send_ref, residual, renormed, hidden, outs, ups, downs, out_sems, up_sems,
     down_sems) = refs[n_after:]
    blocks, rows, width = own_ref.shape
    half = blocks * rows
    span = outs.shape[1]
    up_steps, down_steps = w_up.shape[1] // UP_TILE, width // DOWN_TILE

    def load_up(step):
        columns = pl.ds(pl.multiple_of(step * UP_TILE, UP_TILE), UP_TILE)
        slot = lax.rem(step, SLOTS)
        return pltpu.make_async_copy(w_up.at[:, columns], ups.at[slot], up_sems.at[slot])

    def load_down(step):
        columns = pl.ds(pl.multiple_of(step * DOWN_TILE, DOWN_TILE), DOWN_TILE)
        slot = lax.rem(step, SLOTS)
        return pltpu.make_async_copy(w_down.at[:, columns], downs.at[slot], down_sems.at[slot])

    out_loads = [
        pltpu.make_async_copy(source, outs.at[number], out_sems.at[number])
        for number, source in enumerate((w_mine, w_theirs))
    ]
    for load in out_loads[given:]:
        load.start()
    load_up(jnp.int32(0)).start()
    gain, shift = rows_ref[2:3, :], rows_ref[3:4, :]
    mine = mine_ref[...].reshape(2 * half, mine_ref.shape[3])
    theirs = jnp.concatenate(
        [theirs_ref[1].reshape(half, span), theirs_ref[0].reshape(half, span)], axis=0
    )
    for number, attended in enumerate((mine, theirs)):
        if number >= given:
            out_loads[number].wait()
        for slot in (range(1, 3), range(3, SLOTS))[number]:
            load_up(jnp.int32(slot)).start()
        for column in range(0, width, DOWN_TILE):
            columns = slice(column, column + DOWN_TILE)
            if number < given:
                part = attended[:, columns].astype(F32)
            else:
                part = jnp.dot(attended, outs[number, :, columns], preferred_element_type=F32)
                part = part.astype(BF16).astype(F32)
            if number == 0:
                residual[:, columns] = part + rows_ref[4:5, columns]
            else:
                residual[:, columns] += part
    for side, ref in enumerate((own_ref, other_ref)):
        for block in range(blocks):
            at = slice((side * blocks + block) * rows, (side * blocks + block + 1) * rows)
            value = ref[block].astype(F32) + residual[at]
            if side == 0:
                residual[at] = value
            renormed[at] = norm_rows(value, gain, shift).astype(BF16)

    def one_up(step, carry):
        load_up(step).wait()
        slot = lax.rem(step, SLOTS)
        for part in range(0, UP_TILE, 256):
            columns = pl.ds(pl.multiple_of(step * UP_TILE + part, 256), 256)
            raised = jnp.dot(
                renormed[...], ups[slot, :, part : part + 256], preferred_element_type=F32
            )
            raised = raised + b_up_ref[0:1, columns]
            hidden[:, columns] = jax.nn.gelu(raised, approximate=True).astype(BF16)
        ahead = step + SLOTS

        @pl.when(ahead < up_steps)
        def _():
            load_up(ahead).start()

        @pl.when((ahead >= up_steps) & (ahead < up_steps + down_steps))
        def _():
            load_down(ahead - up_steps).start()

        return carry

    lax.fori_loop(0, up_steps, one_up, 0)

    def one_down(step, carry):
        load_down(step).wait()
        columns = pl.ds(pl.multiple_of(step * DOWN_TILE, DOWN_TILE), DOWN_TILE)
        lowered = jnp.dot(
            hidden[...], downs[lax.rem(step, SLOTS)], preferred_element_type=F32
        )
        kept = residual[:half, columns] + lowered[:half] + rows_ref[5:6, columns]
        keep_ref[:, :, columns] = kept.reshape(blocks, rows, DOWN_TILE)
        send_ref[:, :, columns] = lowered[half:].astype(BF16).reshape(blocks, rows, DOWN_TILE)

        @pl.when(step + SLOTS < down_steps)
        def _():
            load_down(step + SLOTS).start()

        return carry

    lax.fori_loop(0, down_steps, one_down, 0)


def mlp(own, other, mine, theirs, rows_params, b_up, weights, after):
    blocks, rows, width = own.shape
    span = theirs.shape[3]
    given = int(mine.shape[3] != span)
    total = 2 * blocks * rows
    vmem = pl.BlockSpec(memory_space=pltpu.VMEM)
    hbm = pl.BlockSpec(memory_space=pl.ANY)
    w_mine, w_theirs, w_up, w_down = weights
    hidden = w_up.shape[1]
    return pl.pallas_call(
        functools.partial(mlp_kernel, len(after), given),
        out_shape=(
            jax.ShapeDtypeStruct((blocks, rows, width), F32),
            jax.ShapeDtypeStruct((blocks, rows, width), BF16),
        ),
        in_specs=[vmem] * 6 + [hbm] * (4 + len(after)),
        out_specs=(vmem, vmem),
        scratch_shapes=[
            pltpu.VMEM((total, width), F32),
            pltpu.VMEM((total, width), BF16),
            pltpu.VMEM((total, hidden), BF16),
            pltpu.VMEM((2, span, width), BF16),
            pltpu.VMEM((SLOTS, width, UP_TILE), BF16),
            pltpu.VMEM((SLOTS, hidden, DOWN_TILE), BF16),
            pltpu.SemaphoreType.DMA((2,)),
            pltpu.SemaphoreType.DMA((SLOTS,)),
            pltpu.SemaphoreType.DMA((SLOTS,)),
        ],
        compiler_params=pltpu.CompilerParams(vmem_limit_bytes=46 * MIB),
        cost_estimate=pl.CostEstimate(
            flops=8 * total * width * (span + hidden),
            bytes_accessed=4 * width * (span + hidden),
            transcendentals=0,
        ),
        name="mlp",
    )(
        own, other, mine, theirs, rows_params, b_up, in_hbm(w_mine), w_theirs, in_hbm(w_up),
        in_hbm(w_down), *after,
    )


def add_kernel(n_after, keep_ref, came_ref, *refs):
    out_ref = refs[n_after]
    out_ref[...] = (keep_ref[...] + came_ref[...].astype(F32)).astype(BF16)


def add(keep, came, after):
    vmem = pl.BlockSpec(memory_space=pltpu.VMEM)
    return pl.pallas_call(
        functools.partial(add_kernel, len(after)),
        out_shape=jax.ShapeDtypeStruct(came.shape, BF16),
        in_specs=[vmem] * 2 + [pl.BlockSpec(memory_space=pl.ANY)] * len(after),
        out_specs=vmem,
        compiler_params=pltpu.CompilerParams(vmem_limit_bytes=8 * MIB),
        cost_estimate=SMALL_COST,
        name="add",
    )(keep, came, *after)


def swap(value):
    return lax.ppermute(value, "tensor", [(0, 1), (1, 0)])


def line_up_kernel(total, n_after, *refs):
    sources, out_ref, sems = refs[:total], refs[total + n_after], refs[-1]
    copies = [
        pltpu.make_async_copy(source, out_ref.at[number], sems.at[number])
        for number, source in enumerate(sources)
    ]
    for copy in copies:
        copy.start()
    for copy in copies:
        copy.wait()


def line_up(arrays, after, name):
    any_space = pl.BlockSpec(memory_space=pl.ANY)
    total = len(arrays)
    return pl.pallas_call(
        functools.partial(line_up_kernel, total, len(after)),
        out_shape=jax.ShapeDtypeStruct((total,) + arrays[0].shape, arrays[0].dtype),
        in_specs=[any_space] * (total + len(after)),
        out_specs=pl.BlockSpec(memory_space=pltpu.VMEM),
        scratch_shapes=[pltpu.SemaphoreType.DMA((total,))],
        compiler_params=pltpu.CompilerParams(vmem_limit_bytes=8 * MIB),
        cost_estimate=SMALL_COST,
        name=name,
    )(*arrays, *after)


def w_out_place(w_out):
    core = lax.axis_index("dp") & 1
    group = lax.axis_index("groups")
    return 2 * group + core, 2 * (1 - group) + core, w_out.shape[0] // 4


def piece_kernel(n_after, number_ref, w_ref, *refs):
    out_ref, sem = refs[n_after:]
    piece = out_ref.shape[0]
    rows = pl.ds(pl.multiple_of(number_ref[0] * piece, piece), piece)
    copy = pltpu.make_async_copy(w_ref.at[rows, :], out_ref, sem)
    copy.start()
    copy.wait()


def w_out_piece(w_out, after):
    number, _, piece = w_out_place(w_out)
    any_space = pl.BlockSpec(memory_space=pl.ANY)
    return pl.pallas_call(
        functools.partial(piece_kernel, len(after)),
        out_shape=jax.ShapeDtypeStruct((piece, w_out.shape[1]), BF16),
        in_specs=[pl.BlockSpec(memory_space=pltpu.SMEM)] + [any_space] * (1 + len(after)),
        out_specs=pl.BlockSpec(memory_space=pltpu.VMEM),
        scratch_shapes=[pltpu.SemaphoreType.DMA],
        compiler_params=pltpu.CompilerParams(vmem_limit_bytes=4 * MIB),
        cost_estimate=SMALL_COST,
        name="w_piece",
    )(number.astype(jnp.int32).reshape(1), in_hbm(w_out), *after)


def other_w_out(w_out, near, side, after):
    number, other, _ = w_out_place(w_out)
    dp_size = lax.axis_size("dp")
    both = line_up([near, side], after, "w_both")
    mate = lax.ppermute(both, "dp", [(d, d ^ 1) for d in range(dp_size)])
    spots = jnp.stack([number, other, number ^ 1, other ^ 1]).astype(jnp.int32)
    return join(spots, near, side, mate)


def attend_rows(projected):
    row_total, count_blocks, width = (projected.shape[0], projected.shape[1], projected.shape[3])
    head_count = width // HEAD_DIM
    queries = projected[:, :, 0].reshape(row_total, count_blocks, head_count, HEAD_DIM)
    key_rows = projected[:, :, 1].reshape(row_total, count_blocks, head_count, HEAD_DIM)
    values = projected[:, :, 2].astype(BF16).reshape(row_total, count_blocks, head_count, HEAD_DIM)
    scores = jnp.einsum(
        "qnhd,snhd->nhqs", queries, key_rows, precision=lax.Precision.HIGHEST
    ) * HEAD_DIM ** (-0.5)
    weights = jax.nn.softmax(scores, axis=-1).astype(BF16)
    attended = jnp.einsum("nhqs,snhd->qnhd", weights, values, preferred_element_type=F32)
    return attended.astype(BF16).reshape(row_total, count_blocks, width)


def encode_split(own, params):
    (pre_gain, pre_shift, w_qkv, b_qkv, w_out, b_out, mlp_gain, mlp_shift, w_up, b_up, w_down,
     b_down) = params
    block_rows = jnp.swapaxes(own, 0, 1)
    rows_dev = block_rows.shape[0]
    gathered = lax.all_gather(block_rows, "tensor", axis=0, tiled=True)
    normed = norm_rows(gathered.astype(F32), pre_gain, pre_shift).astype(BF16)
    attended = attend_rows(
        jnp.einsum("qnd,jde->qnje", normed, w_qkv, preferred_element_type=F32) + b_qkv[None, None]
    )
    partial_value = jnp.einsum("qne,ed->qnd", attended, w_out, preferred_element_type=F32)
    summed = lax.psum(partial_value.astype(BF16), "tensor").astype(F32)
    residual_all = gathered.astype(F32) + summed + b_out
    renormed = norm_rows(residual_all, mlp_gain, mlp_shift).astype(BF16)
    raised = jnp.einsum("qnd,df->qnf", renormed, w_up, preferred_element_type=F32) + b_up
    hidden = jax.nn.gelu(raised, approximate=True).astype(BF16)
    residual = lax.dynamic_slice_in_dim(
        residual_all, lax.axis_index("tensor") * rows_dev, rows_dev, 0
    )
    mlp_out = lax.psum_scatter(
        jnp.einsum("qnf,fd->qnd", hidden, w_down, preferred_element_type=F32).astype(BF16),
        "tensor", scatter_dimension=0, tiled=True,
    ).astype(F32)
    return jnp.swapaxes((residual + mlp_out + b_down).astype(BF16), 0, 1)


def per_device(paired, patches, kept_count, keep_list, *params):
    home = in_hbm(patches[0])
    keep_row = in_hbm(keep_list[0])
    kept_count = in_hbm(kept_count)
    dp_size = lax.axis_size("dp")
    device = lax.axis_index("dp").astype(jnp.int32).reshape(1)
    mates = [(d, d ^ 1) for d in range(dp_size)]
    pairs = [(d, d ^ 2) for d in range(dp_size)]
    nexts = [
        (d, d ^ 1 if d < 2 or d >= dp_size - 2 else ((d + 2) ^ 2) - 2) for d in range(dp_size)
    ]

    def to_mate(value):
        return lax.ppermute(value, "dp", mates)

    def to_pair(value):
        return lax.ppermute(value, "dp", pairs)

    def to_next(value):
        return lax.ppermute(value, "dp", nexts)

    mine, for_mate = pack(device, kept_count, keep_row, home)
    from_mate = to_mate(for_mate)
    table = make_plan(device, kept_count)
    short = table[AT_SHORT : AT_SHORT + 1].astype(F32)
    if paired:
        short = short + lax.ppermute(short, "groups", [(0, 1), (1, 0)])
    else:
        short = lax.pmax(short, "groups")
    flag = short
    short = flag[0] > 0

    parts = tuple(zip(STARTS, CHUNKS))
    sends = [(AT_PAIR + at, size) for at, size in parts] + [(AT_NEXT + at, size) for at, size in parts]
    going = choose(table, sends, [mine, from_mate], "send")
    came_pair = [to_pair(value) for value in going[: len(parts)]]
    came_next = [to_next(value) for value in going[len(parts) :]]

    def deal_fast(chunk, after):
        came = [came_pair[min(part, chunk)] for part in range(len(parts))]
        came = came + [came_next[min(part, chunk)] for part in range(len(parts))]
        at, size = parts[chunk]
        sources = [mine, from_mate] + came
        return choose(table, [(AT_DEALT + at, size)], sources, "deal_%d" % chunk, after)[0]

    def deal_slow(chunk):
        chips = dp_size // 2
        (picked,) = choose(table, [(AT_SLOW_SEND, ROOM * chips)], [mine, from_mate], "deal_slow")
        picked = picked.reshape((chips, ROOM) + picked.shape[1:])
        spread = jnp.repeat(picked, 2, axis=0)
        arrived = lax.all_to_all(spread, "dp", split_axis=0, concat_axis=0, tiled=True)
        at, size = parts[chunk]
        return jnp.stack(
            [
                arrived[table[AT_SLOW_SOURCE + j], table[AT_SLOW_PLACE + j]]
                for j in range(at, at + size)
            ]
        )

    def deal(chunk, after=()):
        return lax.cond(short, lambda: deal_slow(chunk), lambda: deal_fast(chunk, after))

    if paired:
        (pre_gain, pre_shift, w_qkv, b_qkv, w_out, b_out, mlp_gain, mlp_shift, w_up, b_up, w_down,
         b_down) = params
        rows_params = jnp.stack([pre_gain, pre_shift, mlp_gain, mlp_shift, b_out, b_down])
        b_up = b_up.reshape(1, -1)
        w_near = swap(w_out_piece(w_out, [for_mate]))

        def start(own, after):
            other = swap(own)
            mine = attend(own, other, rows_params, w_qkv, b_qkv, after)
            return own, other, mine, swap(mine)

        def finish(state, after):
            keep, send = mlp(*state, rows_params, b_up, weights, after)
            return keep, swap(send)

        blocks_0 = deal(0)
        state_0 = start(blocks_0, [])
        w_sent = line_up([w_near], [flag], "w_near")
        blocks_1 = deal(1, [w_sent])
        state_1 = start(blocks_1, [])
        w_side = lax.ppermute(w_sent, "groups", [(0, 1), (1, 0)])[0]
        w_theirs = other_w_out(w_out, w_near, w_side, [blocks_1])
        weights = (w_out, w_theirs, w_up, w_down)
        own, other, mine_0, theirs = state_0
        state_0 = own, other, project(mine_0, w_out, [state_1[2]]), theirs
        done_0 = finish(state_0, [state_1[2]])
        done_1 = finish(state_1, [done_0[0]])
        results, from_pair, from_next = [], [], []
        for done, beside in ((done_0, done_1[:1]), (done_1, ())):
            results.append(add(*done, list(beside) + from_pair[-1:] + from_next[-1:]))
            from_pair.append(to_pair(results[-1]))
            from_next.append(to_next(results[-1]))
    else:
        results = [encode_split(deal(chunk), params) for chunk in range(len(parts))]
        from_pair = [to_pair(value) for value in results]
        from_next = [to_next(value) for value in results]

    back = results + from_pair + from_next
    last = len(parts) - 1
    back = back + [
        back[place] if place + len(back) in LATE else to_mate(value)
        for place, value in enumerate(back)
    ]

    def home_slow():
        spread = lax.all_gather(jnp.concatenate(results), "dp", axis=0, tiled=True)
        places = table[AT_SLOW_HOME : AT_SLOW_HOME + 2 * PAGE_HALF]
        return (
            jnp.take(spread, places[:PAGE_HALF], axis=0),
            jnp.take(spread, places[PAGE_HALF:], axis=0),
        )

    found = lax.cond(short, home_slow, lambda: (mine, from_mate))
    slots = 2 * PAGE_HALF
    codes = jnp.where(
        short, table[AT_IN_ORDER : AT_IN_ORDER + slots], table[AT_HOME : AT_HOME + slots]
    )
    early = [results[0] if place in LATE else value for place, value in enumerate(back)]
    (gathered,) = choose(codes, [(0, slots)], early + list(found), "gather")
    late = [from_pair[last], from_next[last]]
    mates_late = to_mate(line_up(late, [gathered], "late"))
    late.append(mates_late.reshape((-1,) + mates_late.shape[2:]))
    return merge(device, kept_count, keep_row, codes, home, gathered, late)[None]


def solution(mesh):
    in_specs = (
        P(("groups", "dp"), "tensor", None, None),
        P("groups"),
        P(("groups", "dp"), None),
        P(),
        P(),
        P(None, None, "tensor"),
        P(None, "tensor"),
        P("tensor", None),
        P(),
        P(),
        P(),
        P(None, "tensor"),
        P("tensor"),
        P("tensor", None),
        P(),
    )
    out_specs = P(("groups", "dp"), "tensor", None, None)
    paired = mesh.shape["tensor"] == 2 and mesh.shape["groups"] == 2
    return jax.shard_map(
        functools.partial(per_device, paired), mesh=mesh, in_specs=in_specs, out_specs=out_specs,
        check_vma=False,
    )
```

```python
import functools

import jax
import jax.numpy as jnp
from jax import lax
from jax.experimental import pallas as pl
from jax.experimental.pallas import tpu as pltpu
from jax.sharding import PartitionSpec as P

HEAD_DIM = 112
CHUNKS = (3, 2)
STARTS = (0, 3)
ROOM = 5
PAGE_HALF = 8
GROUP_ROWS = 16
F32 = jnp.float32
BF16 = jnp.bfloat16
MIB = 1 << 20
SMALL_COST = pl.CostEstimate(flops=1000, bytes_accessed=1000, transcendentals=0)


def norm_rows(inputs, gain, shift):
    average = jnp.mean(inputs, axis=-1, keepdims=True)
    centred = inputs - average
    variance = jnp.mean(centred * centred, axis=-1, keepdims=True)
    return centred * lax.rsqrt(variance + 1e-06) * gain + shift


def pick_at(values, index):
    total = jnp.int32(0)
    for place, value in enumerate(values):
        total = total + jnp.where(index == place, value, 0)
    return total


def page_ends_of(count_ref, pages):
    ends = [jnp.int32(0)]
    for page in range(pages):
        ends.append(ends[-1] + count_ref[page])
    return ends


def chunk_of(slot):
    number, start = jnp.int32(0), jnp.int32(0)
    for chunk in range(1, len(CHUNKS)):
        number = jnp.where(slot >= STARTS[chunk], chunk, number)
        start = jnp.where(slot >= STARTS[chunk], STARTS[chunk], start)
    return number, slot - start


def line_plan(ends, chips, core):
    held = [(ends[2 * chip] + 1 - core) >> 1 for chip in range(chips + 1)]
    total = held[chips]
    wanted = [
        jnp.clip(held[i], jnp.maximum(total - ROOM * (chips - i), 0), jnp.minimum(total, ROOM * i))
        for i in range(chips + 1)
    ]
    below, above = list(wanted), list(wanted)
    for i in range(1, chips + 1):
        below[i] = jnp.minimum(below[i], below[i - 1] + ROOM)
    for i in range(chips - 1, -1, -1):
        above[i] = jnp.maximum(above[i], above[i + 1] - ROOM)
    dealt = [(low + high) >> 1 for low, high in zip(below, above)]
    short = jnp.int32(0)
    for cut in range(1, chips):
        right = held[cut] - dealt[cut]
        most_right = jnp.minimum(held[cut] - held[cut - 1], ROOM)
        most_left = jnp.minimum(held[cut + 1] - held[cut], ROOM)
        short = short + jnp.where((right > most_right) | (-right > most_left), 1, 0)
    return held, dealt, short


AT_PAIR = 0
AT_NEXT = AT_PAIR + ROOM
AT_DEALT = AT_NEXT + ROOM
AT_HOME = AT_DEALT + ROOM
AT_SHORT = AT_HOME + 2 * PAGE_HALF
AT_SLOW_SOURCE = AT_SHORT + 1
AT_SLOW_PLACE = AT_SLOW_SOURCE + ROOM
AT_SLOW_HOME = AT_SLOW_PLACE + ROOM
AT_IN_ORDER = AT_SLOW_HOME + 2 * PAGE_HALF
AT_SLOW_SEND = AT_IN_ORDER + 2 * PAGE_HALF


def plan_kernel(pages, device_ref, count_ref, table_ref):
    chips = pages // 2
    device = device_ref[0]
    core, chip = device & 1, device >> 1
    ends = page_ends_of(count_ref, pages)
    held, dealt, short = line_plan(ends, chips, core)
    held_mate, dealt_mate, short_mate = line_plan(ends, chips, 1 - core)
    table_ref[AT_SHORT] = jnp.where(short + short_mate > 0, 1, 0)
    falls, falls_mate = (
        [jnp.where(ranks[i] - ranks_dealt[i] > 2, 1, 0) for i in range(chips)]
        for ranks, ranks_dealt in ((held, dealt), (held_mate, dealt_mate))
    )

    low, high = pick_at(held, chip), pick_at(held, chip + 1)
    first, end = pick_at(dealt, chip), pick_at(dealt, chip + 1)
    falls_here = pick_at(falls, chip)
    own_start, own_end = pick_at(ends, device), pick_at(ends, device + 1)
    mate_start = pick_at(ends, device ^ 1)

    def turned(offset, falling):
        return jnp.where(falling > 0, ROOM - 1 - offset, offset)

    def local_code(rank):
        position = 2 * rank + core
        own = (position >= own_start) & (position < own_end)
        return jnp.where(own, (position - own_start) >> 1, 16 + ((position - mate_start) >> 1))

    def part_code(count, source):
        number, place = chunk_of(count)
        return (source + number) * 16 + place

    sides = len(CHUNKS)
    odd = chip & 1
    right_side, left_side = sides * odd, sides * (1 - odd)

    for slot in range(ROOM):
        rightwards, leftwards = local_code(high - 1 - slot), local_code(low + slot)
        table_ref[AT_PAIR + slot] = jnp.where(odd > 0, leftwards, rightwards)
        table_ref[AT_NEXT + slot] = jnp.where(odd > 0, rightwards, leftwards)
        offset = turned(jnp.int32(slot), falls_here)
        rank = first + offset
        code = jnp.where(rank < low, part_code(low - 1 - rank, 2 + left_side), local_code(rank))
        code = jnp.where(rank >= high, part_code(rank - high, 2 + right_side), code)
        table_ref[AT_DEALT + slot] = code
        node = jnp.int32(0)
        for place in range(1, chips):
            node = node + jnp.where(held[place] <= rank, 1, 0)
        table_ref[AT_SLOW_SOURCE + slot] = 2 * node + core
        table_ref[AT_SLOW_PLACE + slot] = offset
    for half, (ranks_dealt, turns) in enumerate(((dealt, falls), (dealt_mate, falls_mate))):
        lane = core ^ half
        here, there = pick_at(ranks_dealt, chip), pick_at(ranks_dealt, chip + 1)
        before = pick_at(ranks_dealt, chip - 1)
        turns_here, turns_right, turns_left = (pick_at(turns, chip + i) for i in (0, 1, -1))
        for slot in range(PAGE_HALF):
            rank = (own_start + ((own_start + lane) & 1) + 2 * slot - lane) >> 1
            at = half * PAGE_HALF + slot
            base = 3 * sides * half
            code = part_code(turned(rank - here, turns_here), base)
            right = part_code(turned(rank - there, turns_right), base + sides + right_side)
            left = part_code(turned(rank - before, turns_left), base + sides + left_side)
            code = jnp.where(rank >= there, right, code)
            table_ref[AT_HOME + at] = jnp.where(rank < here, left, code)
            node, start_there, turns_there = jnp.int32(0), jnp.int32(0), turns[0]
            for place in range(1, chips):
                beyond = ranks_dealt[place] <= rank
                node = node + jnp.where(beyond, 1, 0)
                start_there = jnp.where(beyond, ranks_dealt[place], start_there)
                turns_there = jnp.where(beyond, turns[place], turns_there)
            slow = (2 * node + lane) * ROOM + turned(rank - start_there, turns_there)
            table_ref[AT_SLOW_HOME + at] = jnp.clip(slow, 0, pages * ROOM - 1)
            table_ref[AT_IN_ORDER + at] = jnp.int32((6 * sides + half) * 16 + slot)
    for node in range(chips):
        for slot in range(ROOM):
            code = local_code(dealt[node] + slot)
            table_ref[AT_SLOW_SEND + node * ROOM + slot] = jnp.clip(code, 0, 31)


def make_plan(device, kept_count):
    pages = kept_count.shape[0]
    size = AT_SLOW_SEND + ROOM * (pages // 2)
    return pl.pallas_call(
        functools.partial(plan_kernel, pages),
        out_shape=jax.ShapeDtypeStruct((size,), jnp.int32),
        in_specs=[pl.BlockSpec(memory_space=pltpu.SMEM)] * 2,
        out_specs=pl.BlockSpec(memory_space=pltpu.SMEM),
        compiler_params=pltpu.CompilerParams(vmem_limit_bytes=MIB),
        cost_estimate=SMALL_COST,
        name="plan",
    )(device, kept_count)


def kept_blocks(device_ref, count_ref, keep_ref, pages):
    device = device_ref[0]
    start, count = jnp.int32(0), jnp.int32(0)
    for page in range(pages):
        start = start + jnp.where(page < device, count_ref[page], 0)
        count = count + jnp.where(page == device, count_ref[page], 0)
    blocks = []
    for half in range(2):
        offset = (start + device + half) & 1
        for slot in range(PAGE_HALF):
            index = 2 * slot + offset
            block = keep_ref[jnp.minimum(index, 2 * PAGE_HALF - 1)]
            blocks.append(jnp.where(index < count, block, -1))
    return blocks


def kept_blocks_once(device_ref, count_ref, keep_ref, pages, held):
    @pl.when(pl.program_id(0) == 0)
    def _():
        for slot, block in enumerate(kept_blocks(device_ref, count_ref, keep_ref, pages)):
            held[slot] = block

    return [held[slot] for slot in range(2 * PAGE_HALF)]


def pack_kernel(pages, device_ref, count_ref, keep_ref, home_ref, mine_ref, mate_ref, held):
    page_blocks, width = home_ref.shape[1], home_ref.shape[2]
    blocks = kept_blocks_once(device_ref, count_ref, keep_ref, pages, held)
    span = GROUP_ROWS * page_blocks
    row = lax.broadcasted_iota(jnp.int32, (GROUP_ROWS, span), 0)
    column = lax.broadcasted_iota(jnp.int32, (GROUP_ROWS, span), 1)
    chosen = jnp.concatenate(
        [jnp.where(column == row * page_blocks + block, 1.0, 0.0).astype(BF16) for block in blocks],
        axis=0,
    )
    packed = jnp.dot(
        chosen, home_ref[...].reshape(span, width), preferred_element_type=F32
    ).astype(BF16)
    half = PAGE_HALF * GROUP_ROWS
    mine_ref[...] = packed[:half].reshape(PAGE_HALF, GROUP_ROWS, width)
    mate_ref[...] = packed[half:].reshape(PAGE_HALF, GROUP_ROWS, width)


def pack(device, kept_count, keep_row, home):
    rows, page_blocks, width = home.shape
    shape = jax.ShapeDtypeStruct((PAGE_HALF, rows, width), BF16)
    place = pl.BlockSpec((PAGE_HALF, GROUP_ROWS, width), lambda step, *_: (0, step, 0))
    return pl.pallas_call(
        functools.partial(pack_kernel, kept_count.shape[0]),
        out_shape=(shape, shape),
        grid_spec=pltpu.PrefetchScalarGridSpec(
            num_scalar_prefetch=3,
            grid=(rows // GROUP_ROWS,),
            in_specs=[
                pl.BlockSpec((GROUP_ROWS, page_blocks, width), lambda step, *_: (step, 0, 0))
            ],
            out_specs=(place, place),
            scratch_shapes=[pltpu.SMEM((2 * PAGE_HALF,), jnp.int32)],
        ),
        compiler_params=pltpu.CompilerParams(vmem_limit_bytes=16 * MIB),
        name="pack",
    )(device, kept_count, keep_row, home)


LATE = (3, 5, 9, 11)


def merge_kernel(pages, device_ref, count_ref, keep_ref, code_ref, home_ref, found_ref, *refs):
    late, out_ref, held = refs[:-2], refs[-2], refs[-1]
    page_blocks, width = home_ref.shape[1], home_ref.shape[2]
    slots, size = 2 * PAGE_HALF, CHUNKS[-1]
    places = slots + size * len(LATE)

    @pl.when(pl.program_id(0) == 0)
    def _():
        blocks = kept_blocks(device_ref, count_ref, keep_ref, pages)
        spots = []
        for slot in range(slots):
            code = code_ref[slot]
            spot = jnp.int32(slot)
            for number, source in enumerate(LATE):
                spot = jnp.where(code >> 4 == source, slots + number * size + (code & 15), spot)
            spots.append(jnp.where(blocks[slot] >= 0, spot, -1))
        for place in range(places):
            block = jnp.int32(-1)
            for slot in range(slots) if place >= slots else (place,):
                block = jnp.where(spots[slot] == place, blocks[slot], block)
            held[place] = block

    span = GROUP_ROWS * page_blocks
    depth = places * GROUP_ROWS
    row = lax.broadcasted_iota(jnp.int32, (span, depth), 0)
    column = lax.broadcasted_iota(jnp.int32, (span, depth), 1)
    place_id = lax.broadcasted_iota(jnp.int32, (1, depth), 1) // GROUP_ROWS
    block_id = lax.broadcasted_iota(jnp.int32, (span, 1), 0) % page_blocks
    wanted = jnp.full((1, depth), -1, jnp.int32)
    kept = jnp.zeros((span, 1), jnp.int32)
    for place in range(places):
        block = held[place]
        wanted = jnp.where(place_id == place, block, wanted)
        kept = kept + jnp.where(block_id == block, 1, 0)
    chosen = jnp.where(
        (row // page_blocks == column % GROUP_ROWS) & (row % page_blocks == wanted), 1.0, 0.0
    ).astype(BF16)
    source = jnp.concatenate(
        [ref[...].reshape(-1, width) for ref in (found_ref,) + tuple(late)], axis=0
    )
    landed = jnp.dot(chosen, source, preferred_element_type=F32)
    home = home_ref[...].reshape(span, width).astype(F32)
    merged = jnp.where(kept > 0, landed, home).astype(BF16)
    out_ref[...] = merged.reshape(GROUP_ROWS, page_blocks, width)


def merge(device, kept_count, keep_row, codes, home, found, late):
    rows, page_blocks, width = home.shape
    page = pl.BlockSpec((GROUP_ROWS, page_blocks, width), lambda step, *_: (step, 0, 0))

    def some(array):
        return pl.BlockSpec((array.shape[0], GROUP_ROWS, width), lambda step, *_: (0, step, 0))

    return pl.pallas_call(
        functools.partial(merge_kernel, kept_count.shape[0]),
        out_shape=jax.ShapeDtypeStruct(home.shape, BF16),
        grid_spec=pltpu.PrefetchScalarGridSpec(
            num_scalar_prefetch=4,
            grid=(rows // GROUP_ROWS,),
            in_specs=[page, some(found)] + [some(array) for array in late],
            out_specs=page,
            scratch_shapes=[
                pltpu.SMEM((found.shape[0] + CHUNKS[-1] * len(LATE),), jnp.int32)
            ],
        ),
        compiler_params=pltpu.CompilerParams(vmem_limit_bytes=20 * MIB),
        cost_estimate=SMALL_COST,
        name="merge",
    )(device, kept_count, keep_row, codes, home, found, *late)


def start_copies(sources, wanted):
    for code, target, sem in wanted:
        which, place = code >> 4, code & 15
        for index, source in enumerate(sources):
            if len(sources) == 1:
                here = which > -(1 << 20)
            elif index == 0:
                here = which <= 0
            elif index == len(sources) - 1:
                here = which >= index
            else:
                here = which == index

            @pl.when(here)
            def _(source=source, place=place, target=target, sem=sem):
                inside = jnp.minimum(place, source.shape[0] - 1)
                pltpu.make_async_copy(source.at[inside], target, sem).start()


def choose_kernel(parts, n_sources, table_ref, *refs):
    sources, outs, sems = refs[:n_sources], refs[-1 - len(parts) : -1], refs[-1]
    targets = [
        (at + slot, out_ref.at[slot])
        for (at, total), out_ref in zip(parts, outs)
        for slot in range(total)
    ]
    start_copies(
        sources,
        [(table_ref[at], target, sems.at[number]) for number, (at, target) in enumerate(targets)],
    )
    for number, (_, target) in enumerate(targets):
        pltpu.make_async_copy(sources[0].at[0], target, sems.at[number]).wait()


def choose(table, parts, sources, name, after=()):
    block = sources[0].shape[1:]
    total = sum(count for _, count in parts)
    return pl.pallas_call(
        functools.partial(choose_kernel, parts, len(sources)),
        out_shape=tuple(jax.ShapeDtypeStruct((count,) + block, BF16) for _, count in parts),
        in_specs=[pl.BlockSpec(memory_space=pltpu.SMEM)]
        + [pl.BlockSpec(memory_space=pl.ANY)] * (len(sources) + len(after)),
        out_specs=tuple(pl.BlockSpec(memory_space=pltpu.VMEM) for _ in parts),
        scratch_shapes=[pltpu.SemaphoreType.DMA((total,))],
        compiler_params=pltpu.CompilerParams(vmem_limit_bytes=8 * MIB),
        cost_estimate=SMALL_COST,
        name=name,
    )(table, *sources, *after)


def join_kernel(spots_ref, near, side, mate, out_ref, sems):
    piece = near.shape[0]
    sources = (near, side, mate.at[0], mate.at[1])
    copies = []
    for number, source in enumerate(sources):
        place = pl.ds(pl.multiple_of(spots_ref[number] * piece, piece), piece)
        copies.append(pltpu.make_async_copy(source, out_ref.at[place, :], sems.at[number]))
    for copy in copies:
        copy.start()
    for copy in copies:
        copy.wait()


def join(spots, near, side, mate):
    shape = (4 * near.shape[0], near.shape[1])
    any_space = pl.BlockSpec(memory_space=pl.ANY)
    return pl.pallas_call(
        join_kernel,
        out_shape=jax.ShapeDtypeStruct(shape, BF16),
        in_specs=[pl.BlockSpec(memory_space=pltpu.SMEM)] + [any_space] * 3,
        out_specs=pl.BlockSpec(memory_space=pltpu.VMEM),
        scratch_shapes=[pltpu.SemaphoreType.DMA((4,))],
        compiler_params=pltpu.CompilerParams(vmem_limit_bytes=8 * MIB),
        name="join",
    )(spots, near, side, mate)


def in_hbm(array):
    return pltpu.with_memory_space_constraint(array, pltpu.HBM)


def split_store(value, high_ref, low_ref):
    high = value.astype(BF16)
    high_ref[...] = high
    low_ref[...] = (value - high.astype(F32)).astype(BF16)


def attend_kernel(n_after, own_ref, other_ref, rows_ref, b_ref, w_ref, *refs):
    (out_ref, held, normed, q_high, q_low, k_high, k_low, values, scores, sems) = refs[n_after:]
    blocks, rows, width = own_ref.shape
    span = held.shape[2]
    loads = [pltpu.make_async_copy(w_ref.at[j], held.at[j], sems.at[j]) for j in range(3)]
    for load in loads:
        load.start()
    gain, shift = rows_ref[0:1, :], rows_ref[1:2, :]
    for half, ref in enumerate((own_ref, other_ref)):
        for block in range(blocks):
            at = (half * blocks + block) * rows
            normed[at : at + rows] = norm_rows(ref[block].astype(F32), gain, shift).astype(BF16)

    def project(j):
        loads[j].wait()
        product = jnp.dot(normed[...], held[j], preferred_element_type=F32)
        return product + b_ref[j : j + 1, :]

    split_store(project(0) * HEAD_DIM ** (-0.5), q_high, q_low)
    split_store(project(1), k_high, k_low)
    values[...] = project(2).astype(BF16)
    tiles = span // 128
    heads = span // HEAD_DIM
    size = 2 * rows
    lane = lax.broadcasted_iota(jnp.int32, (1, 256), 1)

    def window(head):
        tile = min(head * HEAD_DIM // 128, tiles - 2)
        first = head * HEAD_DIM - tile * 128
        inside = (lane >= first) & (lane < first + HEAD_DIM)
        return tile, slice(tile * 128, tile * 128 + 256), inside

    def one_block(block, carry):
        near = pl.ds(pl.multiple_of(block * rows, rows), rows)
        far = pl.ds(pl.multiple_of((blocks + block) * rows, rows), rows)

        def both(ref, columns):
            return jnp.concatenate([ref[near, columns], ref[far, columns]], axis=0)

        def times(left, right):
            return lax.dot_general(
                left, right, (((1,), (1,)), ((), ())), preferred_element_type=F32
            )

        for head in range(heads):
            _, columns, inside = window(head)
            none = jnp.zeros((), BF16)
            qh = jnp.where(inside, both(q_high, columns), none)
            ql = jnp.where(inside, both(q_low, columns), none)
            kh, kl = both(k_high, columns), both(k_low, columns)
            scores[head * size : (head + 1) * size, :] = (
                times(qh, kh) + times(qh, kl) + times(ql, kh)
            )
        value = scores[...]
        value = jnp.exp(value - jnp.max(value, axis=-1, keepdims=True))
        weights = (value * (1.0 / jnp.sum(value, axis=-1, keepdims=True))).astype(BF16)
        sums = [None] * tiles
        for head in range(heads):
            tile, columns, inside = window(head)
            mixed = jnp.dot(
                weights[head * size : (head + 1) * size, :], both(values, columns),
                preferred_element_type=F32,
            )
            mixed = jnp.where(inside, mixed, 0.0)
            for part in range(2):
                piece = mixed[:, part * 128 : part * 128 + 128]
                old = sums[tile + part]
                sums[tile + part] = piece if old is None else old + piece
        result = jnp.concatenate(sums, axis=1).astype(BF16)
        out_ref[0, block] = result[:rows]
        out_ref[1, block] = result[rows:]
        return carry

    lax.fori_loop(0, blocks, one_block, 0)


def attend(own, other, rows_params, w_qkv, b_qkv, after=()):
    blocks, rows, width = own.shape
    span = w_qkv.shape[2]
    total = 2 * blocks * rows
    vmem = pl.BlockSpec(memory_space=pltpu.VMEM)
    return pl.pallas_call(
        functools.partial(attend_kernel, len(after)),
        out_shape=jax.ShapeDtypeStruct((2, blocks, rows, span), BF16),
        in_specs=[vmem] * 4 + [pl.BlockSpec(memory_space=pl.ANY)] * (1 + len(after)),
        out_specs=vmem,
        scratch_shapes=[pltpu.VMEM((3, width, span), BF16), pltpu.VMEM((total, width), BF16)]
        + [pltpu.VMEM((total, span), BF16)] * 5
        + [
            pltpu.VMEM((2 * rows * (span // HEAD_DIM), 2 * rows), F32),
            pltpu.SemaphoreType.DMA((3,)),
        ],
        compiler_params=pltpu.CompilerParams(vmem_limit_bytes=28 * MIB),
        cost_estimate=pl.CostEstimate(
            flops=24 * total * width * span, bytes_accessed=6 * width * span, transcendentals=0
        ),
        name="attend",
    )(own, other, rows_params, b_qkv, in_hbm(w_qkv), *after)


UP_TILE = 1536
DOWN_TILE = 256
SLOTS = 3


def mlp_kernel(n_after, own_ref, other_ref, mine_ref, theirs_ref, rows_ref, b_up_ref, w_mine, w_theirs,
               w_up, w_down, *refs):
    (keep_ref, send_ref, residual, renormed, hidden, outs, ups, downs, out_sems, up_sems,
     down_sems) = refs[n_after:]
    blocks, rows, width = own_ref.shape
    half = blocks * rows
    span = outs.shape[1]
    up_steps, down_steps = w_up.shape[1] // UP_TILE, width // DOWN_TILE

    def load_up(step):
        columns = pl.ds(pl.multiple_of(step * UP_TILE, UP_TILE), UP_TILE)
        slot = lax.rem(step, SLOTS)
        return pltpu.make_async_copy(w_up.at[:, columns], ups.at[slot], up_sems.at[slot])

    def load_down(step):
        columns = pl.ds(pl.multiple_of(step * DOWN_TILE, DOWN_TILE), DOWN_TILE)
        slot = lax.rem(step, SLOTS)
        return pltpu.make_async_copy(w_down.at[:, columns], downs.at[slot], down_sems.at[slot])

    out_loads = [
        pltpu.make_async_copy(source, outs.at[number], out_sems.at[number])
        for number, source in enumerate((w_mine, w_theirs))
    ]
    for load in out_loads:
        load.start()
    load_up(jnp.int32(0)).start()
    gain, shift = rows_ref[2:3, :], rows_ref[3:4, :]
    mine = mine_ref[...].reshape(2 * half, span)
    theirs = jnp.concatenate(
        [theirs_ref[1].reshape(half, span), theirs_ref[0].reshape(half, span)], axis=0
    )
    for number, attended in enumerate((mine, theirs)):
        out_loads[number].wait()
        for slot in (range(1, 3), range(3, SLOTS))[number]:
            load_up(jnp.int32(slot)).start()
        for column in range(0, width, DOWN_TILE):
            columns = slice(column, column + DOWN_TILE)
            part = jnp.dot(attended, outs[number, :, columns], preferred_element_type=F32)
            part = part.astype(BF16).astype(F32)
            if number == 0:
                residual[:, columns] = part + rows_ref[4:5, columns]
            else:
                residual[:, columns] += part
    for side, ref in enumerate((own_ref, other_ref)):
        for block in range(blocks):
            at = slice((side * blocks + block) * rows, (side * blocks + block + 1) * rows)
            value = ref[block].astype(F32) + residual[at]
            if side == 0:
                residual[at] = value
            renormed[at] = norm_rows(value, gain, shift).astype(BF16)

    def one_up(step, carry):
        load_up(step).wait()
        slot = lax.rem(step, SLOTS)
        for part in range(0, UP_TILE, 256):
            columns = pl.ds(pl.multiple_of(step * UP_TILE + part, 256), 256)
            raised = jnp.dot(
                renormed[...], ups[slot, :, part : part + 256], preferred_element_type=F32
            )
            raised = raised + b_up_ref[0:1, columns]
            hidden[:, columns] = jax.nn.gelu(raised, approximate=True).astype(BF16)
        ahead = step + SLOTS

        @pl.when(ahead < up_steps)
        def _():
            load_up(ahead).start()

        @pl.when((ahead >= up_steps) & (ahead < up_steps + down_steps))
        def _():
            load_down(ahead - up_steps).start()

        return carry

    lax.fori_loop(0, up_steps, one_up, 0)

    def one_down(step, carry):
        load_down(step).wait()
        columns = pl.ds(pl.multiple_of(step * DOWN_TILE, DOWN_TILE), DOWN_TILE)
        lowered = jnp.dot(
            hidden[...], downs[lax.rem(step, SLOTS)], preferred_element_type=F32
        )
        kept = residual[:half, columns] + lowered[:half] + rows_ref[5:6, columns]
        keep_ref[:, :, columns] = kept.reshape(blocks, rows, DOWN_TILE)
        send_ref[:, :, columns] = lowered[half:].astype(BF16).reshape(blocks, rows, DOWN_TILE)

        @pl.when(step + SLOTS < down_steps)
        def _():
            load_down(step + SLOTS).start()

        return carry

    lax.fori_loop(0, down_steps, one_down, 0)


def mlp(own, other, mine, theirs, rows_params, b_up, weights, after):
    blocks, rows, width = own.shape
    span = mine.shape[3]
    total = 2 * blocks * rows
    vmem = pl.BlockSpec(memory_space=pltpu.VMEM)
    hbm = pl.BlockSpec(memory_space=pl.ANY)
    w_mine, w_theirs, w_up, w_down = weights
    hidden = w_up.shape[1]
    return pl.pallas_call(
        functools.partial(mlp_kernel, len(after)),
        out_shape=(
            jax.ShapeDtypeStruct((blocks, rows, width), F32),
            jax.ShapeDtypeStruct((blocks, rows, width), BF16),
        ),
        in_specs=[vmem] * 6 + [hbm] * (4 + len(after)),
        out_specs=(vmem, vmem),
        scratch_shapes=[
            pltpu.VMEM((total, width), F32),
            pltpu.VMEM((total, width), BF16),
            pltpu.VMEM((total, hidden), BF16),
            pltpu.VMEM((2, span, width), BF16),
            pltpu.VMEM((SLOTS, width, UP_TILE), BF16),
            pltpu.VMEM((SLOTS, hidden, DOWN_TILE), BF16),
            pltpu.SemaphoreType.DMA((2,)),
            pltpu.SemaphoreType.DMA((SLOTS,)),
            pltpu.SemaphoreType.DMA((SLOTS,)),
        ],
        compiler_params=pltpu.CompilerParams(vmem_limit_bytes=46 * MIB),
        cost_estimate=pl.CostEstimate(
            flops=8 * total * width * (span + hidden),
            bytes_accessed=4 * width * (span + hidden),
            transcendentals=0,
        ),
        name="mlp",
    )(
        own, other, mine, theirs, rows_params, b_up, in_hbm(w_mine), w_theirs, in_hbm(w_up),
        in_hbm(w_down), *after,
    )


def add_kernel(n_after, keep_ref, came_ref, *refs):
    out_ref = refs[n_after]
    out_ref[...] = (keep_ref[...] + came_ref[...].astype(F32)).astype(BF16)


def add(keep, came, after):
    vmem = pl.BlockSpec(memory_space=pltpu.VMEM)
    return pl.pallas_call(
        functools.partial(add_kernel, len(after)),
        out_shape=jax.ShapeDtypeStruct(came.shape, BF16),
        in_specs=[vmem] * 2 + [pl.BlockSpec(memory_space=pl.ANY)] * len(after),
        out_specs=vmem,
        compiler_params=pltpu.CompilerParams(vmem_limit_bytes=8 * MIB),
        cost_estimate=SMALL_COST,
        name="add",
    )(keep, came, *after)


def swap(value):
    return lax.ppermute(value, "tensor", [(0, 1), (1, 0)])


def line_up_kernel(total, n_after, *refs):
    sources, out_ref, sems = refs[:total], refs[total + n_after], refs[-1]
    copies = [
        pltpu.make_async_copy(source, out_ref.at[number], sems.at[number])
        for number, source in enumerate(sources)
    ]
    for copy in copies:
        copy.start()
    for copy in copies:
        copy.wait()


def line_up(arrays, after, name):
    any_space = pl.BlockSpec(memory_space=pl.ANY)
    total = len(arrays)
    return pl.pallas_call(
        functools.partial(line_up_kernel, total, len(after)),
        out_shape=jax.ShapeDtypeStruct((total,) + arrays[0].shape, arrays[0].dtype),
        in_specs=[any_space] * (total + len(after)),
        out_specs=pl.BlockSpec(memory_space=pltpu.VMEM),
        scratch_shapes=[pltpu.SemaphoreType.DMA((total,))],
        compiler_params=pltpu.CompilerParams(vmem_limit_bytes=8 * MIB),
        cost_estimate=SMALL_COST,
        name=name,
    )(*arrays, *after)


def w_out_place(w_out):
    core = lax.axis_index("dp") & 1
    group = lax.axis_index("groups")
    return 2 * group + core, 2 * (1 - group) + core, w_out.shape[0] // 4


def piece_kernel(n_after, number_ref, w_ref, *refs):
    out_ref, sem = refs[n_after:]
    piece = out_ref.shape[0]
    rows = pl.ds(pl.multiple_of(number_ref[0] * piece, piece), piece)
    copy = pltpu.make_async_copy(w_ref.at[rows, :], out_ref, sem)
    copy.start()
    copy.wait()


def w_out_piece(w_out, after):
    number, _, piece = w_out_place(w_out)
    any_space = pl.BlockSpec(memory_space=pl.ANY)
    return pl.pallas_call(
        functools.partial(piece_kernel, len(after)),
        out_shape=jax.ShapeDtypeStruct((piece, w_out.shape[1]), BF16),
        in_specs=[pl.BlockSpec(memory_space=pltpu.SMEM)] + [any_space] * (1 + len(after)),
        out_specs=pl.BlockSpec(memory_space=pltpu.VMEM),
        scratch_shapes=[pltpu.SemaphoreType.DMA],
        compiler_params=pltpu.CompilerParams(vmem_limit_bytes=4 * MIB),
        cost_estimate=SMALL_COST,
        name="w_piece",
    )(number.astype(jnp.int32).reshape(1), in_hbm(w_out), *after)


def other_w_out(w_out, near, side, after):
    number, other, _ = w_out_place(w_out)
    dp_size = lax.axis_size("dp")
    both = line_up([near, side], after, "w_both")
    mate = lax.ppermute(both, "dp", [(d, d ^ 1) for d in range(dp_size)])
    spots = jnp.stack([number, other, number ^ 1, other ^ 1]).astype(jnp.int32)
    return join(spots, near, side, mate)


def attend_rows(projected):
    row_total, count_blocks, width = (projected.shape[0], projected.shape[1], projected.shape[3])
    head_count = width // HEAD_DIM
    queries = projected[:, :, 0].reshape(row_total, count_blocks, head_count, HEAD_DIM)
    key_rows = projected[:, :, 1].reshape(row_total, count_blocks, head_count, HEAD_DIM)
    values = projected[:, :, 2].astype(BF16).reshape(row_total, count_blocks, head_count, HEAD_DIM)
    scores = jnp.einsum(
        "qnhd,snhd->nhqs", queries, key_rows, precision=lax.Precision.HIGHEST
    ) * HEAD_DIM ** (-0.5)
    weights = jax.nn.softmax(scores, axis=-1).astype(BF16)
    attended = jnp.einsum("nhqs,snhd->qnhd", weights, values, preferred_element_type=F32)
    return attended.astype(BF16).reshape(row_total, count_blocks, width)


def encode_split(own, params):
    (pre_gain, pre_shift, w_qkv, b_qkv, w_out, b_out, mlp_gain, mlp_shift, w_up, b_up, w_down,
     b_down) = params
    block_rows = jnp.swapaxes(own, 0, 1)
    rows_dev = block_rows.shape[0]
    gathered = lax.all_gather(block_rows, "tensor", axis=0, tiled=True)
    normed = norm_rows(gathered.astype(F32), pre_gain, pre_shift).astype(BF16)
    attended = attend_rows(
        jnp.einsum("qnd,jde->qnje", normed, w_qkv, preferred_element_type=F32) + b_qkv[None, None]
    )
    partial_value = jnp.einsum("qne,ed->qnd", attended, w_out, preferred_element_type=F32)
    summed = lax.psum(partial_value.astype(BF16), "tensor").astype(F32)
    residual_all = gathered.astype(F32) + summed + b_out
    renormed = norm_rows(residual_all, mlp_gain, mlp_shift).astype(BF16)
    raised = jnp.einsum("qnd,df->qnf", renormed, w_up, preferred_element_type=F32) + b_up
    hidden = jax.nn.gelu(raised, approximate=True).astype(BF16)
    residual = lax.dynamic_slice_in_dim(
        residual_all, lax.axis_index("tensor") * rows_dev, rows_dev, 0
    )
    mlp_out = lax.psum_scatter(
        jnp.einsum("qnf,fd->qnd", hidden, w_down, preferred_element_type=F32).astype(BF16),
        "tensor", scatter_dimension=0, tiled=True,
    ).astype(F32)
    return jnp.swapaxes((residual + mlp_out + b_down).astype(BF16), 0, 1)


def per_device(paired, patches, kept_count, keep_list, *params):
    home = in_hbm(patches[0])
    keep_row = in_hbm(keep_list[0])
    kept_count = in_hbm(kept_count)
    dp_size = lax.axis_size("dp")
    device = lax.axis_index("dp").astype(jnp.int32).reshape(1)
    mates = [(d, d ^ 1) for d in range(dp_size)]
    pairs = [(d, d ^ 2) for d in range(dp_size)]
    nexts = [
        (d, d ^ 1 if d < 2 or d >= dp_size - 2 else ((d + 2) ^ 2) - 2) for d in range(dp_size)
    ]

    def to_mate(value):
        return lax.ppermute(value, "dp", mates)

    def to_pair(value):
        return lax.ppermute(value, "dp", pairs)

    def to_next(value):
        return lax.ppermute(value, "dp", nexts)

    mine, for_mate = pack(device, kept_count, keep_row, home)
    from_mate = to_mate(for_mate)
    table = make_plan(device, kept_count)
    short = table[AT_SHORT : AT_SHORT + 1].astype(F32)
    if paired:
        short = short + lax.ppermute(short, "groups", [(0, 1), (1, 0)])
    else:
        short = lax.pmax(short, "groups")
    flag = short
    short = flag[0] > 0

    parts = tuple(zip(STARTS, CHUNKS))
    sends = [(AT_PAIR + at, size) for at, size in parts] + [(AT_NEXT + at, size) for at, size in parts]
    going = choose(table, sends, [mine, from_mate], "send")
    came_pair = [to_pair(value) for value in going[: len(parts)]]
    came_next = [to_next(value) for value in going[len(parts) :]]

    def deal_fast(chunk, after):
        came = [came_pair[min(part, chunk)] for part in range(len(parts))]
        came = came + [came_next[min(part, chunk)] for part in range(len(parts))]
        at, size = parts[chunk]
        sources = [mine, from_mate] + came
        return choose(table, [(AT_DEALT + at, size)], sources, "deal_%d" % chunk, after)[0]

    def deal_slow(chunk):
        chips = dp_size // 2
        (picked,) = choose(table, [(AT_SLOW_SEND, ROOM * chips)], [mine, from_mate], "deal_slow")
        picked = picked.reshape((chips, ROOM) + picked.shape[1:])
        spread = jnp.repeat(picked, 2, axis=0)
        arrived = lax.all_to_all(spread, "dp", split_axis=0, concat_axis=0, tiled=True)
        at, size = parts[chunk]
        return jnp.stack(
            [
                arrived[table[AT_SLOW_SOURCE + j], table[AT_SLOW_PLACE + j]]
                for j in range(at, at + size)
            ]
        )

    def deal(chunk, after=()):
        return lax.cond(short, lambda: deal_slow(chunk), lambda: deal_fast(chunk, after))

    if paired:
        (pre_gain, pre_shift, w_qkv, b_qkv, w_out, b_out, mlp_gain, mlp_shift, w_up, b_up, w_down,
         b_down) = params
        rows_params = jnp.stack([pre_gain, pre_shift, mlp_gain, mlp_shift, b_out, b_down])
        b_up = b_up.reshape(1, -1)
        w_near = swap(w_out_piece(w_out, [for_mate]))

        def start(own, after):
            other = swap(own)
            mine = attend(own, other, rows_params, w_qkv, b_qkv, after)
            return own, other, mine, swap(mine)

        def finish(state, after):
            keep, send = mlp(*state, rows_params, b_up, weights, after)
            return keep, swap(send)

        blocks_0 = deal(0)
        state_0 = start(blocks_0, [])
        w_sent = line_up([w_near], [flag], "w_near")
        blocks_1 = deal(1, [w_sent])
        state_1 = start(blocks_1, [])
        w_side = lax.ppermute(w_sent, "groups", [(0, 1), (1, 0)])[0]
        w_theirs = other_w_out(w_out, w_near, w_side, [blocks_1])
        weights = (w_out, w_theirs, w_up, w_down)
        done_0 = finish(state_0, [state_1[2]])
        done_1 = finish(state_1, [done_0[0]])
        results, from_pair, from_next = [], [], []
        for done, beside in ((done_0, done_1[:1]), (done_1, ())):
            results.append(add(*done, list(beside) + from_pair[-1:] + from_next[-1:]))
            from_pair.append(to_pair(results[-1]))
            from_next.append(to_next(results[-1]))
    else:
        results = [encode_split(deal(chunk), params) for chunk in range(len(parts))]
        from_pair = [to_pair(value) for value in results]
        from_next = [to_next(value) for value in results]

    back = results + from_pair + from_next
    last = len(parts) - 1
    back = back + [
        back[place] if place + len(back) in LATE else to_mate(value)
        for place, value in enumerate(back)
    ]

    def home_slow():
        spread = lax.all_gather(jnp.concatenate(results), "dp", axis=0, tiled=True)
        places = table[AT_SLOW_HOME : AT_SLOW_HOME + 2 * PAGE_HALF]
        return (
            jnp.take(spread, places[:PAGE_HALF], axis=0),
            jnp.take(spread, places[PAGE_HALF:], axis=0),
        )

    found = lax.cond(short, home_slow, lambda: (mine, from_mate))
    slots = 2 * PAGE_HALF
    codes = jnp.where(
        short, table[AT_IN_ORDER : AT_IN_ORDER + slots], table[AT_HOME : AT_HOME + slots]
    )
    early = [results[0] if place in LATE else value for place, value in enumerate(back)]
    (gathered,) = choose(codes, [(0, slots)], early + list(found), "gather")
    late = [from_pair[last], from_next[last]]
    mates_late = to_mate(line_up(late, [gathered], "late"))
    late.append(mates_late.reshape((-1,) + mates_late.shape[2:]))
    return merge(device, kept_count, keep_row, codes, home, gathered, late)[None]


def solution(mesh):
    in_specs = (
        P(("groups", "dp"), "tensor", None, None),
        P("groups"),
        P(("groups", "dp"), None),
        P(),
        P(),
        P(None, None, "tensor"),
        P(None, "tensor"),
        P("tensor", None),
        P(),
        P(),
        P(),
        P(None, "tensor"),
        P("tensor"),
        P("tensor", None),
        P(),
    )
    out_specs = P(("groups", "dp"), "tensor", None, None)
    paired = mesh.shape["tensor"] == 2 and mesh.shape["groups"] == 2
    return jax.shard_map(
        functools.partial(per_device, paired), mesh=mesh, in_specs=in_specs, out_specs=out_specs,
        check_vma=False,
    )
```

```python
import functools

import jax
import jax.numpy as jnp
from jax import lax
from jax.experimental import pallas as pl
from jax.experimental.pallas import tpu as pltpu
from jax.sharding import PartitionSpec as P

HEAD_DIM = 112
CHUNKS = (3, 2)
STARTS = (0, 3)
ROOM = 5
PAGE_HALF = 8
GROUP_ROWS = 16
F32 = jnp.float32
BF16 = jnp.bfloat16
MIB = 1 << 20
SMALL_COST = pl.CostEstimate(flops=1000, bytes_accessed=1000, transcendentals=0)


def norm_rows(inputs, gain, shift):
    average = jnp.mean(inputs, axis=-1, keepdims=True)
    centred = inputs - average
    variance = jnp.mean(centred * centred, axis=-1, keepdims=True)
    return centred * lax.rsqrt(variance + 1e-06) * gain + shift


def pick_at(values, index):
    total = jnp.int32(0)
    for place, value in enumerate(values):
        total = total + jnp.where(index == place, value, 0)
    return total


def page_ends_of(count_ref, pages):
    ends = [jnp.int32(0)]
    for page in range(pages):
        ends.append(ends[-1] + count_ref[page])
    return ends


def chunk_of(slot):
    number, start = jnp.int32(0), jnp.int32(0)
    for chunk in range(1, len(CHUNKS)):
        number = jnp.where(slot >= STARTS[chunk], chunk, number)
        start = jnp.where(slot >= STARTS[chunk], STARTS[chunk], start)
    return number, slot - start


def line_plan(ends, chips, core):
    held = [(ends[2 * chip] + 1 - core) >> 1 for chip in range(chips + 1)]
    total = held[chips]
    wanted = [
        jnp.clip(held[i], jnp.maximum(total - ROOM * (chips - i), 0), jnp.minimum(total, ROOM * i))
        for i in range(chips + 1)
    ]
    below, above = list(wanted), list(wanted)
    for i in range(1, chips + 1):
        below[i] = jnp.minimum(below[i], below[i - 1] + ROOM)
    for i in range(chips - 1, -1, -1):
        above[i] = jnp.maximum(above[i], above[i + 1] - ROOM)
    dealt = [(low + high) >> 1 for low, high in zip(below, above)]
    short = jnp.int32(0)
    for cut in range(1, chips):
        right = held[cut] - dealt[cut]
        most_right = jnp.minimum(held[cut] - held[cut - 1], ROOM)
        most_left = jnp.minimum(held[cut + 1] - held[cut], ROOM)
        short = short + jnp.where((right > most_right) | (-right > most_left), 1, 0)
    return held, dealt, short


AT_PAIR = 0
AT_NEXT = AT_PAIR + ROOM
AT_DEALT = AT_NEXT + ROOM
AT_HOME = AT_DEALT + ROOM
AT_SHORT = AT_HOME + 2 * PAGE_HALF
AT_SLOW_SOURCE = AT_SHORT + 1
AT_SLOW_PLACE = AT_SLOW_SOURCE + ROOM
AT_SLOW_HOME = AT_SLOW_PLACE + ROOM
AT_IN_ORDER = AT_SLOW_HOME + 2 * PAGE_HALF
AT_SLOW_SEND = AT_IN_ORDER + 2 * PAGE_HALF


def plan_kernel(pages, device_ref, count_ref, table_ref):
    chips = pages // 2
    device = device_ref[0]
    core, chip = device & 1, device >> 1
    ends = page_ends_of(count_ref, pages)
    held, dealt, short = line_plan(ends, chips, core)
    held_mate, dealt_mate, short_mate = line_plan(ends, chips, 1 - core)
    table_ref[AT_SHORT] = jnp.where(short + short_mate > 0, 1, 0)
    falls, falls_mate = (
        [jnp.where(ranks[i] - ranks_dealt[i] > 2, 1, 0) for i in range(chips)]
        for ranks, ranks_dealt in ((held, dealt), (held_mate, dealt_mate))
    )

    low, high = pick_at(held, chip), pick_at(held, chip + 1)
    first, end = pick_at(dealt, chip), pick_at(dealt, chip + 1)
    falls_here = pick_at(falls, chip)
    own_start, own_end = pick_at(ends, device), pick_at(ends, device + 1)
    mate_start = pick_at(ends, device ^ 1)

    def turned(offset, falling):
        return jnp.where(falling > 0, ROOM - 1 - offset, offset)

    def local_code(rank):
        position = 2 * rank + core
        own = (position >= own_start) & (position < own_end)
        return jnp.where(own, (position - own_start) >> 1, 16 + ((position - mate_start) >> 1))

    def part_code(count, source):
        number, place = chunk_of(count)
        return (source + number) * 16 + place

    sides = len(CHUNKS)
    odd = chip & 1
    right_side, left_side = sides * odd, sides * (1 - odd)

    for slot in range(ROOM):
        rightwards, leftwards = local_code(high - 1 - slot), local_code(low + slot)
        table_ref[AT_PAIR + slot] = jnp.where(odd > 0, leftwards, rightwards)
        table_ref[AT_NEXT + slot] = jnp.where(odd > 0, rightwards, leftwards)
        offset = turned(jnp.int32(slot), falls_here)
        rank = first + offset
        code = jnp.where(rank < low, part_code(low - 1 - rank, 2 + left_side), local_code(rank))
        code = jnp.where(rank >= high, part_code(rank - high, 2 + right_side), code)
        table_ref[AT_DEALT + slot] = code
        node = jnp.int32(0)
        for place in range(1, chips):
            node = node + jnp.where(held[place] <= rank, 1, 0)
        table_ref[AT_SLOW_SOURCE + slot] = 2 * node + core
        table_ref[AT_SLOW_PLACE + slot] = offset
    for half, (ranks_dealt, turns) in enumerate(((dealt, falls), (dealt_mate, falls_mate))):
        lane = core ^ half
        here, there = pick_at(ranks_dealt, chip), pick_at(ranks_dealt, chip + 1)
        before = pick_at(ranks_dealt, chip - 1)
        turns_here, turns_right, turns_left = (pick_at(turns, chip + i) for i in (0, 1, -1))
        for slot in range(PAGE_HALF):
            rank = (own_start + ((own_start + lane) & 1) + 2 * slot - lane) >> 1
            at = half * PAGE_HALF + slot
            base = 3 * sides * half
            code = part_code(turned(rank - here, turns_here), base)
            right = part_code(turned(rank - there, turns_right), base + sides + right_side)
            left = part_code(turned(rank - before, turns_left), base + sides + left_side)
            code = jnp.where(rank >= there, right, code)
            table_ref[AT_HOME + at] = jnp.where(rank < here, left, code)
            node, start_there, turns_there = jnp.int32(0), jnp.int32(0), turns[0]
            for place in range(1, chips):
                beyond = ranks_dealt[place] <= rank
                node = node + jnp.where(beyond, 1, 0)
                start_there = jnp.where(beyond, ranks_dealt[place], start_there)
                turns_there = jnp.where(beyond, turns[place], turns_there)
            slow = (2 * node + lane) * ROOM + turned(rank - start_there, turns_there)
            table_ref[AT_SLOW_HOME + at] = jnp.clip(slow, 0, pages * ROOM - 1)
            table_ref[AT_IN_ORDER + at] = jnp.int32((6 * sides + half) * 16 + slot)
    for node in range(chips):
        for slot in range(ROOM):
            code = local_code(dealt[node] + slot)
            table_ref[AT_SLOW_SEND + node * ROOM + slot] = jnp.clip(code, 0, 31)


def make_plan(device, kept_count):
    pages = kept_count.shape[0]
    size = AT_SLOW_SEND + ROOM * (pages // 2)
    return pl.pallas_call(
        functools.partial(plan_kernel, pages),
        out_shape=jax.ShapeDtypeStruct((size,), jnp.int32),
        in_specs=[pl.BlockSpec(memory_space=pltpu.SMEM)] * 2,
        out_specs=pl.BlockSpec(memory_space=pltpu.SMEM),
        compiler_params=pltpu.CompilerParams(vmem_limit_bytes=MIB),
        cost_estimate=SMALL_COST,
        name="plan",
    )(device, kept_count)


def kept_blocks(device_ref, count_ref, keep_ref, pages):
    device = device_ref[0]
    start, count = jnp.int32(0), jnp.int32(0)
    for page in range(pages):
        start = start + jnp.where(page < device, count_ref[page], 0)
        count = count + jnp.where(page == device, count_ref[page], 0)
    blocks = []
    for half in range(2):
        offset = (start + device + half) & 1
        for slot in range(PAGE_HALF):
            index = 2 * slot + offset
            block = keep_ref[jnp.minimum(index, 2 * PAGE_HALF - 1)]
            blocks.append(jnp.where(index < count, block, -1))
    return blocks


def kept_blocks_once(device_ref, count_ref, keep_ref, pages, held):
    @pl.when(pl.program_id(0) == 0)
    def _():
        for slot, block in enumerate(kept_blocks(device_ref, count_ref, keep_ref, pages)):
            held[slot] = block

    return [held[slot] for slot in range(2 * PAGE_HALF)]


def pack_kernel(pages, device_ref, count_ref, keep_ref, home_ref, mine_ref, mate_ref, held):
    page_blocks, width = home_ref.shape[1], home_ref.shape[2]
    blocks = kept_blocks_once(device_ref, count_ref, keep_ref, pages, held)
    span = GROUP_ROWS * page_blocks
    row = lax.broadcasted_iota(jnp.int32, (GROUP_ROWS, span), 0)
    column = lax.broadcasted_iota(jnp.int32, (GROUP_ROWS, span), 1)
    chosen = jnp.concatenate(
        [jnp.where(column == row * page_blocks + block, 1.0, 0.0).astype(BF16) for block in blocks],
        axis=0,
    )
    packed = jnp.dot(
        chosen, home_ref[...].reshape(span, width), preferred_element_type=F32
    ).astype(BF16)
    half = PAGE_HALF * GROUP_ROWS
    mine_ref[...] = packed[:half].reshape(PAGE_HALF, GROUP_ROWS, width)
    mate_ref[...] = packed[half:].reshape(PAGE_HALF, GROUP_ROWS, width)


def pack(device, kept_count, keep_row, home):
    rows, page_blocks, width = home.shape
    shape = jax.ShapeDtypeStruct((PAGE_HALF, rows, width), BF16)
    place = pl.BlockSpec((PAGE_HALF, GROUP_ROWS, width), lambda step, *_: (0, step, 0))
    return pl.pallas_call(
        functools.partial(pack_kernel, kept_count.shape[0]),
        out_shape=(shape, shape),
        grid_spec=pltpu.PrefetchScalarGridSpec(
            num_scalar_prefetch=3,
            grid=(rows // GROUP_ROWS,),
            in_specs=[
                pl.BlockSpec((GROUP_ROWS, page_blocks, width), lambda step, *_: (step, 0, 0))
            ],
            out_specs=(place, place),
            scratch_shapes=[pltpu.SMEM((2 * PAGE_HALF,), jnp.int32)],
        ),
        compiler_params=pltpu.CompilerParams(vmem_limit_bytes=16 * MIB),
        name="pack",
    )(device, kept_count, keep_row, home)


LATE = (3, 5, 9, 11)


def merge_kernel(pages, device_ref, count_ref, keep_ref, code_ref, home_ref, found_ref, *refs):
    late, out_ref, held = refs[:-2], refs[-2], refs[-1]
    page_blocks, width = home_ref.shape[1], home_ref.shape[2]
    slots, size = 2 * PAGE_HALF, CHUNKS[-1]
    places = slots + size * len(LATE)

    @pl.when(pl.program_id(0) == 0)
    def _():
        blocks = kept_blocks(device_ref, count_ref, keep_ref, pages)
        spots = []
        for slot in range(slots):
            code = code_ref[slot]
            spot = jnp.int32(slot)
            for number, source in enumerate(LATE):
                spot = jnp.where(code >> 4 == source, slots + number * size + (code & 15), spot)
            spots.append(jnp.where(blocks[slot] >= 0, spot, -1))
        for place in range(places):
            block = jnp.int32(-1)
            for slot in range(slots) if place >= slots else (place,):
                block = jnp.where(spots[slot] == place, blocks[slot], block)
            held[place] = block

    span = GROUP_ROWS * page_blocks
    depth = places * GROUP_ROWS
    row = lax.broadcasted_iota(jnp.int32, (span, depth), 0)
    column = lax.broadcasted_iota(jnp.int32, (span, depth), 1)
    place_id = lax.broadcasted_iota(jnp.int32, (1, depth), 1) // GROUP_ROWS
    block_id = lax.broadcasted_iota(jnp.int32, (span, 1), 0) % page_blocks
    wanted = jnp.full((1, depth), -1, jnp.int32)
    kept = jnp.zeros((span, 1), jnp.int32)
    for place in range(places):
        block = held[place]
        wanted = jnp.where(place_id == place, block, wanted)
        kept = kept + jnp.where(block_id == block, 1, 0)
    chosen = jnp.where(
        (row // page_blocks == column % GROUP_ROWS) & (row % page_blocks == wanted), 1.0, 0.0
    ).astype(BF16)
    source = jnp.concatenate(
        [ref[...].reshape(-1, width) for ref in (found_ref,) + tuple(late)], axis=0
    )
    landed = jnp.dot(chosen, source, preferred_element_type=F32)
    home = home_ref[...].reshape(span, width).astype(F32)
    merged = jnp.where(kept > 0, landed, home).astype(BF16)
    out_ref[...] = merged.reshape(GROUP_ROWS, page_blocks, width)


def merge(device, kept_count, keep_row, codes, home, found, late):
    rows, page_blocks, width = home.shape
    page = pl.BlockSpec((GROUP_ROWS, page_blocks, width), lambda step, *_: (step, 0, 0))

    def some(array):
        return pl.BlockSpec((array.shape[0], GROUP_ROWS, width), lambda step, *_: (0, step, 0))

    return pl.pallas_call(
        functools.partial(merge_kernel, kept_count.shape[0]),
        out_shape=jax.ShapeDtypeStruct(home.shape, BF16),
        grid_spec=pltpu.PrefetchScalarGridSpec(
            num_scalar_prefetch=4,
            grid=(rows // GROUP_ROWS,),
            in_specs=[page, some(found)] + [some(array) for array in late],
            out_specs=page,
            scratch_shapes=[
                pltpu.SMEM((found.shape[0] + CHUNKS[-1] * len(LATE),), jnp.int32)
            ],
        ),
        compiler_params=pltpu.CompilerParams(vmem_limit_bytes=20 * MIB),
        cost_estimate=SMALL_COST,
        name="merge",
    )(device, kept_count, keep_row, codes, home, found, *late)


def start_copies(sources, wanted):
    for code, target, sem in wanted:
        which, place = code >> 4, code & 15
        for index, source in enumerate(sources):
            if len(sources) == 1:
                here = which > -(1 << 20)
            elif index == 0:
                here = which <= 0
            elif index == len(sources) - 1:
                here = which >= index
            else:
                here = which == index

            @pl.when(here)
            def _(source=source, place=place, target=target, sem=sem):
                inside = jnp.minimum(place, source.shape[0] - 1)
                pltpu.make_async_copy(source.at[inside], target, sem).start()


def choose_kernel(parts, n_sources, table_ref, *refs):
    sources, outs, sems = refs[:n_sources], refs[-1 - len(parts) : -1], refs[-1]
    targets = [
        (at + slot, out_ref.at[slot])
        for (at, total), out_ref in zip(parts, outs)
        for slot in range(total)
    ]
    start_copies(
        sources,
        [(table_ref[at], target, sems.at[number]) for number, (at, target) in enumerate(targets)],
    )
    for number, (_, target) in enumerate(targets):
        pltpu.make_async_copy(sources[0].at[0], target, sems.at[number]).wait()


def choose(table, parts, sources, name, after=()):
    block = sources[0].shape[1:]
    total = sum(count for _, count in parts)
    return pl.pallas_call(
        functools.partial(choose_kernel, parts, len(sources)),
        out_shape=tuple(jax.ShapeDtypeStruct((count,) + block, BF16) for _, count in parts),
        in_specs=[pl.BlockSpec(memory_space=pltpu.SMEM)]
        + [pl.BlockSpec(memory_space=pl.ANY)] * (len(sources) + len(after)),
        out_specs=tuple(pl.BlockSpec(memory_space=pltpu.VMEM) for _ in parts),
        scratch_shapes=[pltpu.SemaphoreType.DMA((total,))],
        compiler_params=pltpu.CompilerParams(vmem_limit_bytes=8 * MIB),
        cost_estimate=SMALL_COST,
        name=name,
    )(table, *sources, *after)


def join_kernel(spots_ref, near, side, mate, out_ref, sems):
    piece = near.shape[0]
    sources = (near, side, mate.at[0], mate.at[1])
    copies = []
    for number, source in enumerate(sources):
        place = pl.ds(pl.multiple_of(spots_ref[number] * piece, piece), piece)
        copies.append(pltpu.make_async_copy(source, out_ref.at[place, :], sems.at[number]))
    for copy in copies:
        copy.start()
    for copy in copies:
        copy.wait()


def join(spots, near, side, mate):
    shape = (4 * near.shape[0], near.shape[1])
    any_space = pl.BlockSpec(memory_space=pl.ANY)
    return pl.pallas_call(
        join_kernel,
        out_shape=jax.ShapeDtypeStruct(shape, BF16),
        in_specs=[pl.BlockSpec(memory_space=pltpu.SMEM)] + [any_space] * 3,
        out_specs=pl.BlockSpec(memory_space=pltpu.VMEM),
        scratch_shapes=[pltpu.SemaphoreType.DMA((4,))],
        compiler_params=pltpu.CompilerParams(vmem_limit_bytes=8 * MIB),
        name="join",
    )(spots, near, side, mate)


def in_hbm(array):
    return pltpu.with_memory_space_constraint(array, pltpu.HBM)


def split_store(value, high_ref, low_ref):
    high = value.astype(BF16)
    high_ref[...] = high
    low_ref[...] = (value - high.astype(F32)).astype(BF16)


def attend_kernel(n_after, own_ref, other_ref, rows_ref, b_ref, w_ref, *refs):
    (out_ref, held, normed, q_high, q_low, k_high, k_low, values, scores, sems) = refs[n_after:]
    blocks, rows, width = own_ref.shape
    span = held.shape[2]
    loads = [pltpu.make_async_copy(w_ref.at[j], held.at[j], sems.at[j]) for j in range(3)]
    for load in loads:
        load.start()
    gain, shift = rows_ref[0:1, :], rows_ref[1:2, :]
    for half, ref in enumerate((own_ref, other_ref)):
        for block in range(blocks):
            at = (half * blocks + block) * rows
            normed[at : at + rows] = norm_rows(ref[block].astype(F32), gain, shift).astype(BF16)

    def project(j):
        loads[j].wait()
        product = jnp.dot(normed[...], held[j], preferred_element_type=F32)
        return product + b_ref[j : j + 1, :]

    split_store(project(0) * HEAD_DIM ** (-0.5), q_high, q_low)
    split_store(project(1), k_high, k_low)
    values[...] = project(2).astype(BF16)
    tiles = span // 128
    heads = span // HEAD_DIM
    size = 2 * rows
    lane = lax.broadcasted_iota(jnp.int32, (1, 256), 1)

    def window(head):
        tile = min(head * HEAD_DIM // 128, tiles - 2)
        first = head * HEAD_DIM - tile * 128
        inside = (lane >= first) & (lane < first + HEAD_DIM)
        return tile, slice(tile * 128, tile * 128 + 256), inside

    def one_block(block, carry):
        near = pl.ds(pl.multiple_of(block * rows, rows), rows)
        far = pl.ds(pl.multiple_of((blocks + block) * rows, rows), rows)

        def both(ref, columns):
            return jnp.concatenate([ref[near, columns], ref[far, columns]], axis=0)

        def times(left, right):
            return lax.dot_general(
                left, right, (((1,), (1,)), ((), ())), preferred_element_type=F32
            )

        for head in range(heads):
            _, columns, inside = window(head)
            none = jnp.zeros((), BF16)
            qh = jnp.where(inside, both(q_high, columns), none)
            ql = jnp.where(inside, both(q_low, columns), none)
            kh, kl = both(k_high, columns), both(k_low, columns)
            scores[head * size : (head + 1) * size, :] = (
                times(qh, kh) + times(qh, kl) + times(ql, kh)
            )
        value = scores[...]
        value = jnp.exp(value - jnp.max(value, axis=-1, keepdims=True))
        weights = (value * (1.0 / jnp.sum(value, axis=-1, keepdims=True))).astype(BF16)
        sums = [None] * tiles
        for head in range(heads):
            tile, columns, inside = window(head)
            mixed = jnp.dot(
                weights[head * size : (head + 1) * size, :], both(values, columns),
                preferred_element_type=F32,
            )
            mixed = jnp.where(inside, mixed, 0.0)
            for part in range(2):
                piece = mixed[:, part * 128 : part * 128 + 128]
                old = sums[tile + part]
                sums[tile + part] = piece if old is None else old + piece
        result = jnp.concatenate(sums, axis=1).astype(BF16)
        out_ref[0, block] = result[:rows]
        out_ref[1, block] = result[rows:]
        return carry

    lax.fori_loop(0, blocks, one_block, 0)


def attend(own, other, rows_params, w_qkv, b_qkv, after=()):
    blocks, rows, width = own.shape
    span = w_qkv.shape[2]
    total = 2 * blocks * rows
    vmem = pl.BlockSpec(memory_space=pltpu.VMEM)
    return pl.pallas_call(
        functools.partial(attend_kernel, len(after)),
        out_shape=jax.ShapeDtypeStruct((2, blocks, rows, span), BF16),
        in_specs=[vmem] * 4 + [pl.BlockSpec(memory_space=pl.ANY)] * (1 + len(after)),
        out_specs=vmem,
        scratch_shapes=[pltpu.VMEM((3, width, span), BF16), pltpu.VMEM((total, width), BF16)]
        + [pltpu.VMEM((total, span), BF16)] * 5
        + [
            pltpu.VMEM((2 * rows * (span // HEAD_DIM), 2 * rows), F32),
            pltpu.SemaphoreType.DMA((3,)),
        ],
        compiler_params=pltpu.CompilerParams(vmem_limit_bytes=28 * MIB),
        cost_estimate=pl.CostEstimate(
            flops=24 * total * width * span, bytes_accessed=6 * width * span, transcendentals=0
        ),
        name="attend",
    )(own, other, rows_params, b_qkv, in_hbm(w_qkv), *after)


UP_TILE = 768
DOWN_TILE = 256
SLOTS = 4


def mlp_kernel(n_after, own_ref, other_ref, mine_ref, theirs_ref, rows_ref, b_up_ref, w_mine, w_theirs,
               w_up, w_down, *refs):
    (keep_ref, send_ref, residual, renormed, hidden, outs, ups, downs, out_sems, up_sems,
     down_sems) = refs[n_after:]
    blocks, rows, width = own_ref.shape
    half = blocks * rows
    span = outs.shape[1]
    up_steps, down_steps = w_up.shape[1] // UP_TILE, width // DOWN_TILE

    def load_up(step):
        columns = pl.ds(pl.multiple_of(step * UP_TILE, UP_TILE), UP_TILE)
        slot = lax.rem(step, SLOTS)
        return pltpu.make_async_copy(w_up.at[:, columns], ups.at[slot], up_sems.at[slot])

    def load_down(step):
        columns = pl.ds(pl.multiple_of(step * DOWN_TILE, DOWN_TILE), DOWN_TILE)
        slot = lax.rem(step, SLOTS)
        return pltpu.make_async_copy(w_down.at[:, columns], downs.at[slot], down_sems.at[slot])

    out_loads = [
        pltpu.make_async_copy(source, outs.at[number], out_sems.at[number])
        for number, source in enumerate((w_mine, w_theirs))
    ]
    for load in out_loads:
        load.start()
    load_up(jnp.int32(0)).start()
    gain, shift = rows_ref[2:3, :], rows_ref[3:4, :]
    mine = mine_ref[...].reshape(2 * half, span)
    theirs = jnp.concatenate(
        [theirs_ref[1].reshape(half, span), theirs_ref[0].reshape(half, span)], axis=0
    )
    for number, attended in enumerate((mine, theirs)):
        out_loads[number].wait()
        for slot in (range(1, 3), range(3, SLOTS))[number]:
            load_up(jnp.int32(slot)).start()
        for column in range(0, width, DOWN_TILE):
            columns = slice(column, column + DOWN_TILE)
            part = jnp.dot(attended, outs[number, :, columns], preferred_element_type=F32)
            part = part.astype(BF16).astype(F32)
            if number == 0:
                residual[:, columns] = part + rows_ref[4:5, columns]
            else:
                residual[:, columns] += part
    for side, ref in enumerate((own_ref, other_ref)):
        for block in range(blocks):
            at = slice((side * blocks + block) * rows, (side * blocks + block + 1) * rows)
            value = ref[block].astype(F32) + residual[at]
            if side == 0:
                residual[at] = value
            renormed[at] = norm_rows(value, gain, shift).astype(BF16)

    def one_up(step, carry):
        load_up(step).wait()
        slot = lax.rem(step, SLOTS)
        for part in range(0, UP_TILE, 256):
            columns = pl.ds(pl.multiple_of(step * UP_TILE + part, 256), 256)
            raised = jnp.dot(
                renormed[...], ups[slot, :, part : part + 256], preferred_element_type=F32
            )
            raised = raised + b_up_ref[0:1, columns]
            hidden[:, columns] = jax.nn.gelu(raised, approximate=True).astype(BF16)
        ahead = step + SLOTS

        @pl.when(ahead < up_steps)
        def _():
            load_up(ahead).start()

        @pl.when((ahead >= up_steps) & (ahead < up_steps + down_steps))
        def _():
            load_down(ahead - up_steps).start()

        return carry

    lax.fori_loop(0, up_steps, one_up, 0)

    def one_down(step, carry):
        load_down(step).wait()
        columns = pl.ds(pl.multiple_of(step * DOWN_TILE, DOWN_TILE), DOWN_TILE)
        lowered = jnp.dot(
            hidden[...], downs[lax.rem(step, SLOTS)], preferred_element_type=F32
        )
        kept = residual[:half, columns] + lowered[:half] + rows_ref[5:6, columns]
        keep_ref[:, :, columns] = kept.reshape(blocks, rows, DOWN_TILE)
        send_ref[:, :, columns] = lowered[half:].astype(BF16).reshape(blocks, rows, DOWN_TILE)

        @pl.when(step + SLOTS < down_steps)
        def _():
            load_down(step + SLOTS).start()

        return carry

    lax.fori_loop(0, down_steps, one_down, 0)


def mlp(own, other, mine, theirs, rows_params, b_up, weights, after):
    blocks, rows, width = own.shape
    span = mine.shape[3]
    total = 2 * blocks * rows
    vmem = pl.BlockSpec(memory_space=pltpu.VMEM)
    hbm = pl.BlockSpec(memory_space=pl.ANY)
    w_mine, w_theirs, w_up, w_down = weights
    hidden = w_up.shape[1]
    return pl.pallas_call(
        functools.partial(mlp_kernel, len(after)),
        out_shape=(
            jax.ShapeDtypeStruct((blocks, rows, width), F32),
            jax.ShapeDtypeStruct((blocks, rows, width), BF16),
        ),
        in_specs=[vmem] * 6 + [hbm] * (4 + len(after)),
        out_specs=(vmem, vmem),
        scratch_shapes=[
            pltpu.VMEM((total, width), F32),
            pltpu.VMEM((total, width), BF16),
            pltpu.VMEM((total, hidden), BF16),
            pltpu.VMEM((2, span, width), BF16),
            pltpu.VMEM((SLOTS, width, UP_TILE), BF16),
            pltpu.VMEM((SLOTS, hidden, DOWN_TILE), BF16),
            pltpu.SemaphoreType.DMA((2,)),
            pltpu.SemaphoreType.DMA((SLOTS,)),
            pltpu.SemaphoreType.DMA((SLOTS,)),
        ],
        compiler_params=pltpu.CompilerParams(vmem_limit_bytes=46 * MIB),
        cost_estimate=pl.CostEstimate(
            flops=8 * total * width * (span + hidden),
            bytes_accessed=4 * width * (span + hidden),
            transcendentals=0,
        ),
        name="mlp",
    )(
        own, other, mine, theirs, rows_params, b_up, in_hbm(w_mine), w_theirs, in_hbm(w_up),
        in_hbm(w_down), *after,
    )


def add_kernel(n_after, keep_ref, came_ref, *refs):
    out_ref = refs[n_after]
    out_ref[...] = (keep_ref[...] + came_ref[...].astype(F32)).astype(BF16)


def add(keep, came, after):
    vmem = pl.BlockSpec(memory_space=pltpu.VMEM)
    return pl.pallas_call(
        functools.partial(add_kernel, len(after)),
        out_shape=jax.ShapeDtypeStruct(came.shape, BF16),
        in_specs=[vmem] * 2 + [pl.BlockSpec(memory_space=pl.ANY)] * len(after),
        out_specs=vmem,
        compiler_params=pltpu.CompilerParams(vmem_limit_bytes=8 * MIB),
        cost_estimate=SMALL_COST,
        name="add",
    )(keep, came, *after)


def swap(value):
    return lax.ppermute(value, "tensor", [(0, 1), (1, 0)])


def line_up_kernel(total, n_after, *refs):
    sources, out_ref, sems = refs[:total], refs[total + n_after], refs[-1]
    copies = [
        pltpu.make_async_copy(source, out_ref.at[number], sems.at[number])
        for number, source in enumerate(sources)
    ]
    for copy in copies:
        copy.start()
    for copy in copies:
        copy.wait()


def line_up(arrays, after, name):
    any_space = pl.BlockSpec(memory_space=pl.ANY)
    total = len(arrays)
    return pl.pallas_call(
        functools.partial(line_up_kernel, total, len(after)),
        out_shape=jax.ShapeDtypeStruct((total,) + arrays[0].shape, arrays[0].dtype),
        in_specs=[any_space] * (total + len(after)),
        out_specs=pl.BlockSpec(memory_space=pltpu.VMEM),
        scratch_shapes=[pltpu.SemaphoreType.DMA((total,))],
        compiler_params=pltpu.CompilerParams(vmem_limit_bytes=8 * MIB),
        cost_estimate=SMALL_COST,
        name=name,
    )(*arrays, *after)


def w_out_place(w_out):
    core = lax.axis_index("dp") & 1
    group = lax.axis_index("groups")
    return 2 * group + core, 2 * (1 - group) + core, w_out.shape[0] // 4


def piece_kernel(n_after, number_ref, w_ref, *refs):
    out_ref, sem = refs[n_after:]
    piece = out_ref.shape[0]
    rows = pl.ds(pl.multiple_of(number_ref[0] * piece, piece), piece)
    copy = pltpu.make_async_copy(w_ref.at[rows, :], out_ref, sem)
    copy.start()
    copy.wait()


def w_out_piece(w_out, after):
    number, _, piece = w_out_place(w_out)
    any_space = pl.BlockSpec(memory_space=pl.ANY)
    return pl.pallas_call(
        functools.partial(piece_kernel, len(after)),
        out_shape=jax.ShapeDtypeStruct((piece, w_out.shape[1]), BF16),
        in_specs=[pl.BlockSpec(memory_space=pltpu.SMEM)] + [any_space] * (1 + len(after)),
        out_specs=pl.BlockSpec(memory_space=pltpu.VMEM),
        scratch_shapes=[pltpu.SemaphoreType.DMA],
        compiler_params=pltpu.CompilerParams(vmem_limit_bytes=4 * MIB),
        cost_estimate=SMALL_COST,
        name="w_piece",
    )(number.astype(jnp.int32).reshape(1), in_hbm(w_out), *after)


def other_w_out(w_out, near, side, after):
    number, other, _ = w_out_place(w_out)
    dp_size = lax.axis_size("dp")
    both = line_up([near, side], after, "w_both")
    mate = lax.ppermute(both, "dp", [(d, d ^ 1) for d in range(dp_size)])
    spots = jnp.stack([number, other, number ^ 1, other ^ 1]).astype(jnp.int32)
    return join(spots, near, side, mate)


def attend_rows(projected):
    row_total, count_blocks, width = (projected.shape[0], projected.shape[1], projected.shape[3])
    head_count = width // HEAD_DIM
    queries = projected[:, :, 0].reshape(row_total, count_blocks, head_count, HEAD_DIM)
    key_rows = projected[:, :, 1].reshape(row_total, count_blocks, head_count, HEAD_DIM)
    values = projected[:, :, 2].astype(BF16).reshape(row_total, count_blocks, head_count, HEAD_DIM)
    scores = jnp.einsum(
        "qnhd,snhd->nhqs", queries, key_rows, precision=lax.Precision.HIGHEST
    ) * HEAD_DIM ** (-0.5)
    weights = jax.nn.softmax(scores, axis=-1).astype(BF16)
    attended = jnp.einsum("nhqs,snhd->qnhd", weights, values, preferred_element_type=F32)
    return attended.astype(BF16).reshape(row_total, count_blocks, width)


def encode_split(own, params):
    (pre_gain, pre_shift, w_qkv, b_qkv, w_out, b_out, mlp_gain, mlp_shift, w_up, b_up, w_down,
     b_down) = params
    block_rows = jnp.swapaxes(own, 0, 1)
    rows_dev = block_rows.shape[0]
    gathered = lax.all_gather(block_rows, "tensor", axis=0, tiled=True)
    normed = norm_rows(gathered.astype(F32), pre_gain, pre_shift).astype(BF16)
    attended = attend_rows(
        jnp.einsum("qnd,jde->qnje", normed, w_qkv, preferred_element_type=F32) + b_qkv[None, None]
    )
    partial_value = jnp.einsum("qne,ed->qnd", attended, w_out, preferred_element_type=F32)
    summed = lax.psum(partial_value.astype(BF16), "tensor").astype(F32)
    residual_all = gathered.astype(F32) + summed + b_out
    renormed = norm_rows(residual_all, mlp_gain, mlp_shift).astype(BF16)
    raised = jnp.einsum("qnd,df->qnf", renormed, w_up, preferred_element_type=F32) + b_up
    hidden = jax.nn.gelu(raised, approximate=True).astype(BF16)
    residual = lax.dynamic_slice_in_dim(
        residual_all, lax.axis_index("tensor") * rows_dev, rows_dev, 0
    )
    mlp_out = lax.psum_scatter(
        jnp.einsum("qnf,fd->qnd", hidden, w_down, preferred_element_type=F32).astype(BF16),
        "tensor", scatter_dimension=0, tiled=True,
    ).astype(F32)
    return jnp.swapaxes((residual + mlp_out + b_down).astype(BF16), 0, 1)


def per_device(paired, patches, kept_count, keep_list, *params):
    home = in_hbm(patches[0])
    keep_row = in_hbm(keep_list[0])
    kept_count = in_hbm(kept_count)
    dp_size = lax.axis_size("dp")
    device = lax.axis_index("dp").astype(jnp.int32).reshape(1)
    mates = [(d, d ^ 1) for d in range(dp_size)]
    pairs = [(d, d ^ 2) for d in range(dp_size)]
    nexts = [
        (d, d ^ 1 if d < 2 or d >= dp_size - 2 else ((d + 2) ^ 2) - 2) for d in range(dp_size)
    ]

    def to_mate(value):
        return lax.ppermute(value, "dp", mates)

    def to_pair(value):
        return lax.ppermute(value, "dp", pairs)

    def to_next(value):
        return lax.ppermute(value, "dp", nexts)

    mine, for_mate = pack(device, kept_count, keep_row, home)
    from_mate = to_mate(for_mate)
    table = make_plan(device, kept_count)
    short = table[AT_SHORT : AT_SHORT + 1].astype(F32)
    if paired:
        short = short + lax.ppermute(short, "groups", [(0, 1), (1, 0)])
    else:
        short = lax.pmax(short, "groups")
    flag = short
    short = flag[0] > 0

    parts = tuple(zip(STARTS, CHUNKS))
    sends = [(AT_PAIR + at, size) for at, size in parts] + [(AT_NEXT + at, size) for at, size in parts]
    going = choose(table, sends, [mine, from_mate], "send")
    came_pair = [to_pair(value) for value in going[: len(parts)]]
    came_next = [to_next(value) for value in going[len(parts) :]]

    def deal_fast(chunk, after):
        came = [came_pair[min(part, chunk)] for part in range(len(parts))]
        came = came + [came_next[min(part, chunk)] for part in range(len(parts))]
        at, size = parts[chunk]
        sources = [mine, from_mate] + came
        return choose(table, [(AT_DEALT + at, size)], sources, "deal_%d" % chunk, after)[0]

    def deal_slow(chunk):
        chips = dp_size // 2
        (picked,) = choose(table, [(AT_SLOW_SEND, ROOM * chips)], [mine, from_mate], "deal_slow")
        picked = picked.reshape((chips, ROOM) + picked.shape[1:])
        spread = jnp.repeat(picked, 2, axis=0)
        arrived = lax.all_to_all(spread, "dp", split_axis=0, concat_axis=0, tiled=True)
        at, size = parts[chunk]
        return jnp.stack(
            [
                arrived[table[AT_SLOW_SOURCE + j], table[AT_SLOW_PLACE + j]]
                for j in range(at, at + size)
            ]
        )

    def deal(chunk, after=()):
        return lax.cond(short, lambda: deal_slow(chunk), lambda: deal_fast(chunk, after))

    if paired:
        (pre_gain, pre_shift, w_qkv, b_qkv, w_out, b_out, mlp_gain, mlp_shift, w_up, b_up, w_down,
         b_down) = params
        rows_params = jnp.stack([pre_gain, pre_shift, mlp_gain, mlp_shift, b_out, b_down])
        b_up = b_up.reshape(1, -1)
        w_near = swap(w_out_piece(w_out, [for_mate]))

        def start(own, after):
            other = swap(own)
            mine = attend(own, other, rows_params, w_qkv, b_qkv, after)
            return own, other, mine, swap(mine)

        def finish(state, after):
            keep, send = mlp(*state, rows_params, b_up, weights, after)
            return keep, swap(send)

        blocks_0 = deal(0)
        state_0 = start(blocks_0, [])
        w_sent = line_up([w_near], [flag], "w_near")
        blocks_1 = deal(1, [w_sent])
        state_1 = start(blocks_1, [])
        w_side = lax.ppermute(w_sent, "groups", [(0, 1), (1, 0)])[0]
        w_theirs = other_w_out(w_out, w_near, w_side, [blocks_1])
        weights = (w_out, w_theirs, w_up, w_down)
        done_0 = finish(state_0, [state_1[2]])
        done_1 = finish(state_1, [done_0[0]])
        results, from_pair, from_next = [], [], []
        for done, beside in ((done_0, done_1[:1]), (done_1, ())):
            results.append(add(*done, list(beside) + from_pair[-1:] + from_next[-1:]))
            from_pair.append(to_pair(results[-1]))
            from_next.append(to_next(results[-1]))
    else:
        results = [encode_split(deal(chunk), params) for chunk in range(len(parts))]
        from_pair = [to_pair(value) for value in results]
        from_next = [to_next(value) for value in results]

    back = results + from_pair + from_next
    last = len(parts) - 1
    back = back + [
        back[place] if place + len(back) in LATE else to_mate(value)
        for place, value in enumerate(back)
    ]

    def home_slow():
        spread = lax.all_gather(jnp.concatenate(results), "dp", axis=0, tiled=True)
        places = table[AT_SLOW_HOME : AT_SLOW_HOME + 2 * PAGE_HALF]
        return (
            jnp.take(spread, places[:PAGE_HALF], axis=0),
            jnp.take(spread, places[PAGE_HALF:], axis=0),
        )

    found = lax.cond(short, home_slow, lambda: (mine, from_mate))
    slots = 2 * PAGE_HALF
    codes = jnp.where(
        short, table[AT_IN_ORDER : AT_IN_ORDER + slots], table[AT_HOME : AT_HOME + slots]
    )
    early = [results[0] if place in LATE else value for place, value in enumerate(back)]
    (gathered,) = choose(codes, [(0, slots)], early + list(found), "gather")
    late = [from_pair[last], from_next[last]]
    mates_late = to_mate(line_up(late, [gathered], "late"))
    late.append(mates_late.reshape((-1,) + mates_late.shape[2:]))
    return merge(device, kept_count, keep_row, codes, home, gathered, late)[None]


def solution(mesh):
    in_specs = (
        P(("groups", "dp"), "tensor", None, None),
        P("groups"),
        P(("groups", "dp"), None),
        P(),
        P(),
        P(None, None, "tensor"),
        P(None, "tensor"),
        P("tensor", None),
        P(),
        P(),
        P(),
        P(None, "tensor"),
        P("tensor"),
        P("tensor", None),
        P(),
    )
    out_specs = P(("groups", "dp"), "tensor", None, None)
    paired = mesh.shape["tensor"] == 2 and mesh.shape["groups"] == 2
    return jax.shard_map(
        functools.partial(per_device, paired), mesh=mesh, in_specs=in_specs, out_specs=out_specs,
        check_vma=False,
    )
```
